32 devices in a mesh: batch: 8 (over z, core), mp: 4 (over y, x).
Axes of the slice: x: 2, y: 2, z: 4, core: 2. Of those that a mesh axis runs over, the one named last changes fastest.
Arguments:
- hidden_states: bfloat16 [128, 4, 16384], P('batch', None, 'mp'), may hold values from -6 to 6
- accepted: int32 [128], P('batch'), may hold values from 1 to 4
- norm_gain: float32 [16384], replicated, may hold values from 0.25 to 1.75
- head_weight: bfloat16 [2, 16384, 16384], P(None, 'batch', 'mp'), may hold values from -0.046875 to 0.046875
- head_bias: float32 [2, 16384], P(None, 'mp'), may hold values from -4 to 4
- vocab_weight: bfloat16 [16384, 65536], P('mp', 'batch')
- cand_ids: int32 [128, 2, 10], P('mp'), may hold values from 0 to 65535
- tree_paths: int32 [64, 2], replicated, may hold values from 0 to 9
Outputs:
- log_probs: float32 [128, 2, 65536], P('mp', None, 'batch')
- path_scores: float32 [128, 64], P('mp')
The draws below stay inside these ranges and needn't reach their ends.
All inputs are finite; a program needn't handle non-finite values.
Results may differ from the reference program's by a relative error of at most 0.0032.
Values may be sent and summed in bfloat16 or wider, within the bound.
No kernel may reach another device: no remote copies, remote signals or barrier semaphores. Data moves between devices by JAX's collectives and lax.ppermute only.
A program may use at most 256 MiB of HBM per device.

```python
import jax
import jax.numpy as jnp
from jax import lax

D = 16384
V = 65536
HEADS = 2
POSITIONS = 4
CANDS = 10
PATHS = 64
ROWS = 128


def draw_vocab_weight(key, part):
    key = jax.random.fold_in(key, 7)
    noise_key, scale_key = jax.random.split(key, 2)
    gaussian = jax.random.normal(noise_key, (D, V), jnp.float32) * D ** (-0.5)
    col_spread = jnp.exp(jax.random.uniform(scale_key, (V,), jnp.float32, jnp.log(0.6), jnp.log(6.0)))
    rising = 1.0 + 0.25 * jnp.arange(V, dtype=jnp.float32) / V
    weight = gaussian * (col_spread * rising)[None, :]
    return weight.astype(jnp.bfloat16)


def place_ends(values, stream_key, low, high):
    dims = values.shape
    index_at = [jax.random.randint(jax.random.fold_in(stream_key, axis), (), 0, dims[axis]) for axis in range(len(dims))]
    values = values.at[tuple(index_at)].set(low)
    longest = dims.index(max(dims))
    index_at[longest] = (index_at[longest] + 1) % dims[longest]
    return values.at[tuple(index_at)].set(high)


def shard_levels(stream_key, shape, pieces, smallest, top_value):
    def one(dim, blocks):
        heights = jax.random.uniform(jax.random.fold_in(jax.random.fold_in(stream_key, 6), dim), (blocks,), jnp.float32, smallest / len(pieces), top_value / len(pieces))
        return jnp.repeat(jnp.exp(heights), shape[dim] // blocks).reshape((-1,) + (1,) * (len(shape) - dim - 1))

    level = one(*pieces[0])
    for cut in pieces[1:]:
        level = level * one(*cut)
    return level


def centred(key, dims, spread, limit, cuts=(), held_as=jnp.bfloat16):
    gain = shard_levels(key, dims, cuts, -0.22, 0.18) if cuts else 1.0
    values = jax.random.normal(key, dims, jnp.float32) * spread * gain
    return jnp.minimum(jnp.maximum(values, -limit), limit).astype(held_as)


def setup_inputs(seed: int = 0) -> dict:
    seeds = jax.random.split(jax.random.key(seed), 9)
    return {
        "hidden_states": centred(seeds[0], (ROWS, POSITIONS, D), 1.0, 6.0, ((0, 8), (2, 4))),
        "accepted": place_ends(jax.random.randint(seeds[1], (ROWS,), 1, POSITIONS + 1), jax.random.fold_in(seeds[1], 1), 1, POSITIONS).astype(jnp.int32),
        "norm_gain": jnp.clip(1.0 + 0.15 * jax.random.normal(seeds[2], (D,), jnp.float32), 0.25, 1.75),
        "head_weight": centred(seeds[3], (HEADS, D, D), D ** -0.5, 0.046875, ((1, 8), (2, 4))),
        "head_bias": centred(seeds[4], (HEADS, D), 1.0, 4.0, ((1, 4),), jnp.float32),
        "vocab_weight": draw_vocab_weight(jax.random.fold_in(seeds[8], 71), 0),
        "cand_ids": place_ends(jax.random.randint(seeds[6], (ROWS, HEADS, CANDS), 0, V), jax.random.fold_in(seeds[6], 1), 0, V - 1).astype(jnp.int32),
        "tree_paths": place_ends(jax.random.randint(seeds[7], (PATHS, HEADS), 0, CANDS), jax.random.fold_in(seeds[7], 1), 0, CANDS - 1).astype(jnp.int32),
    }


EPSILON = 1e-05

def reference(hidden_states, accepted, norm_gain, head_weight, head_bias, vocab_weight, cand_ids, tree_paths):
    position = (accepted - 1).astype(jnp.int32)[:, None, None]
    chosen = jnp.take_along_axis(hidden_states, position, axis=1)[:, 0, :].astype(jnp.float32)
    mean_square = lax.optimization_barrier(jnp.mean(chosen * chosen, axis=1, keepdims=True))
    normed = (chosen * lax.rsqrt(mean_square + EPSILON) * norm_gain).astype(jnp.bfloat16)
    log_list = []
    path_scores = jnp.zeros((ROWS, PATHS), jnp.float32)
    for head_index in range(HEADS):
        before = jnp.dot(normed, head_weight[head_index], preferred_element_type=jnp.float32) + head_bias[head_index]
        residual = (normed.astype(jnp.float32) + jax.nn.silu(before)).astype(jnp.bfloat16)
        logits = jnp.dot(residual, vocab_weight, preferred_element_type=jnp.float32)
        largest = lax.optimization_barrier(jnp.max(logits, axis=1, keepdims=True))
        row_total = lax.optimization_barrier(jnp.sum(jnp.exp(logits - largest), axis=1, keepdims=True))
        log_probs = logits - (largest + jnp.log(row_total))
        log_list.append(log_probs)
        picked = jnp.take_along_axis(log_probs, cand_ids[:, head_index, :].astype(jnp.int32), axis=1)
        path_scores = path_scores + picked[:, tree_paths[:, head_index].astype(jnp.int32)]
    return (jnp.stack(log_list, axis=1), path_scores)
```

```python
import functools

import jax
import jax.numpy as jnp
from jax import lax
from jax.experimental import pallas as pl
from jax.experimental.pallas import tpu as pltpu
from jax.sharding import PartitionSpec as P

EPSILON = 1e-05
MIB = 1024 * 1024


def bits_of(count):
    return [1 << i for i in range(count.bit_length() - 1)]


def exchange(array, axis, bit):
    size = lax.axis_size(axis)
    return lax.ppermute(array, axis, [(i, i ^ bit) for i in range(size)])


def place(index, stages):
    spot = 0
    for bit in stages:
        spot = 2 * spot + (index & bit) // bit
    return spot


def widest(limit, size):
    tile = min(limit, size)
    while size % tile:
        tile //= 2
    return tile


def head_body(spots, *refs, count):
    received, (weight, keep, send, rows) = refs[:count], refs[count:]
    height = received[0].shape[0]

    @pl.when(pl.program_id(0) == 0)
    def _():
        for k in range(count):
            start = pl.multiple_of(spots[k] * height, height)
            rows[pl.ds(start, height), :] = received[k][...]

    total = jnp.dot(rows[...], weight[0], preferred_element_type=jnp.float32)
    half = total.shape[0] // 2
    keep[...] = total[:half]
    send[...] = total[half:].astype(jnp.bfloat16)


def head_matmul(spots, received, head_weight, head):
    count = len(received)
    height, depth = received[0].shape
    width = head_weight.shape[2]
    tile = widest(512, width)
    half = count * height // 2
    return pl.pallas_call(
        functools.partial(head_body, count=count),
        grid_spec=pltpu.PrefetchScalarGridSpec(
            num_scalar_prefetch=1,
            grid=(width // tile,),
            in_specs=[pl.BlockSpec((height, depth), lambda n, s: (0, 0))] * count
            + [pl.BlockSpec((1, depth, tile), lambda n, s: (head, 0, n))],
            out_specs=[pl.BlockSpec((half, tile), lambda n, s: (0, n))] * 2,
            scratch_shapes=[pltpu.VMEM((count * height, depth), jnp.bfloat16)],
        ),
        out_shape=[
            jax.ShapeDtypeStruct((half, width), jnp.float32),
            jax.ShapeDtypeStruct((half, width), jnp.bfloat16),
        ],
        compiler_params=pltpu.CompilerParams(vmem_limit_bytes=32 * MIB),
        cost_estimate=pl.CostEstimate(
            flops=2 * count * height * depth * width,
            bytes_accessed=2 * depth * width,
            transcendentals=0,
        ),
    )(spots, *received, head_weight)


def vocab_body(spots, *refs, heads, height):
    parts, (weight, keep, send, rows) = refs[:heads], refs[heads:]
    blocks = parts[0].shape[0] // height

    @pl.when(pl.program_id(0) == 0)
    def _():
        for head in range(heads):
            for block in range(blocks):
                start = pl.multiple_of(spots[head * blocks + block] * height, height)
                rows[pl.ds(start, height), :] = parts[head][block * height : (block + 1) * height, :]

    total = jnp.dot(rows[...], weight[...], preferred_element_type=jnp.float32)
    half = total.shape[0] // 2
    keep[...] = total[:half]
    send[...] = total[half:].astype(jnp.bfloat16)


def vocab_matmul(spots, parts, height, vocab_weight, first, width):
    heads = len(parts)
    depth = vocab_weight.shape[0]
    all_rows = sum(p.shape[0] for p in parts)
    half = all_rows // 2
    tile = widest(256, width)
    base = first // tile
    return pl.pallas_call(
        functools.partial(vocab_body, heads=heads, height=height),
        grid_spec=pltpu.PrefetchScalarGridSpec(
            num_scalar_prefetch=1,
            grid=(width // tile,),
            in_specs=[pl.BlockSpec(p.shape, lambda n, s: (0, 0)) for p in parts]
            + [pl.BlockSpec((depth, tile), lambda n, s: (0, base + n))],
            out_specs=[pl.BlockSpec((half, tile), lambda n, s: (0, n))] * 2,
            scratch_shapes=[pltpu.VMEM((all_rows, depth), jnp.bfloat16)],
        ),
        out_shape=[
            jax.ShapeDtypeStruct((half, width), jnp.float32),
            jax.ShapeDtypeStruct((half, width), jnp.bfloat16),
        ],
        compiler_params=pltpu.CompilerParams(vmem_limit_bytes=32 * MIB),
        cost_estimate=pl.CostEstimate(
            flops=2 * all_rows * depth * width,
            bytes_accessed=2 * depth * width,
            transcendentals=0,
        ),
    )(spots, *parts, vocab_weight)


def stats_body(wanted, *refs, chunks, choices):
    kept, came, (logits, stats) = refs[:chunks], refs[chunks : 2 * chunks], refs[2 * chunks :]
    width = kept[0].shape[1]
    block = 16

    def one(step, carry):
        here = pl.ds(pl.multiple_of(step * block, block), block)
        ids = wanted[here, :]
        peak = jnp.full((block, 1), -jnp.inf, jnp.float32)
        for c in range(chunks):
            value = kept[c][here, :] + came[c][here, :].astype(jnp.float32)
            logits[here, c * width : (c + 1) * width] = value
            peak = jnp.maximum(peak, jnp.max(value, axis=1, keepdims=True))
        total = jnp.zeros((block, 1), jnp.float32)
        picks = [jnp.zeros((block, 1), jnp.float32) for _ in range(choices)]
        columns = lax.broadcasted_iota(jnp.int32, (block, width), 1)
        for c in range(chunks):
            value = logits[here, c * width : (c + 1) * width]
            total = total + jnp.sum(jnp.exp(value - peak), axis=1, keepdims=True)
            for k in range(choices):
                hit = columns == ids[:, k : k + 1] - c * width
                picks[k] = picks[k] + jnp.sum(jnp.where(hit, value, 0.0), axis=1, keepdims=True)
        lane = lax.broadcasted_iota(jnp.int32, (block, stats.shape[1]), 1)
        out = jnp.where(lane == 0, peak, 0.0)
        for k, item in enumerate([total] + picks):
            out = jnp.where(lane == k + 1, item, out)
        stats[here, :] = out
        return carry

    lax.fori_loop(0, logits.shape[0] // block, one, 0)


def row_stats(wanted, kept, came, choices):
    chunks = len(kept)
    rows, width = kept[0].shape
    lanes = wanted.shape[1]
    vmem = pl.BlockSpec(memory_space=pltpu.VMEM)
    return pl.pallas_call(
        functools.partial(stats_body, chunks=chunks, choices=choices),
        in_specs=[vmem] * (1 + 2 * chunks),
        out_specs=[vmem] * 2,
        out_shape=[
            jax.ShapeDtypeStruct((rows, chunks * width), jnp.float32),
            jax.ShapeDtypeStruct((rows, lanes), jnp.float32),
        ],
        compiler_params=pltpu.CompilerParams(vmem_limit_bytes=32 * MIB),
    )(wanted, *kept, *came)


def shards(
    hidden_states, accepted, norm_gain, head_weight, head_bias, vocab_weight, cand_ids, tree_paths
):
    batch, mp = lax.axis_size("batch"), lax.axis_size("mp")
    b, m = lax.axis_index("batch"), lax.axis_index("mp")
    rows, positions, feat = hidden_states.shape
    heads, inner, _ = head_weight.shape
    vocab_width = vocab_weight.shape[1]
    out_rows = cand_ids.shape[0]
    choices = cand_ids.shape[2]
    pieces = feat // inner
    ratio = out_rows // rows
    batch_bits, mp_bits = bits_of(batch), bits_of(mp)

    chosen = hidden_states[:, 0, :]
    for position in range(1, positions):
        chosen = jnp.where((accepted == position + 1)[:, None], hidden_states[:, position, :], chosen)
    chosen = chosen.astype(jnp.float32)
    square_sum = jnp.sum(chosen * chosen, axis=1, keepdims=True)
    gain = lax.dynamic_slice_in_dim(norm_gain, m * feat, feat, 0)
    scaled = (chosen * gain).astype(jnp.bfloat16)

    outgoing = [
        lax.dynamic_slice_in_dim(scaled, ((b // mp) ^ q) * inner, inner, 1) for q in range(pieces)
    ]
    received = []
    for k in range(batch):
        perm = []
        for src in range(batch):
            target = src ^ k
            for col in range(mp):
                perm.append((src * mp + col, (col * pieces + target // mp) * mp + target % mp))
        received.append(lax.ppermute(outgoing[k // mp], ("batch", "mp"), perm))
    turn = ((b % pieces) * mp + m) ^ b

    for bit in mp_bits:
        square_sum = square_sum + exchange(square_sum, "mp", bit)
    row_scale = lax.rsqrt(square_sum / (mp * feat) + EPSILON)
    own_normed = (chosen * row_scale * gain).astype(jnp.bfloat16).astype(jnp.float32)

    spots = jnp.stack([place(turn ^ k, batch_bits) for k in range(batch)]).astype(jnp.int32)
    gathered, orders = [], []
    for head in range(heads):
        outer = batch_bits[1:]
        stages = batch_bits[:1] + (outer if head % 2 == 0 else outer[::-1])
        keep, send = head_matmul(spots, received, head_weight, head)
        order = sorted(range(batch), key=lambda j: place(j, batch_bits))
        order = order[: batch // 2]
        total = keep + exchange(send, "batch", stages[0]).astype(jnp.float32)
        for bit in stages[1:]:
            blocks = total.reshape(len(order), rows, feat)
            stay = [i for i, j in enumerate(order) if not j & bit]
            leave = [i for i, j in enumerate(order) if j & bit]
            outbound = jnp.concatenate([blocks[i] for i in leave], axis=0).astype(jnp.bfloat16)
            home = jnp.concatenate([blocks[i] for i in stay], axis=0)
            total = home + exchange(outbound, "batch", bit).astype(jnp.float32)
            order = [order[i] for i in stay]
        before = total * row_scale + head_bias[head][None, :]
        block = (own_normed + jax.nn.silu(before)).astype(jnp.bfloat16)
        order = [0]
        for bit in stages[::-1]:
            block = jnp.concatenate([block, exchange(block, "batch", bit)], axis=0)
            order = order + [j ^ bit for j in order]
        gathered.append(block)
        orders.append(order)

    width = widest(1024, vocab_width)
    chunks = vocab_width // width
    kept, came = [], []
    spots_by_stage = []
    for stages in (mp_bits, mp_bits[::-1]):
        table = []
        for head in range(heads):
            for j in orders[head]:
                source = b ^ j
                spot = place((source // ratio) ^ m, stages)
                table.append((spot * ratio + source % ratio) * heads + head)
        spots_by_stage.append(jnp.stack(table).astype(jnp.int32))
    for chunk in range(chunks):
        stages = mp_bits if chunk % 2 == 0 else mp_bits[::-1]
        keep, send = vocab_matmul(
            spots_by_stage[chunk % 2], gathered, rows, vocab_weight, chunk * width, width
        )
        for index, bit in enumerate(stages):
            arrived = exchange(send, "mp", bit)
            if index + 1 < len(stages):
                total = keep + arrived.astype(jnp.float32)
                half = total.shape[0] // 2
                keep, send = total[:half], total[half:].astype(jnp.bfloat16)
        kept.append(keep)
        came.append(arrived)

    wanted = (cand_ids - b * vocab_width).reshape(ratio, rows, heads, choices)
    wanted = wanted.transpose(0, 2, 1, 3).reshape(out_rows * heads, choices)
    wanted = jnp.pad(wanted, ((0, 0), (0, 128 - choices)), constant_values=-1)
    logits, stats = row_stats(wanted, kept, came, choices)

    level = [stats] + [
        lax.ppermute(stats, "batch", [(i, i ^ j) for i in range(batch)]) for j in range(1, batch)
    ]
    peak = functools.reduce(jnp.maximum, [s[:, :1] for s in level])
    sums = [
        jnp.concatenate([s[:, 1:2] * jnp.exp(s[:, :1] - peak), s[:, 2 : 2 + choices]], axis=1)
        for s in level
    ]
    while len(sums) > 1:
        sums = [x + y for x, y in zip(sums[::2], sums[1::2])]
    normalizer = peak + jnp.log(sums[0][:, :1])
    picked = sums[0][:, 1:] - normalizer

    def natural(array):
        array = array.reshape(ratio, heads, rows, array.shape[1])
        return array.transpose(0, 2, 1, 3).reshape(out_rows, heads, array.shape[3])

    log_probs = natural(logits - normalizer)
    picked = natural(picked)
    path_scores = jnp.zeros((out_rows, tree_paths.shape[0]), jnp.float32)
    for head in range(heads):
        found = jnp.zeros_like(path_scores)
        for choice in range(choices):
            taken = tree_paths[:, head][None, :] == choice
            found = jnp.where(taken, picked[:, head, choice : choice + 1], found)
        path_scores = path_scores + found
    return (log_probs, path_scores)


def solution(mesh):
    return jax.shard_map(
        shards,
        mesh=mesh,
        in_specs=(
            P("batch", None, "mp"),
            P("batch"),
            P(),
            P(None, "batch", "mp"),
            P(None, "mp"),
            P("mp", "batch"),
            P("mp", None, None),
            P(),
        ),
        out_specs=(P("mp", None, "batch"), P("mp", None)),
        check_vma=False,
    )
```

```python
import functools

import jax
import jax.numpy as jnp
from jax import lax
from jax.experimental import pallas as pl
from jax.experimental.pallas import tpu as pltpu
from jax.sharding import PartitionSpec as P

EPSILON = 1e-05
MIB = 1024 * 1024
LANES = 128
CODE_BITS = 14


def bits_of(count):
    return [1 << i for i in range(count.bit_length() - 1)]


def swap(array, axis, partner):
    return lax.ppermute(array, axis, [(i, partner(i)) for i in range(lax.axis_size(axis))])


def place(index, stages):
    spot = 0
    for bit in stages:
        spot = 2 * spot + (index & bit) // bit
    return spot


def unplace(spot, stages):
    index = 0
    for step, bit in enumerate(stages[::-1]):
        index = index + ((spot >> step) & 1) * bit
    return index


def widest(limit, size):
    tile = min(limit, size)
    while size % tile:
        tile //= 2
    return tile


def weight_specs(ways, depth, tile, index):
    share = depth // ways
    return [pl.BlockSpec((share, tile), functools.partial(index, way)) for way in range(ways)]


def head_body(info, came, *refs, ways, height):
    weights, (out, rows) = refs[:ways], refs[ways:]

    @pl.when(pl.program_id(0) == 0)
    def _():
        for unit in range(came.shape[0] // height):
            start = pl.multiple_of(info[1 + unit] * height, height)
            rows[pl.ds(start, height), :] = came[unit * height : (unit + 1) * height, :]

    share = rows.shape[1] // ways
    total = None
    for way in range(ways):
        term = jnp.dot(
            rows[:, way * share : (way + 1) * share],
            weights[way][0],
            preferred_element_type=jnp.float32,
        )
        total = term if total is None else total + term
    out[...] = total.astype(out.dtype)


def head_matmul(info, came, head_weight, height, out_type):
    count, depth = came.shape
    width = head_weight.shape[2]
    tile = widest(512, width)
    ways = 4
    share = depth // ways
    specs = [
        pl.BlockSpec(
            (1, share, tile),
            functools.partial(lambda way, n, s: (s[0], way, n), way),
        )
        for way in range(ways)
    ]
    return pl.pallas_call(
        functools.partial(head_body, ways=ways, height=height),
        grid_spec=pltpu.PrefetchScalarGridSpec(
            num_scalar_prefetch=1,
            grid=(width // tile,),
            in_specs=[pl.BlockSpec((count, depth), lambda n, s: (0, 0))] + specs,
            out_specs=pl.BlockSpec((count, tile), lambda n, s: (0, n)),
            scratch_shapes=[pltpu.VMEM((count, depth), jnp.bfloat16)],
        ),
        out_shape=jax.ShapeDtypeStruct((count, width), out_type),
        compiler_params=pltpu.CompilerParams(vmem_limit_bytes=32 * MIB),
        cost_estimate=pl.CostEstimate(
            flops=2 * count * depth * width, bytes_accessed=2 * depth * width, transcendentals=0
        ),
    )(info, came, *[head_weight] * ways)


def encode(value):
    top = jnp.max(jnp.abs(value), axis=1, keepdims=True)
    power = jnp.floor(jnp.log2(jnp.maximum(top, 1e-30))) + 1.0
    code = jnp.floor(value * jnp.exp2(CODE_BITS - power) + 0.5)
    return code.astype(jnp.int32).astype(jnp.int16), power


def decode(code, power):
    return code.astype(jnp.int32).astype(jnp.float32) * jnp.exp2(power - CODE_BITS)


def marks_of(powers, height):
    lane = lax.broadcasted_iota(jnp.int32, (height, LANES), 1)
    marks = jnp.zeros((height, LANES), jnp.float32)
    for index, power in enumerate(powers):
        marks = jnp.where(lane == index, power, marks)
    return marks.astype(jnp.int32).astype(jnp.int16)


def vocab_body(spots, *refs, heads, height, ways, tile, waits):
    parts, refs = refs[:heads], refs[heads:]
    weights, (keep, send, rows, powers) = refs[:ways], refs[ways + waits :]
    blocks = parts[0].shape[0] // height
    step = pl.program_id(0)

    @pl.when(step == 0)
    def _():
        powers[...] = jnp.zeros_like(powers)
        for head in range(heads):
            for block in range(blocks):
                start = pl.multiple_of(spots[head * blocks + block] * height, height)
                rows[pl.ds(start, height), :] = parts[head][block * height : (block + 1) * height, :]

    share = rows.shape[1] // ways
    total = None
    for way in range(ways):
        term = jnp.dot(
            rows[:, way * share : (way + 1) * share],
            weights[way][...],
            preferred_element_type=jnp.float32,
        )
        total = term if total is None else total + term
    half = total.shape[0] // 2
    keep[...] = total[:half]
    code, power = encode(total[half:])
    send[:, pl.ds(pl.multiple_of(step * tile, tile), tile)] = code
    lane = lax.broadcasted_iota(jnp.int32, powers.shape, 1)
    powers[...] = jnp.where(lane == step, power, powers[...])

    @pl.when(step == pl.num_programs(0) - 1)
    def _():
        width = send.shape[1] - LANES
        send[:, width:] = powers[...].astype(jnp.int32).astype(jnp.int16)


def vocab_matmul(spots, parts, height, vocab_weight, first, width, tile, after):
    heads = len(parts)
    depth = vocab_weight.shape[0]
    all_rows = sum(p.shape[0] for p in parts)
    half = all_rows // 2
    base = first // tile
    ways = 4
    return pl.pallas_call(
        functools.partial(
            vocab_body, heads=heads, height=height, ways=ways, tile=tile, waits=len(after)
        ),
        grid_spec=pltpu.PrefetchScalarGridSpec(
            num_scalar_prefetch=1,
            grid=(width // tile,),
            in_specs=[pl.BlockSpec(p.shape, lambda n, s: (0, 0)) for p in parts]
            + weight_specs(ways, depth, tile, lambda way, n, s: (way, base + n))
            + [pl.BlockSpec(memory_space=pl.ANY)] * len(after),
            out_specs=[
                pl.BlockSpec((half, tile), lambda n, s: (0, n)),
                pl.BlockSpec((half, width + LANES), lambda n, s: (0, 0)),
            ],
            scratch_shapes=[
                pltpu.VMEM((all_rows, depth), jnp.bfloat16),
                pltpu.VMEM((half, LANES), jnp.float32),
            ],
        ),
        out_shape=[
            jax.ShapeDtypeStruct((half, width), jnp.float32),
            jax.ShapeDtypeStruct((half, width + LANES), jnp.int16),
        ],
        compiler_params=pltpu.CompilerParams(vmem_limit_bytes=40 * MIB),
        cost_estimate=pl.CostEstimate(
            flops=2 * all_rows * depth * width, bytes_accessed=2 * depth * width, transcendentals=0
        ),
    )(spots, *parts, *[vocab_weight] * ways, *after)


def fold_body(keep, came, stay, send, *, tile):
    half, width = stay.shape
    for row in range(0, 2 * half, 16):
        here = slice(row, row + 16)
        marks = came[here, width:].astype(jnp.int32).astype(jnp.float32)
        powers = []
        for step in range(width // tile):
            block = slice(step * tile, (step + 1) * tile)
            value = keep[here, block] + decode(came[here, block], marks[:, step : step + 1])
            if row < half:
                stay[here, block] = value
            else:
                there = slice(row - half, row - half + 16)
                code, power = encode(value)
                send[there, block] = code
                powers.append(power)
        if row >= half:
            send[row - half : row - half + 16, width:] = marks_of(powers, 16)


def fold(keep, came, tile):
    rows, width = keep.shape
    half = rows // 2
    vmem = pl.BlockSpec(memory_space=pltpu.VMEM)
    return pl.pallas_call(
        functools.partial(fold_body, tile=tile),
        in_specs=[vmem] * 2,
        out_specs=[vmem] * 2,
        out_shape=[
            jax.ShapeDtypeStruct((half, width), jnp.float32),
            jax.ShapeDtypeStruct((half, width + LANES), jnp.int16),
        ],
        compiler_params=pltpu.CompilerParams(vmem_limit_bytes=16 * MIB),
    )(keep, came)


def finish_body(wanted, keep, came, logits, stats, *, tile, choices, first):
    rows, width = keep.shape
    height = 16
    lane = lax.broadcasted_iota(jnp.int32, (height, LANES), 1)
    for row in range(0, rows, height):
        here = slice(row, row + height)
        marks = came[here, width:].astype(jnp.int32).astype(jnp.float32)
        ids = wanted[here, :] - first
        columns = [jnp.broadcast_to(ids[:, k : k + 1], (height, LANES)) for k in range(choices)]
        peak = None
        picks = [None] * choices
        for step in range(width // tile):
            scale = marks[:, step : step + 1]
            block = slice(step * tile, (step + 1) * tile)
            value = keep[here, block] + decode(came[here, block], scale)
            logits[here, block] = value
            for part in range(tile // LANES):
                piece = value[:, part * LANES : (part + 1) * LANES]
                at = lane + (step * tile + part * LANES)
                peak = piece if peak is None else jnp.maximum(peak, piece)
                for k in range(choices):
                    term = jnp.where(at == columns[k], piece, 0.0)
                    picks[k] = term if picks[k] is None else picks[k] + term
        peak = jnp.max(peak, axis=1, keepdims=True)
        total = None
        for part in range(width // LANES):
            term = jnp.exp(logits[here, part * LANES : (part + 1) * LANES] - peak)
            total = term if total is None else total + term
        out = jnp.where(lane == 0, peak, jnp.zeros((height, LANES), jnp.float32))
        for k, item in enumerate([total] + picks):
            out = jnp.where(lane == k + 1, jnp.sum(item, axis=1, keepdims=True), out)
        stats[here, :] = out


def finish(wanted, keep, came, tile, choices, first):
    rows, width = keep.shape
    vmem = pl.BlockSpec(memory_space=pltpu.VMEM)
    return pl.pallas_call(
        functools.partial(finish_body, tile=tile, choices=choices, first=first),
        in_specs=[vmem] * 3,
        out_specs=[vmem] * 2,
        out_shape=[
            jax.ShapeDtypeStruct((rows, width), jnp.float32),
            jax.ShapeDtypeStruct((rows, LANES), jnp.float32),
        ],
        compiler_params=pltpu.CompilerParams(vmem_limit_bytes=16 * MIB),
    )(wanted, keep, came)


def merge(one, two):
    peak = jnp.maximum(one[:, :1], two[:, :1])
    lane = lax.broadcasted_iota(jnp.int32, one.shape, 1)
    factor_one = jnp.where(lane == 1, jnp.exp(one[:, :1] - peak), 1.0)
    factor_two = jnp.where(lane == 1, jnp.exp(two[:, :1] - peak), 1.0)
    return jnp.where(lane == 0, peak, one * factor_one + two * factor_two)


def shards(
    hidden_states, accepted, norm_gain, head_weight, head_bias, vocab_weight, cand_ids, tree_paths
):
    batch, mp = lax.axis_size("batch"), lax.axis_size("mp")
    b, m = lax.axis_index("batch"), lax.axis_index("mp")
    rows, positions, feat = hidden_states.shape
    heads, inner, _ = head_weight.shape
    vocab_width = vocab_weight.shape[1]
    out_rows, _, choices = cand_ids.shape
    pieces = feat // inner
    ratio = out_rows // rows
    mp_bits = bits_of(mp)
    pair, core = b // 2, b % 2
    pair_bits = [bits_of(batch // 2), bits_of(batch // 2)[::-1]]

    chosen = hidden_states[:, 0, :]
    for position in range(1, positions):
        chosen = jnp.where((accepted == position + 1)[:, None], hidden_states[:, position, :], chosen)
    other = swap(chosen, "batch", lambda i: i ^ 1)
    chosen = jnp.concatenate(
        [jnp.where(core == 0, chosen, other), jnp.where(core == 0, other, chosen)], axis=0
    ).astype(jnp.float32)
    gain = lax.dynamic_slice_in_dim(norm_gain, m * feat, feat, 0)

    if pieces == 2:
        sent = lax.dynamic_slice_in_dim(chosen, core * inner, inner, 1)
        sent_gain = lax.dynamic_slice_in_dim(gain, core * inner, inner, 0)
    else:
        sent = lax.dynamic_slice_in_dim(chosen, core * rows, rows, 0)
        sent_gain = gain
    sent = (sent * sent_gain).astype(jnp.bfloat16)
    perm = []
    for i in range(batch):
        for j in range(mp):
            perm.append((i * mp + j, (j * pieces + i % pieces) * mp + i // pieces))
    block = lax.ppermute(sent, ("batch", "mp"), perm)
    for bit in mp_bits:
        block = jnp.concatenate([block, swap(block, "mp", lambda i: i ^ bit)], axis=0)

    square_sum = jnp.sum(chosen * chosen, axis=1, keepdims=True)
    for bit in mp_bits:
        square_sum = square_sum + swap(square_sum, "mp", lambda i: i ^ bit)
    row_scale = lax.rsqrt(square_sum / (mp * feat) + EPSILON)
    own_normed = (chosen * row_scale * gain).astype(jnp.bfloat16).astype(jnp.float32)

    spots = []
    for unit in range(batch):
        source = (m ^ (unit // pieces)) * pieces + unit % pieces
        apart = (source // 2) ^ pair
        spot = jnp.where(core == 0, place(apart, pair_bits[0]), place(apart, pair_bits[1]))
        spots.append(spot * 2 + source % 2)
    send = head_matmul(
        jnp.stack([1 - core] + spots).astype(jnp.int32), block, head_weight, rows, jnp.bfloat16
    )
    came = swap(send, "batch", lambda i: i ^ 1)
    keep = head_matmul(
        jnp.stack([core] + spots).astype(jnp.int32), block, head_weight, rows, jnp.float32
    )
    units = batch // 2
    turned = [place(unplace(u, pair_bits[0]), pair_bits[1]) for u in range(units)]
    came = came.reshape(units, 2 * rows, feat)
    came = jnp.concatenate([came[u] for u in turned], axis=0)
    total = keep + came.astype(jnp.float32)
    for step in range(len(pair_bits[0])):
        half = total.shape[0] // 2
        outbound = total[half:].astype(jnp.bfloat16)
        came = swap(outbound, "batch", lambda i: i ^ (2 * pair_bits[i % 2][step]))
        total = total[:half] + came.astype(jnp.float32)
    bias = lax.dynamic_slice_in_dim(head_bias, core, 1, 0)
    before = total * row_scale + bias
    residual = (own_normed + jax.nn.silu(before)).astype(jnp.bfloat16)
    for step in reversed(range(len(pair_bits[0]))):
        came = swap(residual, "batch", lambda i: i ^ (2 * pair_bits[i % 2][step]))
        residual = jnp.concatenate([residual, came], axis=0)
    parts = [residual, swap(residual, "batch", lambda i: i ^ 1)]

    orders = (mp_bits, mp_bits[::-1])
    spot_tables = []
    for stages in orders:
        table = []
        for whose in (core, 1 - core):
            for unit in range(batch):
                apart = jnp.where(
                    whose == 0, unplace(unit // 2, pair_bits[0]), unplace(unit // 2, pair_bits[1])
                )
                source = (pair ^ apart) * 2 + unit % 2
                spot = place((source // ratio) ^ m, stages)
                table.append((spot * ratio + source % ratio) * heads + whose)
        spot_tables.append(jnp.stack(table).astype(jnp.int32))
    wanted = (cand_ids - b * vocab_width).reshape(ratio, rows, heads, choices)
    wanted = wanted.transpose(0, 2, 1, 3).reshape(out_rows * heads, choices)
    wanted = jnp.pad(wanted, ((0, 0), (0, LANES - choices)), constant_values=-1)

    quarter = vocab_width // 4
    widths = [quarter, quarter, quarter, quarter // 2, quarter // 2]
    tile = widest(512, quarter // 2)
    first = 0
    arrivals, logits, stats = [], [], None
    for chunk, width in enumerate(widths):
        stages = orders[chunk % 2]
        after = []
        if chunk == 2:
            after = [arrivals[0]]
        elif chunk > 2:
            after = [arrivals[1], previous]
        keep, send = vocab_matmul(
            spot_tables[chunk % 2], parts, rows, vocab_weight, first, width, tile, after
        )
        previous = send
        for index, bit in enumerate(stages):
            came = swap(send, "mp", lambda i: i ^ bit)
            if index == 0:
                arrivals.append(came)
            if index + 1 < len(stages):
                keep, send = fold(keep, came, tile)
        block, part = finish(wanted, keep, came, tile, choices, first)
        logits.append(block)
        stats = part if stats is None else merge(stats, part)
        first += width

    for bit in bits_of(batch):
        came = swap(stats, "batch", lambda i: i ^ bit)
        low = (b & bit) == 0
        stats = merge(jnp.where(low, stats, came), jnp.where(low, came, stats))
    normalizer = stats[:, :1] + jnp.log(stats[:, 1:2])
    picked = stats[:, 2 : 2 + choices] - normalizer

    def natural(array):
        array = array.reshape(ratio, heads, rows, array.shape[1])
        return array.transpose(0, 2, 1, 3).reshape(out_rows, heads, array.shape[3])

    log_probs = natural(jnp.concatenate(logits, axis=1) - normalizer)
    picked = natural(picked)
    path_scores = jnp.zeros((out_rows, tree_paths.shape[0]), jnp.float32)
    for head in range(heads):
        found = jnp.zeros_like(path_scores)
        for choice in range(choices):
            taken = tree_paths[:, head][None, :] == choice
            found = jnp.where(taken, picked[:, head, choice : choice + 1], found)
        path_scores = path_scores + found
    return (log_probs, path_scores)


def solution(mesh):
    return jax.shard_map(
        shards,
        mesh=mesh,
        in_specs=(
            P("batch", None, "mp"),
            P("batch"),
            P(),
            P(None, "batch", "mp"),
            P(None, "mp"),
            P("mp", "batch"),
            P("mp", None, None),
            P(),
        ),
        out_specs=(P("mp", None, "batch"), P("mp", None)),
        check_vma=False,
    )
```

```python
import functools

import jax
import jax.numpy as jnp
from jax import lax
from jax.experimental import pallas as pl
from jax.experimental.pallas import tpu as pltpu
from jax.sharding import PartitionSpec as P

EPSILON = 1e-05
MIB = 1024 * 1024
LANES = 128
CODE_BITS = 14
VMEM_LIMIT = 4 * MIB
HEAD_LIMIT = 24 * MIB


def together(*arrays):
    return lax.optimization_barrier(arrays)


def bits_of(count):
    return [1 << i for i in range(count.bit_length() - 1)]


def swap(array, axis, partner):
    return lax.ppermute(array, axis, [(i, partner(i)) for i in range(lax.axis_size(axis))])


def place(index, stages):
    spot = 0
    for bit in stages:
        spot = 2 * spot + (index & bit) // bit
    return spot


def unplace(spot, stages):
    index = 0
    for step, bit in enumerate(stages[::-1]):
        index = index + ((spot >> step) & 1) * bit
    return index


def widest(limit, size):
    tile = min(limit, size)
    while size % tile:
        tile //= 2
    return tile


VMEM = pl.BlockSpec(memory_space=pltpu.VMEM)
ANY = pl.BlockSpec(memory_space=pl.ANY)
WAYS = 4


def copies_in(source, target, sems, first):
    depth, width = target.shape
    share = depth // WAYS
    return [
        pltpu.make_async_copy(
            source.at[pl.ds(way * share, share), pl.ds(first, width)],
            target.at[pl.ds(way * share, share), :],
            sems.at[way],
        )
        for way in range(WAYS)
    ]


def fetch_body(info, weight, *refs, firsts):
    targets, sems = refs[-1 - len(firsts) : -1], refs[-1]
    source = weight.at[info[0]] if len(weight.shape) == 3 else weight
    copies = []
    for index, target in enumerate(targets):
        copies += copies_in(source, target, sems.at[index], firsts[index])
    for copy in copies:
        copy.start()
    for copy in copies:
        copy.wait()


def fetch(info, weight, firsts, width, after, limit=VMEM_LIMIT):
    depth = weight.shape[-2]
    return pl.pallas_call(
        functools.partial(fetch_body, firsts=firsts),
        in_specs=[pl.BlockSpec(memory_space=pltpu.SMEM), ANY] + [ANY] * len(after),
        out_specs=[VMEM] * len(firsts),
        out_shape=[jax.ShapeDtypeStruct((depth, width), weight.dtype)] * len(firsts),
        scratch_shapes=[pltpu.SemaphoreType.DMA((len(firsts), WAYS))],
        compiler_params=pltpu.CompilerParams(vmem_limit_bytes=limit),
        cost_estimate=pl.CostEstimate(
            flops=700 * depth * width * len(firsts), bytes_accessed=0, transcendentals=0
        ),
    )(info, weight, *after)


def head_body(info, came, source, *refs, height, held, firsts):
    weights, refs = refs[:held], refs[held:]
    out, targets, (rows, sems) = refs[0], refs[1:-2], refs[-2:]
    copies = []
    for index, target in enumerate(targets):
        copies += copies_in(source.at[info[0]], target, sems.at[index], firsts[index])
    for copy in copies:
        copy.start()
    for unit in range(came.shape[0] // height):
        start = pl.multiple_of(info[1 + unit] * height, height)
        rows[pl.ds(start, height), :] = came[unit * height : (unit + 1) * height, :]
    at = 0
    for weight in weights:
        width = weight.shape[1]
        tile = widest(512, width)
        for n in range(width // tile):
            total = jnp.dot(
                rows[...], weight[:, n * tile : (n + 1) * tile], preferred_element_type=jnp.float32
            )
            out[:, at : at + tile] = total.astype(out.dtype)
            at += tile
    for copy in copies:
        copy.wait()


def head_matmul(info, came, head_weight, weights, height, out_type, firsts):
    count, depth = came.shape
    wide = weights[0].shape[1]
    width = wide * len(weights)
    return pl.pallas_call(
        functools.partial(head_body, height=height, held=len(weights), firsts=firsts),
        in_specs=[pl.BlockSpec(memory_space=pltpu.SMEM), VMEM, ANY] + [VMEM] * len(weights),
        out_specs=[VMEM] * (1 + len(firsts)),
        out_shape=[jax.ShapeDtypeStruct((count, width), out_type)]
        + [jax.ShapeDtypeStruct((depth, wide), head_weight.dtype)] * len(firsts),
        scratch_shapes=[
            pltpu.VMEM((count, depth), jnp.bfloat16),
            pltpu.SemaphoreType.DMA((max(1, len(firsts)), WAYS)),
        ],
        compiler_params=pltpu.CompilerParams(vmem_limit_bytes=VMEM_LIMIT),
        cost_estimate=pl.CostEstimate(
            flops=2 * count * depth * width, bytes_accessed=count * width, transcendentals=0
        ),
    )(info, came, head_weight, *weights)


def encode(value):
    top = jnp.max(jnp.abs(value), axis=1, keepdims=True)
    power = jnp.floor(jnp.log2(jnp.maximum(top, 1e-30))) + 1.0
    code = jnp.floor(value * jnp.exp2(CODE_BITS - power) + 0.5)
    return code.astype(jnp.int32).astype(jnp.int16), power


def decode(code, power):
    return code.astype(jnp.int32).astype(jnp.float32) * jnp.exp2(power - CODE_BITS)


def marks_of(powers, height):
    lane = lax.broadcasted_iota(jnp.int32, (height, LANES), 1)
    marks = jnp.zeros((height, LANES), jnp.float32)
    for index, power in enumerate(powers):
        marks = jnp.where(lane == index, power, marks)
    return marks.astype(jnp.int32).astype(jnp.int16)


def gather_body(spots, *refs, height):
    parts, rows = refs[:-1], refs[-1]
    unit = 0
    for part in parts:
        for block in range(part.shape[0] // height):
            start = pl.multiple_of(spots[unit] * height, height)
            rows[pl.ds(start, height), :] = part[block * height : (block + 1) * height, :]
            unit += 1


def gather_rows(spots, parts, height):
    count = sum(p.shape[0] for p in parts)
    return pl.pallas_call(
        functools.partial(gather_body, height=height),
        in_specs=[pl.BlockSpec(memory_space=pltpu.SMEM)] + [VMEM] * len(parts),
        out_specs=VMEM,
        out_shape=jax.ShapeDtypeStruct((count, parts[0].shape[1]), parts[0].dtype),
        compiler_params=pltpu.CompilerParams(vmem_limit_bytes=VMEM_LIMIT),
    )(spots, *parts)


def vocab_body(rows, source, *refs, order, tile, counts, firsts):
    held, waits = counts
    weights, refs = refs[:held], refs[held + waits :]
    keep, send = refs[:2]
    targets, sems = refs[2:-1], refs[-1]
    copies = []
    for index, target in enumerate(targets):
        copies += copies_in(source, target, sems.at[index], firsts[index])
    for copy in copies:
        copy.start()
    groups = len(order)
    height = rows.shape[0] // groups
    half = groups // 2
    powers = []
    at = 0
    for weight in weights:
        for n in range(weight.shape[1] // tile):
            total = jnp.dot(
                rows[...], weight[:, n * tile : (n + 1) * tile], preferred_element_type=jnp.float32
            )
            sorted_rows = [total[g * height : (g + 1) * height] for g in order]
            for spot, value in enumerate(sorted_rows[:half]):
                keep[spot * height : (spot + 1) * height, at : at + tile] = value
            code, power = encode(jnp.concatenate(sorted_rows[half:], axis=0))
            send[:, at : at + tile] = code
            powers.append(power)
            at += tile
    send[:, at:] = marks_of(powers, send.shape[0])
    for copy in copies:
        copy.wait()


def vocab_matmul(rows, vocab_weight, weights, order, tile, coming, after):
    depth = vocab_weight.shape[0]
    count = rows.shape[0]
    half = count // 2
    width = sum(w.shape[1] for w in weights)
    return pl.pallas_call(
        functools.partial(
            vocab_body,
            order=order,
            tile=tile,
            counts=(len(weights), len(after)),
            firsts=[first for first, _ in coming],
        ),
        in_specs=[VMEM, ANY] + [VMEM] * len(weights) + [ANY] * len(after),
        out_specs=[VMEM] * (2 + len(coming)),
        out_shape=[
            jax.ShapeDtypeStruct((half, width), jnp.float32),
            jax.ShapeDtypeStruct((half, width + LANES), jnp.int16),
        ]
        + [jax.ShapeDtypeStruct((depth, wide), vocab_weight.dtype) for _, wide in coming],
        scratch_shapes=[pltpu.SemaphoreType.DMA((max(1, len(coming)), WAYS))],
        compiler_params=pltpu.CompilerParams(vmem_limit_bytes=VMEM_LIMIT),
        cost_estimate=pl.CostEstimate(
            flops=2 * count * depth * width, bytes_accessed=2 * depth * width, transcendentals=0
        ),
    )(rows, vocab_weight, *weights, *after)


def fold_body(keep, came, *refs, tile):
    send = refs[-1]
    half = send.shape[0]
    width = keep.shape[1]
    for row in range(half, 2 * half, 16):
        here, there = slice(row, row + 16), slice(row - half, row - half + 16)
        marks = came[here, width:].astype(jnp.int32).astype(jnp.float32)
        powers = []
        for step in range(width // tile):
            block = slice(step * tile, (step + 1) * tile)
            value = keep[here, block] + decode(came[here, block], marks[:, step : step + 1])
            code, power = encode(value)
            send[there, block] = code
            powers.append(power)
        send[there, width:] = marks_of(powers, 16)


def fold(keep, came, tile, after):
    rows, width = keep.shape
    return pl.pallas_call(
        functools.partial(fold_body, tile=tile),
        in_specs=[VMEM] * 2 + [ANY] * len(after),
        out_specs=VMEM,
        out_shape=jax.ShapeDtypeStruct((rows // 2, width + LANES), jnp.int16),
        compiler_params=pltpu.CompilerParams(vmem_limit_bytes=VMEM_LIMIT),
    )(keep, came, *after)


def add_body(keep, came, out, *, tile):
    half, width = out.shape
    for row in range(0, half, 16):
        here = slice(row, row + 16)
        marks = came[here, width:].astype(jnp.int32).astype(jnp.float32)
        for step in range(width // tile):
            block = slice(step * tile, (step + 1) * tile)
            out[here, block] = keep[here, block] + decode(came[here, block], marks[:, step : step + 1])


def add_kept(keep, came, tile):
    rows, width = keep.shape
    return pl.pallas_call(
        functools.partial(add_body, tile=tile),
        in_specs=[VMEM] * 2,
        out_specs=VMEM,
        out_shape=jax.ShapeDtypeStruct((rows // 2, width), jnp.float32),
        compiler_params=pltpu.CompilerParams(vmem_limit_bytes=VMEM_LIMIT),
    )(keep, came)


def finish_body(wanted, keep, *refs, tile, choices, first, arrived):
    arrivals, (logits, stats) = refs[:arrived], refs[-2:]
    rows, width = logits.shape
    height = 16
    lane = lax.broadcasted_iota(jnp.int32, (height, LANES), 1)
    for row in range(0, rows, height):
        here = slice(row, row + height)
        marks = [came[here, width:].astype(jnp.int32).astype(jnp.float32) for came in arrivals]
        ids = wanted[here, :] - first
        columns = [jnp.broadcast_to(ids[:, k : k + 1], (height, LANES)) for k in range(choices)]
        peak = None
        picks = [None] * choices
        for step in range(width // tile):
            block = slice(step * tile, (step + 1) * tile)
            value = keep[here, block]
            for came, mark in zip(arrivals, marks):
                value = value + decode(came[here, block], mark[:, step : step + 1])
            logits[here, block] = value
            for part in range(tile // LANES):
                piece = value[:, part * LANES : (part + 1) * LANES]
                at = lane + (step * tile + part * LANES)
                peak = piece if peak is None else jnp.maximum(peak, piece)
                for k in range(choices):
                    term = jnp.where(at == columns[k], piece, 0.0)
                    picks[k] = term if picks[k] is None else picks[k] + term
        peak = jnp.max(peak, axis=1, keepdims=True)
        total = None
        for part in range(width // LANES):
            term = jnp.exp(logits[here, part * LANES : (part + 1) * LANES] - peak)
            total = term if total is None else total + term
        out = jnp.where(lane == 0, peak, jnp.zeros((height, LANES), jnp.float32))
        for k, item in enumerate([total] + picks):
            out = jnp.where(lane == k + 1, jnp.sum(item, axis=1, keepdims=True), out)
        stats[here, :] = out


def finish(wanted, keep, arrivals, tile, choices, first, after):
    rows, width = wanted.shape[0], keep.shape[1]
    return pl.pallas_call(
        functools.partial(
            finish_body, tile=tile, choices=choices, first=first, arrived=len(arrivals)
        ),
        in_specs=[VMEM] * (2 + len(arrivals)) + [ANY] * len(after),
        out_specs=[VMEM] * 2,
        out_shape=[
            jax.ShapeDtypeStruct((rows, width), jnp.float32),
            jax.ShapeDtypeStruct((rows, LANES), jnp.float32),
        ],
        compiler_params=pltpu.CompilerParams(vmem_limit_bytes=VMEM_LIMIT),
    )(wanted, keep, *arrivals, *after)


def tail_body(stats, tree, *refs, heads, height, choices):
    logits, (log_probs, scores) = refs[:-2], refs[-2:]
    blocks = log_probs.shape[0] // height
    paths = scores.shape[1]
    for block in range(blocks):
        there = slice(block * height, (block + 1) * height)
        score = jnp.zeros((height, paths), jnp.float32)
        for head in range(heads):
            row = (block * heads + head) * height
            here = slice(row, row + height)
            normalizer = stats[here, 0:1] + jnp.log(stats[here, 1:2])
            first = 0
            for part in logits:
                width = part.shape[1]
                log_probs[there, head, first : first + width] = part[here, :] - normalizer
                first += width
            found = jnp.zeros((height, paths), jnp.float32)
            for k in range(choices):
                picked = stats[here, 2 + k : 3 + k] - normalizer
                found = jnp.where(tree[head : head + 1, :] == k, picked, found)
            score = score + found
        scores[there, :] = score


def tail(stats, tree, logits, out_rows, height, choices):
    heads, paths = tree.shape
    width = sum(part.shape[1] for part in logits)
    return pl.pallas_call(
        functools.partial(tail_body, heads=heads, height=height, choices=choices),
        in_specs=[VMEM] * (2 + len(logits)),
        out_specs=[VMEM] * 2,
        out_shape=[
            jax.ShapeDtypeStruct((out_rows, heads, width), jnp.float32),
            jax.ShapeDtypeStruct((out_rows, paths), jnp.float32),
        ],
        compiler_params=pltpu.CompilerParams(vmem_limit_bytes=VMEM_LIMIT),
    )(stats, tree, *logits)


def merge(one, two):
    peak = jnp.maximum(one[:, :1], two[:, :1])
    lane = lax.broadcasted_iota(jnp.int32, one.shape, 1)
    factor_one = jnp.where(lane == 1, jnp.exp(one[:, :1] - peak), 1.0)
    factor_two = jnp.where(lane == 1, jnp.exp(two[:, :1] - peak), 1.0)
    return jnp.where(lane == 0, peak, one * factor_one + two * factor_two)


def shards(
    hidden_states, accepted, norm_gain, head_weight, head_bias, vocab_weight, cand_ids, tree_paths
):
    batch, mp = lax.axis_size("batch"), lax.axis_size("mp")
    b, m = lax.axis_index("batch"), lax.axis_index("mp")
    rows, positions, feat = hidden_states.shape
    heads, inner, _ = head_weight.shape
    vocab_width = vocab_weight.shape[1]
    out_rows, _, choices = cand_ids.shape
    pieces = feat // inner
    ratio = out_rows // rows
    mp_bits = bits_of(mp)
    pair, core = b // 2, b % 2
    pair_bits = [bits_of(batch // 2), bits_of(batch // 2)[::-1]]

    chosen = hidden_states[:, 0, :]
    for position in range(1, positions):
        chosen = jnp.where((accepted == position + 1)[:, None], hidden_states[:, position, :], chosen)
    other = swap(chosen, "batch", lambda i: i ^ 1)
    chosen = jnp.concatenate(
        [jnp.where(core == 0, chosen, other), jnp.where(core == 0, other, chosen)], axis=0
    ).astype(jnp.float32)
    gain = lax.dynamic_slice_in_dim(norm_gain, m * feat, feat, 0)

    if pieces == 2:
        sent = lax.dynamic_slice_in_dim(chosen, core * inner, inner, 1)
        sent_gain = lax.dynamic_slice_in_dim(gain, core * inner, inner, 0)
    else:
        sent = lax.dynamic_slice_in_dim(chosen, core * rows, rows, 0)
        sent_gain = gain
    sent = (sent * sent_gain).astype(jnp.bfloat16)
    perm = []
    for i in range(batch):
        for j in range(mp):
            perm.append((i * mp + j, (j * pieces + i % pieces) * mp + ((i // pieces) ^ j)))
    head_first = (1 - core).astype(jnp.int32).reshape(1)
    head_then = core.astype(jnp.int32).reshape(1)
    part = feat // 2
    head_first = (1 - core).astype(jnp.int32).reshape(1)
    head_then = core.astype(jnp.int32).reshape(1)
    part = feat // 4
    firsts = [part * i for i in range(4)]
    weights_first = fetch(head_first, head_weight, firsts, part, [sent], HEAD_LIMIT)
    weights_then = []
    block = lax.ppermute(sent, ("batch", "mp"), perm)
    block, *weights_first = together(block, *weights_first)
    for bit in mp_bits:
        came = swap(block, "mp", lambda i: i ^ bit)
        if not weights_then:
            fetched = fetch(head_then, head_weight, firsts[:2], part, [block], HEAD_LIMIT)
            came, *weights_then = together(came, *fetched)
        block = jnp.concatenate([block, came], axis=0)

    square_sum = jnp.sum(chosen * chosen, axis=1, keepdims=True)
    for bit in mp_bits:
        square_sum = square_sum + swap(square_sum, "mp", lambda i: i ^ bit)
    row_scale = lax.rsqrt(square_sum / (mp * feat) + EPSILON)
    own_normed = (chosen * row_scale * gain).astype(jnp.bfloat16).astype(jnp.float32)

    spots = []
    for unit in range(batch):
        source = (m ^ (unit // pieces) ^ (b // pieces)) * pieces + unit % pieces
        apart = (source // 2) ^ pair
        spot = jnp.where(core == 0, place(apart, pair_bits[0]), place(apart, pair_bits[1]))
        spots.append(spot * 2 + source % 2)
    info = jnp.stack([core] + spots).astype(jnp.int32)
    send, *fetched = head_matmul(
        info, block, head_weight, weights_first, rows, jnp.bfloat16, firsts[2:]
    )
    weights_then = list(weights_then) + fetched
    came = swap(send, "batch", lambda i: i ^ 1)
    (keep,) = head_matmul(info, block, head_weight, weights_then, rows, jnp.float32, [])
    units = batch // 2
    turned = [place(unplace(u, pair_bits[0]), pair_bits[1]) for u in range(units)]
    came = came.reshape(units, 2 * rows, feat)
    came = jnp.concatenate([came[u] for u in turned], axis=0)
    total = keep + came.astype(jnp.float32)
    unit_width = vocab_width // 16
    held = {}

    def fetch_units(units, after):
        firsts = [unit * unit_width for unit in units]
        held.update(zip(units, fetch(head_then, vocab_weight, firsts, unit_width, after)))

    def wait_for(came, units):
        came, *fetched = together(came, *[held[unit] for unit in units])
        held.update(zip(units, fetched))
        return came

    for step in range(len(pair_bits[0])):
        half = total.shape[0] // 2
        outbound = total[half:].astype(jnp.bfloat16)
        units = (range(0, 4), range(4, 6))[step] if step < 2 else ()
        if units:
            fetch_units(units, [outbound])
        came = swap(outbound, "batch", lambda i: i ^ (2 * pair_bits[i % 2][step]))
        if units:
            came = wait_for(came, units)
        total = total[:half] + came.astype(jnp.float32)
    bias = lax.dynamic_slice_in_dim(head_bias, core, 1, 0)
    before = total * row_scale + bias
    residual = (own_normed + jax.nn.silu(before)).astype(jnp.bfloat16)
    for step in reversed(range(len(pair_bits[0]))):
        came = swap(residual, "batch", lambda i: i ^ (2 * pair_bits[i % 2][step]))
        if step:
            residual = jnp.concatenate([residual, came], axis=0)
    own = [residual, came]
    parts = own + [swap(part, "batch", lambda i: i ^ 1) for part in own]

    table = []
    for whose in (core, 1 - core):
        for unit in range(batch):
            apart = jnp.where(
                whose == 0, unplace(unit // 2, pair_bits[0]), unplace(unit // 2, pair_bits[1])
            )
            source = (pair ^ apart) * 2 + unit % 2
            table.append((((source // ratio) ^ m) * ratio + source % ratio) * heads + whose)
    all_rows = gather_rows(jnp.stack(table).astype(jnp.int32), parts, rows)
    wanted = (cand_ids - b * vocab_width).reshape(ratio, rows, heads, choices)
    wanted = wanted.transpose(0, 2, 1, 3).reshape(out_rows * heads, choices)
    wanted = jnp.pad(wanted, ((0, 0), (0, LANES - choices)), constant_values=-1)

    plan = [
        (range(0, 4), range(6, 8)),
        (range(4, 8), range(8, 12)),
        (range(8, 12), range(12, 16)),
        (range(12, 14), ()),
        (range(14, 16), ()),
    ]
    tile = widest(512, unit_width)
    blocks = len(plan)
    stages = [mp_bits if block % 2 == 0 else mp_bits[::-1] for block in range(blocks)]
    keeps, sends, arrivals = [], [], [[] for _ in plan]

    def begin(block, after):
        units, coming = plan[block]
        order = sorted(range(mp), key=lambda g: place(g, stages[block]))
        keep, send, *fetched = vocab_matmul(
            all_rows,
            vocab_weight,
            [held[u] for u in units],
            order,
            tile,
            [(u * unit_width, unit_width) for u in coming],
            after,
        )
        held.update(zip(coming, fetched))
        keeps.append(keep)
        sends.append(send)
        arrivals[block].append(swap(send, "mp", lambda i: i ^ stages[block][0]))

    def go_on(block, after):
        keep = keeps[block]
        for bit in stages[block][1:]:
            while len(arrivals[block]) > 1:
                rest = arrivals[block].pop(0)
                keep = add_kept(keep, rest, tile)
            send = fold(keep, arrivals[block][-1], tile, after)
            arrivals[block].append(swap(send, "mp", lambda i: i ^ bit))
        keeps[block] = keep
        return send

    begin(0, [])
    begin(1, [sends[0]])
    begin(2, [sends[1]])
    last = go_on(0, [sends[2]])
    begin(3, [last])
    last = go_on(1, [sends[3]])
    begin(4, [last])
    lasts = [go_on(block, [sends[4]]) for block in (2, 3, 4)]
    logits, stats = [], None
    for block, (units, _) in enumerate(plan):
        after = lasts[block : block + 1]
        part, part_stats = finish(
            wanted, keeps[block], arrivals[block], tile, choices, units[0] * unit_width, after
        )
        logits.append(part)
        stats = part_stats if stats is None else merge(stats, part_stats)

    for bit in bits_of(batch):
        came = swap(stats, "batch", lambda i: i ^ bit)
        low = (b & bit) == 0
        stats = merge(jnp.where(low, stats, came), jnp.where(low, came, stats))
    log_probs, path_scores = tail(stats, tree_paths.T, logits, out_rows, rows, choices)
    return (log_probs, path_scores)


def solution(mesh):
    return jax.shard_map(
        shards,
        mesh=mesh,
        in_specs=(
            P("batch", None, "mp"),
            P("batch"),
            P(),
            P(None, "batch", "mp"),
            P(None, "mp"),
            P("mp", "batch"),
            P("mp", None, None),
            P(),
        ),
        out_specs=(P("mp", None, "batch"), P("mp", None)),
        check_vma=False,
    )
```

```python
import functools

import jax
import jax.numpy as jnp
from jax import lax
from jax.experimental import pallas as pl
from jax.experimental.pallas import tpu as pltpu
from jax.sharding import PartitionSpec as P

EPSILON = 1e-05
MIB = 1024 * 1024
LANES = 128
CODE_BITS = 14
VMEM_LIMIT = 4 * MIB
HEAD_LIMIT = 24 * MIB


def together(*arrays):
    return lax.optimization_barrier(arrays)


def bits_of(count):
    return [1 << i for i in range(count.bit_length() - 1)]


def swap(array, axis, partner):
    return lax.ppermute(array, axis, [(i, partner(i)) for i in range(lax.axis_size(axis))])


def place(index, stages):
    spot = 0
    for bit in stages:
        spot = 2 * spot + (index & bit) // bit
    return spot


def unplace(spot, stages):
    index = 0
    for step, bit in enumerate(stages[::-1]):
        index = index + ((spot >> step) & 1) * bit
    return index


def widest(limit, size):
    tile = min(limit, size)
    while size % tile:
        tile //= 2
    return tile


VMEM = pl.BlockSpec(memory_space=pltpu.VMEM)
ANY = pl.BlockSpec(memory_space=pl.ANY)
WAYS = 4


def copy_groups(source, targets, sems, firsts):
    groups = []
    for index, target in enumerate(targets):
        depth, width = target.shape
        share, tile = depth // WAYS, widest(512, width)
        for step in range(width // tile):
            groups.append(
                [
                    pltpu.make_async_copy(
                        source.at[pl.ds(way * share, share), pl.ds(firsts[index] + step * tile, tile)],
                        target.at[pl.ds(way * share, share), pl.ds(step * tile, tile)],
                        sems.at[index, step, way],
                    )
                    for way in range(WAYS)
                ]
            )
    return groups


def group_sems(count, width):
    return pltpu.SemaphoreType.DMA((max(1, count), width // widest(512, width), WAYS))


def start_group(group):
    for copy in group:
        copy.start()


def wait_groups(groups):
    for group in groups:
        for copy in group:
            copy.wait()


def fetch_body(info, weight, *refs, firsts):
    targets, sems = refs[-1 - len(firsts) : -1], refs[-1]
    source = weight.at[info[0]] if len(weight.shape) == 3 else weight
    groups = copy_groups(source, targets, sems, firsts)
    for group in groups:
        start_group(group)
    wait_groups(groups)


def fetch(info, weight, firsts, width, after, limit=VMEM_LIMIT):
    depth = weight.shape[-2]
    return pl.pallas_call(
        functools.partial(fetch_body, firsts=firsts),
        in_specs=[pl.BlockSpec(memory_space=pltpu.SMEM), ANY] + [ANY] * len(after),
        out_specs=[VMEM] * len(firsts),
        out_shape=[jax.ShapeDtypeStruct((depth, width), weight.dtype)] * len(firsts),
        scratch_shapes=[group_sems(len(firsts), width)],
        compiler_params=pltpu.CompilerParams(vmem_limit_bytes=limit),
        cost_estimate=pl.CostEstimate(
            flops=700 * depth * width * len(firsts), bytes_accessed=0, transcendentals=0
        ),
    )(info, weight, *after)


def head_body(info, came, source, *refs, height, held, firsts):
    weights, refs = refs[:held], refs[held:]
    out, targets, (rows, sems) = refs[0], refs[1:-2], refs[-2:]
    groups = copy_groups(source.at[info[0]], targets, sems, firsts)
    waiting = list(groups)
    for unit in range(came.shape[0] // height):
        start = pl.multiple_of(info[1 + unit] * height, height)
        rows[pl.ds(start, height), :] = came[unit * height : (unit + 1) * height, :]
    at = 0
    for weight in weights:
        width = weight.shape[1]
        tile = widest(512, width)
        for n in range(width // tile):
            if waiting:
                start_group(waiting.pop(0))
            total = jnp.dot(
                rows[...], weight[:, n * tile : (n + 1) * tile], preferred_element_type=jnp.float32
            )
            out[:, at : at + tile] = total.astype(out.dtype)
            at += tile
    wait_groups(groups)


def head_matmul(info, came, head_weight, weights, height, out_type, firsts):
    count, depth = came.shape
    wide = weights[0].shape[1]
    width = wide * len(weights)
    return pl.pallas_call(
        functools.partial(head_body, height=height, held=len(weights), firsts=firsts),
        in_specs=[pl.BlockSpec(memory_space=pltpu.SMEM), VMEM, ANY] + [VMEM] * len(weights),
        out_specs=[VMEM] * (1 + len(firsts)),
        out_shape=[jax.ShapeDtypeStruct((count, width), out_type)]
        + [jax.ShapeDtypeStruct((depth, wide), head_weight.dtype)] * len(firsts),
        scratch_shapes=[
            pltpu.VMEM((count, depth), jnp.bfloat16),
            group_sems(len(firsts), wide),
        ],
        compiler_params=pltpu.CompilerParams(vmem_limit_bytes=VMEM_LIMIT),
        cost_estimate=pl.CostEstimate(
            flops=2 * count * depth * width, bytes_accessed=count * width, transcendentals=0
        ),
    )(info, came, head_weight, *weights)


def encode(value):
    top = jnp.max(jnp.abs(value), axis=1, keepdims=True)
    power = jnp.floor(jnp.log2(jnp.maximum(top, 1e-30))) + 1.0
    code = jnp.floor(value * jnp.exp2(CODE_BITS - power) + 0.5)
    return code.astype(jnp.int32).astype(jnp.int16), power


def decode(code, power):
    return code.astype(jnp.int32).astype(jnp.float32) * jnp.exp2(power - CODE_BITS)


def marks_of(powers, height):
    lane = lax.broadcasted_iota(jnp.int32, (height, LANES), 1)
    marks = jnp.zeros((height, LANES), jnp.float32)
    for index, power in enumerate(powers):
        marks = jnp.where(lane == index, power, marks)
    return marks.astype(jnp.int32).astype(jnp.int16)


def gather_body(spots, *refs, height):
    parts, rows = refs[:-1], refs[-1]
    unit = 0
    for part in parts:
        for block in range(part.shape[0] // height):
            start = pl.multiple_of(spots[unit] * height, height)
            rows[pl.ds(start, height), :] = part[block * height : (block + 1) * height, :]
            unit += 1


def gather_rows(spots, parts, height):
    count = sum(p.shape[0] for p in parts)
    return pl.pallas_call(
        functools.partial(gather_body, height=height),
        in_specs=[pl.BlockSpec(memory_space=pltpu.SMEM)] + [VMEM] * len(parts),
        out_specs=VMEM,
        out_shape=jax.ShapeDtypeStruct((count, parts[0].shape[1]), parts[0].dtype),
        compiler_params=pltpu.CompilerParams(vmem_limit_bytes=VMEM_LIMIT),
    )(spots, *parts)


def vocab_body(rows, source, *refs, order, tile, counts, firsts):
    held, waits = counts
    weights, refs = refs[:held], refs[held + waits :]
    keep, send = refs[:2]
    targets, sems = refs[2:-1], refs[-1]
    groups = copy_groups(source, targets, sems, firsts)
    waiting = list(groups)
    height = rows.shape[0] // len(order)
    half = len(order) // 2
    powers = []
    at = 0
    for weight in weights:
        for n in range(weight.shape[1] // tile):
            if waiting:
                start_group(waiting.pop(0))
            total = jnp.dot(
                rows[...], weight[:, n * tile : (n + 1) * tile], preferred_element_type=jnp.float32
            )
            sorted_rows = [total[g * height : (g + 1) * height] for g in order]
            for spot, value in enumerate(sorted_rows[:half]):
                keep[spot * height : (spot + 1) * height, at : at + tile] = value
            code, power = encode(jnp.concatenate(sorted_rows[half:], axis=0))
            send[:, at : at + tile] = code
            powers.append(power)
            at += tile
    send[:, at:] = marks_of(powers, send.shape[0])
    wait_groups(groups)


def vocab_matmul(rows, vocab_weight, weights, order, tile, coming, after):
    depth = vocab_weight.shape[0]
    count = rows.shape[0]
    half = count // 2
    width = sum(w.shape[1] for w in weights)
    return pl.pallas_call(
        functools.partial(
            vocab_body,
            order=order,
            tile=tile,
            counts=(len(weights), len(after)),
            firsts=[first for first, _ in coming],
        ),
        in_specs=[VMEM, ANY] + [VMEM] * len(weights) + [ANY] * len(after),
        out_specs=[VMEM] * (2 + len(coming)),
        out_shape=[
            jax.ShapeDtypeStruct((half, width), jnp.float32),
            jax.ShapeDtypeStruct((half, width + LANES), jnp.int16),
        ]
        + [jax.ShapeDtypeStruct((depth, wide), vocab_weight.dtype) for _, wide in coming],
        scratch_shapes=[group_sems(len(coming), coming[0][1] if coming else width)],
        compiler_params=pltpu.CompilerParams(vmem_limit_bytes=VMEM_LIMIT),
        cost_estimate=pl.CostEstimate(
            flops=2 * count * depth * width, bytes_accessed=2 * depth * width, transcendentals=0
        ),
    )(rows, vocab_weight, *weights, *after)


def fold_body(keep, came, *refs, tile):
    send = refs[-1]
    half = send.shape[0]
    width = keep.shape[1]
    for row in range(half, 2 * half, 16):
        here, there = slice(row, row + 16), slice(row - half, row - half + 16)
        marks = came[here, width:].astype(jnp.int32).astype(jnp.float32)
        powers = []
        for step in range(width // tile):
            block = slice(step * tile, (step + 1) * tile)
            value = keep[here, block] + decode(came[here, block], marks[:, step : step + 1])
            code, power = encode(value)
            send[there, block] = code
            powers.append(power)
        send[there, width:] = marks_of(powers, 16)


def fold(keep, came, tile, after):
    rows, width = keep.shape
    return pl.pallas_call(
        functools.partial(fold_body, tile=tile),
        in_specs=[VMEM] * 2 + [ANY] * len(after),
        out_specs=VMEM,
        out_shape=jax.ShapeDtypeStruct((rows // 2, width + LANES), jnp.int16),
        compiler_params=pltpu.CompilerParams(vmem_limit_bytes=VMEM_LIMIT),
    )(keep, came, *after)


def add_body(keep, came, out, *, tile):
    half, width = out.shape
    for row in range(0, half, 16):
        here = slice(row, row + 16)
        marks = came[here, width:].astype(jnp.int32).astype(jnp.float32)
        for step in range(width // tile):
            block = slice(step * tile, (step + 1) * tile)
            out[here, block] = keep[here, block] + decode(came[here, block], marks[:, step : step + 1])


def add_kept(keep, came, tile):
    rows, width = keep.shape
    return pl.pallas_call(
        functools.partial(add_body, tile=tile),
        in_specs=[VMEM] * 2,
        out_specs=VMEM,
        out_shape=jax.ShapeDtypeStruct((rows // 2, width), jnp.float32),
        compiler_params=pltpu.CompilerParams(vmem_limit_bytes=VMEM_LIMIT),
    )(keep, came)


def merge_rows(one, two):
    peak = jnp.maximum(one[:, :1], two[:, :1])
    lane = lax.broadcasted_iota(jnp.int32, one.shape, 1)
    factor_one = jnp.where(lane == 1, jnp.exp(one[:, :1] - peak), 1.0)
    factor_two = jnp.where(lane == 1, jnp.exp(two[:, :1] - peak), 1.0)
    return jnp.where(lane == 0, peak, one * factor_one + two * factor_two)


def finish_body(wanted, keep, *refs, tile, choices, first, arrived, earlier):
    arrivals, (total_logits, stats, logits, sem) = refs[:arrived], refs[-4:]
    before = refs[arrived] if earlier else None
    rows, width = logits.shape
    height = 16
    lane = lax.broadcasted_iota(jnp.int32, (height, LANES), 1)
    for row in range(0, rows, height):
        here = slice(row, row + height)
        marks = [came[here, width:].astype(jnp.int32).astype(jnp.float32) for came in arrivals]
        ids = wanted[here, :] - first
        columns = [jnp.broadcast_to(ids[:, k : k + 1], (height, LANES)) for k in range(choices)]
        peak = None
        picks = [None] * choices
        for step in range(width // tile):
            block = slice(step * tile, (step + 1) * tile)
            value = keep[here, block]
            for came, mark in zip(arrivals, marks):
                value = value + decode(came[here, block], mark[:, step : step + 1])
            logits[here, block] = value
            for part in range(tile // LANES):
                piece = value[:, part * LANES : (part + 1) * LANES]
                at = lane + (step * tile + part * LANES)
                peak = piece if peak is None else jnp.maximum(peak, piece)
                for k in range(choices):
                    term = jnp.where(at == columns[k], piece, 0.0)
                    picks[k] = term if picks[k] is None else picks[k] + term
        peak = jnp.max(peak, axis=1, keepdims=True)
        total = None
        for part in range(width // LANES):
            term = jnp.exp(logits[here, part * LANES : (part + 1) * LANES] - peak)
            total = term if total is None else total + term
        out = jnp.where(lane == 0, peak, jnp.zeros((height, LANES), jnp.float32))
        for k, item in enumerate([total] + picks):
            out = jnp.where(lane == k + 1, jnp.sum(item, axis=1, keepdims=True), out)
        stats[here, :] = out if before is None else merge_rows(before[here, :], out)
    copy = pltpu.make_async_copy(logits, total_logits.at[:, pl.ds(first, width)], sem)
    copy.start()
    copy.wait()


def finish(wanted, keep, arrivals, tile, choices, first, vocab_width, earlier, after):
    rows, width = wanted.shape[0], keep.shape[1]
    operands = [wanted, keep, *arrivals] + ([earlier[1]] if earlier else [])
    buffer = [earlier[0]] if earlier else []
    return pl.pallas_call(
        functools.partial(
            finish_body,
            tile=tile,
            choices=choices,
            first=first,
            arrived=len(arrivals),
            earlier=bool(earlier),
        ),
        in_specs=[VMEM] * len(operands) + [ANY] * len(buffer + after),
        out_specs=[ANY, VMEM],
        out_shape=[
            jax.ShapeDtypeStruct((rows, vocab_width), jnp.float32),
            jax.ShapeDtypeStruct((rows, LANES), jnp.float32),
        ],
        scratch_shapes=[pltpu.VMEM((rows, width), jnp.float32), pltpu.SemaphoreType.DMA],
        input_output_aliases={len(operands): 0} if earlier else {},
        compiler_params=pltpu.CompilerParams(vmem_limit_bytes=VMEM_LIMIT),
    )(*operands, *buffer, *after)


def merge_body(low, own, came, out):
    first = jnp.where(low[0] == 1, own[...], came[...])
    second = jnp.where(low[0] == 1, came[...], own[...])
    out[...] = merge_rows(first, second)


def merge(low, own, came):
    return pl.pallas_call(
        merge_body,
        in_specs=[pl.BlockSpec(memory_space=pltpu.SMEM), VMEM, VMEM],
        out_specs=VMEM,
        out_shape=jax.ShapeDtypeStruct(own.shape, own.dtype),
        compiler_params=pltpu.CompilerParams(vmem_limit_bytes=VMEM_LIMIT),
    )(low, own, came)


def tail_body(low, own, came, tree, logits, log_probs, scores, stats, *, heads, height, choices):
    merge_body(low, own, came, stats)
    blocks = log_probs.shape[0] // height
    paths = scores.shape[1]
    width = logits.shape[1]
    tile = widest(1024, width)
    for block in range(blocks):
        there = slice(block * height, (block + 1) * height)
        score = jnp.zeros((height, paths), jnp.float32)
        for head in range(heads):
            row = (block * heads + head) * height
            here = slice(row, row + height)
            normalizer = stats[here, 0:1] + jnp.log(stats[here, 1:2])
            for at in range(0, width, tile):
                log_probs[there, head, at : at + tile] = logits[here, at : at + tile] - normalizer
            found = jnp.zeros((height, paths), jnp.float32)
            for k in range(choices):
                picked = stats[here, 2 + k : 3 + k] - normalizer
                found = jnp.where(tree[head : head + 1, :] == k, picked, found)
            score = score + found
        scores[there, :] = score


def tail(low, own, came, tree, logits, out_rows, height, choices):
    heads, paths = tree.shape
    return pl.pallas_call(
        functools.partial(tail_body, heads=heads, height=height, choices=choices),
        in_specs=[pl.BlockSpec(memory_space=pltpu.SMEM)] + [VMEM] * 4,
        out_specs=[VMEM] * 2,
        out_shape=[
            jax.ShapeDtypeStruct((out_rows, heads, logits.shape[1]), jnp.float32),
            jax.ShapeDtypeStruct((out_rows, paths), jnp.float32),
        ],
        scratch_shapes=[pltpu.VMEM(own.shape, own.dtype)],
        compiler_params=pltpu.CompilerParams(vmem_limit_bytes=VMEM_LIMIT),
    )(low, own, came, tree, logits)


def shards(
    hidden_states, accepted, norm_gain, head_weight, head_bias, vocab_weight, cand_ids, tree_paths
):
    batch, mp = lax.axis_size("batch"), lax.axis_size("mp")
    b, m = lax.axis_index("batch"), lax.axis_index("mp")
    rows, positions, feat = hidden_states.shape
    heads, inner, _ = head_weight.shape
    vocab_width = vocab_weight.shape[1]
    out_rows, _, choices = cand_ids.shape
    pieces = feat // inner
    ratio = out_rows // rows
    mp_bits = bits_of(mp)
    pair, core = b // 2, b % 2
    pair_bits = [bits_of(batch // 2), bits_of(batch // 2)[::-1]]

    taken = lax.broadcasted_iota(jnp.int32, (rows, positions, 1), 1) == (accepted - 1)[:, None, None]
    chosen = jnp.sum(jnp.where(taken, hidden_states, 0).astype(jnp.float32), axis=1)
    chosen = chosen.astype(jnp.bfloat16)
    other = swap(chosen, "batch", lambda i: i ^ 1)
    chosen = jnp.concatenate(
        [jnp.where(core == 0, chosen, other), jnp.where(core == 0, other, chosen)], axis=0
    ).astype(jnp.float32)
    gain = lax.dynamic_slice_in_dim(norm_gain, m * feat, feat, 0)

    if pieces == 2:
        sent = lax.dynamic_slice_in_dim(chosen, core * inner, inner, 1)
        sent_gain = lax.dynamic_slice_in_dim(gain, core * inner, inner, 0)
    else:
        sent = lax.dynamic_slice_in_dim(chosen, core * rows, rows, 0)
        sent_gain = gain
    sent = (sent * sent_gain).astype(jnp.bfloat16)
    perm = []
    for i in range(batch):
        for j in range(mp):
            perm.append((i * mp + j, (j * pieces + i % pieces) * mp + ((i // pieces) ^ j)))
    head_first = (1 - core).astype(jnp.int32).reshape(1)
    head_then = core.astype(jnp.int32).reshape(1)
    part = feat // 2
    head_first = (1 - core).astype(jnp.int32).reshape(1)
    head_then = core.astype(jnp.int32).reshape(1)
    part = feat // 4
    firsts = [part * i for i in range(4)]
    weights_first = fetch(head_first, head_weight, firsts, part, [sent], HEAD_LIMIT)
    weights_then = []
    block = lax.ppermute(sent, ("batch", "mp"), perm)
    block, *weights_first = together(block, *weights_first)
    for bit in mp_bits:
        came = swap(block, "mp", lambda i: i ^ bit)
        if not weights_then:
            fetched = fetch(head_then, head_weight, firsts[:2], part, [block], HEAD_LIMIT)
            came, *weights_then = together(came, *fetched)
        block = jnp.concatenate([block, came], axis=0)

    square_sum = jnp.sum(chosen * chosen, axis=1, keepdims=True)
    for bit in mp_bits:
        square_sum = square_sum + swap(square_sum, "mp", lambda i: i ^ bit)
    row_scale = lax.rsqrt(square_sum / (mp * feat) + EPSILON)
    own_normed = (chosen * row_scale * gain).astype(jnp.bfloat16).astype(jnp.float32)

    spots = []
    for unit in range(batch):
        source = (m ^ (unit // pieces) ^ (b // pieces)) * pieces + unit % pieces
        apart = (source // 2) ^ pair
        spot = jnp.where(core == 0, place(apart, pair_bits[0]), place(apart, pair_bits[1]))
        spots.append(spot * 2 + source % 2)
    info = jnp.stack([core] + spots).astype(jnp.int32)
    send, *fetched = head_matmul(
        info, block, head_weight, weights_first, rows, jnp.bfloat16, firsts[2:]
    )
    weights_then = list(weights_then) + fetched
    came = swap(send, "batch", lambda i: i ^ 1)
    (keep,) = head_matmul(info, block, head_weight, weights_then, rows, jnp.float32, [])
    units = batch // 2
    turned = [place(unplace(u, pair_bits[0]), pair_bits[1]) for u in range(units)]
    came = came.reshape(units, 2 * rows, feat)
    came = jnp.concatenate([came[u] for u in turned], axis=0)
    total = keep + came.astype(jnp.float32)
    unit_width = vocab_width // 8

    for step in range(len(pair_bits[0])):
        half = total.shape[0] // 2
        outbound = total[half:].astype(jnp.bfloat16)
        came = swap(outbound, "batch", lambda i: i ^ (2 * pair_bits[i % 2][step]))
        total = total[:half] + came.astype(jnp.float32)
    bias = lax.dynamic_slice_in_dim(head_bias, core, 1, 0)
    before = total * row_scale + bias
    residual = (own_normed + jax.nn.silu(before)).astype(jnp.bfloat16)
    (ahead,) = fetch(head_then, vocab_weight, [0], 2 * unit_width, [residual])
    for step in reversed(range(len(pair_bits[0]))):
        came = swap(residual, "batch", lambda i: i ^ (2 * pair_bits[i % 2][step]))
        if step == len(pair_bits[0]) - 1:
            came, ahead = together(came, ahead)
        if step:
            residual = jnp.concatenate([residual, came], axis=0)
    own = [residual, came]
    parts = own + [swap(part, "batch", lambda i: i ^ 1) for part in own]

    table = []
    for whose in (core, 1 - core):
        for unit in range(batch):
            apart = jnp.where(
                whose == 0, unplace(unit // 2, pair_bits[0]), unplace(unit // 2, pair_bits[1])
            )
            source = (pair ^ apart) * 2 + unit % 2
            table.append((((source // ratio) ^ m) * ratio + source % ratio) * heads + whose)
    all_rows = gather_rows(jnp.stack(table).astype(jnp.int32), parts, rows)
    wanted = (cand_ids - b * vocab_width).reshape(ratio, rows, heads, choices)
    wanted = wanted.transpose(0, 2, 1, 3).reshape(out_rows * heads, choices)
    wanted = jnp.pad(wanted, ((0, 0), (0, LANES - choices)), constant_values=-1)

    held = {(0, 1): ahead}
    plan = [((0, 1), (2, 3)), ((2, 3), (4, 5)), ((4, 5), (6, 7)), ((6,), ()), ((7,), ())]
    tile = widest(512, unit_width)
    blocks = len(plan)
    stages = [mp_bits if block % 2 == 0 else mp_bits[::-1] for block in range(blocks)]
    keeps, sends, arrivals = [], [], [[] for _ in plan]

    def begin(block, after):
        units, coming = plan[block]
        order = sorted(range(mp), key=lambda g: place(g, stages[block]))
        keep, send, *fetched = vocab_matmul(
            all_rows,
            vocab_weight,
            [held[units]] if units in held else [held[u] for u in units],
            order,
            tile,
            [(u * unit_width, unit_width) for u in coming],
            after,
        )
        held.update(zip(coming, fetched))
        keeps.append(keep)
        sends.append(send)
        arrivals[block].append(swap(send, "mp", lambda i: i ^ stages[block][0]))

    def go_on(block, after):
        keep = keeps[block]
        for bit in stages[block][1:]:
            while len(arrivals[block]) > 1:
                rest = arrivals[block].pop(0)
                keep = add_kept(keep, rest, tile)
            send = fold(keep, arrivals[block][-1], tile, after)
            arrivals[block].append(swap(send, "mp", lambda i: i ^ bit))
        keeps[block] = keep
        return send

    begin(0, [])
    begin(1, [sends[0]])
    begin(2, [sends[1]])
    last = go_on(0, [sends[2]])
    begin(3, [last])
    last = go_on(1, [sends[3]])
    begin(4, [last])
    lasts = [go_on(block, [sends[4]]) for block in (2, 3, 4)]
    joined = None
    for block, (units, _) in enumerate(plan):
        first = units[0] * unit_width
        joined = finish(
            wanted,
            keeps[block],
            arrivals[block],
            tile,
            choices,
            first,
            vocab_width,
            joined,
            lasts[block : block + 1],
        )
    logits, stats = joined

    for bit in bits_of(batch):
        came = swap(stats, "batch", lambda i: i ^ bit)
        low = (1 - (b & bit) // bit).astype(jnp.int32).reshape(1)
        if 2 * bit < batch:
            stats = merge(low, stats, came)
    log_probs, path_scores = tail(
        low, stats, came, tree_paths.T, logits, out_rows, rows, choices
    )
    return (log_probs, path_scores)


def solution(mesh):
    return jax.shard_map(
        shards,
        mesh=mesh,
        in_specs=(
            P("batch", None, "mp"),
            P("batch"),
            P(),
            P(None, "batch", "mp"),
            P(None, "mp"),
            P("mp", "batch"),
            P("mp", None, None),
            P(),
        ),
        out_specs=(P("mp", None, "batch"), P("mp", None)),
        check_vma=False,
    )
```

```python
import functools

import jax
import jax.numpy as jnp
from jax import lax
from jax.experimental import pallas as pl
from jax.experimental.pallas import tpu as pltpu
from jax.sharding import PartitionSpec as P

EPSILON = 1e-05
MIB = 1024 * 1024
LANES = 128
CODE_BITS = 14
VMEM_LIMIT = 4 * MIB
HEAD_LIMIT = 24 * MIB
VOCAB_LIMIT = 20 * MIB


def together(*arrays):
    return lax.optimization_barrier(arrays)


def bits_of(count):
    return [1 << i for i in range(count.bit_length() - 1)]


def swap(array, axis, partner):
    return lax.ppermute(array, axis, [(i, partner(i)) for i in range(lax.axis_size(axis))])


def place(index, stages):
    spot = 0
    for bit in stages:
        spot = 2 * spot + (index & bit) // bit
    return spot


def unplace(spot, stages):
    index = 0
    for step, bit in enumerate(stages[::-1]):
        index = index + ((spot >> step) & 1) * bit
    return index


def widest(limit, size):
    tile = min(limit, size)
    while size % tile:
        tile //= 2
    return tile


VMEM = pl.BlockSpec(memory_space=pltpu.VMEM)
ANY = pl.BlockSpec(memory_space=pl.ANY)
WAYS = 4


def copy_groups(source, targets, sems, firsts):
    groups = []
    for index, target in enumerate(targets):
        depth, width = target.shape
        share, tile = depth // WAYS, widest(512, width)
        for step in range(width // tile):
            groups.append(
                [
                    pltpu.make_async_copy(
                        source.at[pl.ds(way * share, share), pl.ds(firsts[index] + step * tile, tile)],
                        target.at[pl.ds(way * share, share), pl.ds(step * tile, tile)],
                        sems.at[index, step, way],
                    )
                    for way in range(WAYS)
                ]
            )
    return groups


def group_sems(count, width):
    return pltpu.SemaphoreType.DMA((max(1, count), width // widest(512, width), WAYS))


def start_group(group):
    for copy in group:
        copy.start()


def wait_groups(groups):
    for group in groups:
        for copy in group:
            copy.wait()


def fetch_body(info, weight, *refs, firsts):
    targets, sems = refs[-1 - len(firsts) : -1], refs[-1]
    source = weight.at[info[0]] if len(weight.shape) == 3 else weight
    groups = copy_groups(source, targets, sems, firsts)
    for group in groups:
        start_group(group)
    wait_groups(groups)


def fetch(info, weight, firsts, width, after, limit=VMEM_LIMIT):
    depth = weight.shape[-2]
    return pl.pallas_call(
        functools.partial(fetch_body, firsts=firsts),
        in_specs=[pl.BlockSpec(memory_space=pltpu.SMEM), ANY] + [ANY] * len(after),
        out_specs=[VMEM] * len(firsts),
        out_shape=[jax.ShapeDtypeStruct((depth, width), weight.dtype)] * len(firsts),
        scratch_shapes=[group_sems(len(firsts), width)],
        compiler_params=pltpu.CompilerParams(vmem_limit_bytes=limit),
        cost_estimate=pl.CostEstimate(
            flops=700 * depth * width * len(firsts), bytes_accessed=0, transcendentals=0
        ),
    )(info, weight, *after)


def head_body(info, came, source, *refs, height, held, firsts):
    weights, refs = refs[:held], refs[held:]
    out, targets, (rows, sems) = refs[0], refs[1:-2], refs[-2:]
    groups = copy_groups(source.at[info[0]], targets, sems, firsts)
    for unit in range(came.shape[0] // height):
        start = pl.multiple_of(info[1 + unit] * height, height)
        rows[pl.ds(start, height), :] = came[unit * height : (unit + 1) * height, :]
    waiting = list(groups)
    first = 0
    for weight in weights:
        width = weight.shape[1]
        tile = widest(512, width)
        for group in waiting[: width // tile]:
            start_group(group)
        waiting = waiting[width // tile :]

        def step(n, carry, weight=weight, tile=tile, first=first):
            at = pl.multiple_of(n * tile, tile)
            total = jnp.dot(
                rows[...], weight[:, pl.ds(at, tile)], preferred_element_type=jnp.float32
            )
            out[:, pl.ds(pl.multiple_of(first + at, tile), tile)] = total.astype(out.dtype)
            return carry

        lax.fori_loop(0, width // tile, step, 0)
        first += width
    wait_groups(groups)


def head_matmul(info, came, head_weight, weights, height, out_type, firsts):
    count, depth = came.shape
    wide = weights[0].shape[1]
    width = wide * len(weights)
    return pl.pallas_call(
        functools.partial(head_body, height=height, held=len(weights), firsts=firsts),
        in_specs=[pl.BlockSpec(memory_space=pltpu.SMEM), VMEM, ANY] + [VMEM] * len(weights),
        out_specs=[VMEM] * (1 + len(firsts)),
        out_shape=[jax.ShapeDtypeStruct((count, width), out_type)]
        + [jax.ShapeDtypeStruct((depth, wide), head_weight.dtype)] * len(firsts),
        scratch_shapes=[
            pltpu.VMEM((count, depth), jnp.bfloat16),
            group_sems(len(firsts), wide),
        ],
        compiler_params=pltpu.CompilerParams(vmem_limit_bytes=VMEM_LIMIT),
        cost_estimate=pl.CostEstimate(
            flops=2 * count * depth * width, bytes_accessed=count * width, transcendentals=0
        ),
    )(info, came, head_weight, *weights)


def encode(value):
    top = jnp.max(jnp.abs(value), axis=1, keepdims=True)
    power = jnp.floor(jnp.log2(jnp.maximum(top, 1e-30))) + 1.0
    code = jnp.floor(value * jnp.exp2(CODE_BITS - power) + 0.5)
    return code.astype(jnp.int32).astype(jnp.int16), power


def decode(code, power):
    return code.astype(jnp.int32).astype(jnp.float32) * jnp.exp2(power - CODE_BITS)


def marks_of(powers, height):
    lane = lax.broadcasted_iota(jnp.int32, (height, LANES), 1)
    marks = jnp.zeros((height, LANES), jnp.float32)
    for index, power in enumerate(powers):
        marks = jnp.where(lane == index, power, marks)
    return marks.astype(jnp.int32).astype(jnp.int16)


def gather_body(spots, *refs, height, halves):
    parts, rows = refs[:-1], refs[-1]
    share = rows.shape[1] // halves
    unit = 0
    for part in parts:
        for block in range(part.shape[0] // height):
            for half in range(halves):
                start = pl.multiple_of(spots[unit] * height, height)
                columns = slice(half * share, (half + 1) * share)
                rows[pl.ds(start, height), columns] = part[
                    block * height : (block + 1) * height, columns
                ]
                unit += 1


def gather_rows(spots, parts, height, halves):
    count = sum(p.shape[0] for p in parts)
    return pl.pallas_call(
        functools.partial(gather_body, height=height, halves=halves),
        in_specs=[pl.BlockSpec(memory_space=pltpu.SMEM)] + [VMEM] * len(parts),
        out_specs=VMEM,
        out_shape=jax.ShapeDtypeStruct((count, parts[0].shape[1]), parts[0].dtype),
        compiler_params=pltpu.CompilerParams(vmem_limit_bytes=VMEM_LIMIT),
    )(spots, *parts)


def vocab_body(rows, *refs, order, tile, waits):
    weights, (keep, send, powers) = refs[:WAYS], refs[WAYS + waits :]
    step = pl.program_id(0)
    share = rows.shape[1] // WAYS
    total = None
    for way in range(WAYS):
        term = jnp.dot(
            rows[:, way * share : (way + 1) * share],
            weights[way][...],
            preferred_element_type=jnp.float32,
        )
        total = term if total is None else total + term
    height = rows.shape[0] // len(order)
    half = len(order) // 2
    sorted_rows = [total[g * height : (g + 1) * height] for g in order]
    for spot, value in enumerate(sorted_rows[:half]):
        keep[spot * height : (spot + 1) * height, :] = value
    code, power = encode(jnp.concatenate(sorted_rows[half:], axis=0))
    send[:, pl.ds(pl.multiple_of(step * tile, tile), tile)] = code
    lane = lax.broadcasted_iota(jnp.int32, powers.shape, 1)

    @pl.when(step == 0)
    def _():
        powers[...] = jnp.where(lane == 0, power, jnp.zeros_like(powers))

    @pl.when(step > 0)
    def _():
        powers[...] = jnp.where(lane == step, power, powers[...])

    @pl.when(step == pl.num_programs(0) - 1)
    def _():
        send[:, send.shape[1] - LANES :] = powers[...].astype(jnp.int32).astype(jnp.int16)


def vocab_matmul(rows, vocab_weight, first, width, order, tile, after):
    depth = vocab_weight.shape[0]
    count = rows.shape[0]
    half = count // 2
    base = first // tile
    share = depth // WAYS
    weight_specs = [
        pl.BlockSpec((share, tile), functools.partial(lambda way, n: (way, base + n), way))
        for way in range(WAYS)
    ]
    return pl.pallas_call(
        functools.partial(vocab_body, order=order, tile=tile, waits=len(after)),
        grid=(width // tile,),
        in_specs=[VMEM] + weight_specs + [ANY] * len(after),
        out_specs=[
            pl.BlockSpec((half, tile), lambda n: (0, n)),
            pl.BlockSpec((half, width + LANES), lambda n: (0, 0)),
        ],
        out_shape=[
            jax.ShapeDtypeStruct((half, width), jnp.float32),
            jax.ShapeDtypeStruct((half, width + LANES), jnp.int16),
        ],
        scratch_shapes=[pltpu.VMEM((half, LANES), jnp.float32)],
        compiler_params=pltpu.CompilerParams(vmem_limit_bytes=VOCAB_LIMIT),
        cost_estimate=pl.CostEstimate(
            flops=2 * count * depth * width, bytes_accessed=2 * depth * width, transcendentals=0
        ),
    )(rows, *[vocab_weight] * WAYS, *after)


def fold_body(keep, came, *refs, tile):
    send = refs[-1]
    half = send.shape[0]
    width = keep.shape[1]
    for row in range(half, 2 * half, 16):
        here, there = slice(row, row + 16), slice(row - half, row - half + 16)
        marks = came[here, width:].astype(jnp.int32).astype(jnp.float32)
        powers = []
        for step in range(width // tile):
            block = slice(step * tile, (step + 1) * tile)
            value = keep[here, block] + decode(came[here, block], marks[:, step : step + 1])
            code, power = encode(value)
            send[there, block] = code
            powers.append(power)
        send[there, width:] = marks_of(powers, 16)


def fold(keep, came, tile, after):
    rows, width = keep.shape
    return pl.pallas_call(
        functools.partial(fold_body, tile=tile),
        in_specs=[VMEM] * 2 + [ANY] * len(after),
        out_specs=VMEM,
        out_shape=jax.ShapeDtypeStruct((rows // 2, width + LANES), jnp.int16),
        compiler_params=pltpu.CompilerParams(vmem_limit_bytes=VMEM_LIMIT),
    )(keep, came, *after)


def add_body(keep, came, out, *, tile):
    half, width = out.shape
    for row in range(0, half, 16):
        here = slice(row, row + 16)
        marks = came[here, width:].astype(jnp.int32).astype(jnp.float32)
        for step in range(width // tile):
            block = slice(step * tile, (step + 1) * tile)
            out[here, block] = keep[here, block] + decode(came[here, block], marks[:, step : step + 1])


def add_kept(keep, came, tile):
    rows, width = keep.shape
    return pl.pallas_call(
        functools.partial(add_body, tile=tile),
        in_specs=[VMEM] * 2,
        out_specs=VMEM,
        out_shape=jax.ShapeDtypeStruct((rows // 2, width), jnp.float32),
        compiler_params=pltpu.CompilerParams(vmem_limit_bytes=VMEM_LIMIT),
    )(keep, came)


def merge_rows(one, two):
    peak = jnp.maximum(one[:, :1], two[:, :1])
    lane = lax.broadcasted_iota(jnp.int32, one.shape, 1)
    factor_one = jnp.where(lane == 1, jnp.exp(one[:, :1] - peak), 1.0)
    factor_two = jnp.where(lane == 1, jnp.exp(two[:, :1] - peak), 1.0)
    return jnp.where(lane == 0, peak, one * factor_one + two * factor_two)


def finish_body(wanted, *refs, tile, choices, first, counts, earlier):
    blocks = []
    for count in counts:
        blocks.append((refs[0], refs[1 : 1 + count]))
        refs = refs[1 + count :]
    before = refs[0] if earlier else None
    total_logits, stats, logits, sems = refs[-4:]
    rows, width = logits.shape
    height = 16
    lane = lax.broadcasted_iota(jnp.int32, (height, LANES), 1)
    copies = []
    for index, row in enumerate(range(0, rows, height)):
        here = slice(row, row + height)
        ids = wanted[here, :] - first
        columns = [jnp.broadcast_to(ids[:, k : k + 1], (height, LANES)) for k in range(choices)]
        peak = None
        picks = [None] * choices
        start = 0
        for keep, arrivals in blocks:
            wide = keep.shape[1]
            marks = [came[here, wide:].astype(jnp.int32).astype(jnp.float32) for came in arrivals]
            for step in range(wide // tile):
                block = slice(step * tile, (step + 1) * tile)
                value = keep[here, block]
                for came, mark in zip(arrivals, marks):
                    value = value + decode(came[here, block], mark[:, step : step + 1])
                logits[here, start : start + tile] = value
                for part in range(tile // LANES):
                    piece = value[:, part * LANES : (part + 1) * LANES]
                    at = lane + (start + part * LANES)
                    peak = piece if peak is None else jnp.maximum(peak, piece)
                    for k in range(choices):
                        term = jnp.where(at == columns[k], piece, 0.0)
                        picks[k] = term if picks[k] is None else picks[k] + term
                start += tile
        copies.append(
            pltpu.make_async_copy(
                logits.at[pl.ds(row, height), :],
                total_logits.at[pl.ds(row, height), pl.ds(first, width)],
                sems.at[index],
            )
        )
        copies[-1].start()
        peak = jnp.max(peak, axis=1, keepdims=True)
        total = None
        for part in range(width // LANES):
            term = jnp.exp(logits[here, part * LANES : (part + 1) * LANES] - peak)
            total = term if total is None else total + term
        out = jnp.where(lane == 0, peak, jnp.zeros((height, LANES), jnp.float32))
        for k, item in enumerate([total] + picks):
            out = jnp.where(lane == k + 1, jnp.sum(item, axis=1, keepdims=True), out)
        stats[here, :] = out if before is None else merge_rows(before[here, :], out)
    for copy in copies:
        copy.wait()


def finish(wanted, blocks, tile, choices, first, vocab_width, earlier, after):
    rows = wanted.shape[0]
    width = sum(keep.shape[1] for keep, _ in blocks)
    operands = [wanted]
    for keep, arrivals in blocks:
        operands += [keep, *arrivals]
    operands += [earlier[1]] if earlier else []
    buffer = [earlier[0]] if earlier else []
    return pl.pallas_call(
        functools.partial(
            finish_body,
            tile=tile,
            choices=choices,
            first=first,
            counts=[len(arrivals) for _, arrivals in blocks],
            earlier=bool(earlier),
        ),
        in_specs=[VMEM] * len(operands) + [ANY] * len(buffer + after),
        out_specs=[ANY, VMEM],
        out_shape=[
            jax.ShapeDtypeStruct((rows, vocab_width), jnp.float32),
            jax.ShapeDtypeStruct((rows, LANES), jnp.float32),
        ],
        scratch_shapes=[
            pltpu.VMEM((rows, width), jnp.float32),
            pltpu.SemaphoreType.DMA((rows // 16,)),
        ],
        input_output_aliases={len(operands): 0} if earlier else {},
        compiler_params=pltpu.CompilerParams(vmem_limit_bytes=VOCAB_LIMIT),
    )(*operands, *buffer, *after)


def merge_body(low, own, came, out):
    first = jnp.where(low[0] == 1, own[...], came[...])
    second = jnp.where(low[0] == 1, came[...], own[...])
    out[...] = merge_rows(first, second)


def merge(low, own, came):
    return pl.pallas_call(
        merge_body,
        in_specs=[pl.BlockSpec(memory_space=pltpu.SMEM), VMEM, VMEM],
        out_specs=VMEM,
        out_shape=jax.ShapeDtypeStruct(own.shape, own.dtype),
        compiler_params=pltpu.CompilerParams(vmem_limit_bytes=VMEM_LIMIT),
    )(low, own, came)


def tail_body(low, own, came, tree, logits, log_probs, scores, stats, *, heads, height, choices):
    merge_body(low, own, came, stats)
    blocks = log_probs.shape[0] // height
    paths = scores.shape[1]
    width = logits.shape[1]
    tile = widest(1024, width)
    for block in range(blocks):
        there = slice(block * height, (block + 1) * height)
        score = jnp.zeros((height, paths), jnp.float32)
        for head in range(heads):
            row = (block * heads + head) * height
            here = slice(row, row + height)
            normalizer = stats[here, 0:1] + jnp.log(stats[here, 1:2])
            for at in range(0, width, tile):
                log_probs[there, head, at : at + tile] = logits[here, at : at + tile] - normalizer
            found = jnp.zeros((height, paths), jnp.float32)
            for k in range(choices):
                picked = stats[here, 2 + k : 3 + k] - normalizer
                found = jnp.where(tree[head : head + 1, :] == k, picked, found)
            score = score + found
        scores[there, :] = score


def tail(low, own, came, tree, logits, out_rows, height, choices):
    heads, paths = tree.shape
    return pl.pallas_call(
        functools.partial(tail_body, heads=heads, height=height, choices=choices),
        in_specs=[pl.BlockSpec(memory_space=pltpu.SMEM)] + [VMEM] * 4,
        out_specs=[VMEM] * 2,
        out_shape=[
            jax.ShapeDtypeStruct((out_rows, heads, logits.shape[1]), jnp.float32),
            jax.ShapeDtypeStruct((out_rows, paths), jnp.float32),
        ],
        scratch_shapes=[pltpu.VMEM(own.shape, own.dtype)],
        compiler_params=pltpu.CompilerParams(vmem_limit_bytes=VMEM_LIMIT),
    )(low, own, came, tree, logits)


def shards(
    hidden_states, accepted, norm_gain, head_weight, head_bias, vocab_weight, cand_ids, tree_paths
):
    batch, mp = lax.axis_size("batch"), lax.axis_size("mp")
    b, m = lax.axis_index("batch"), lax.axis_index("mp")
    rows, positions, feat = hidden_states.shape
    heads, inner, _ = head_weight.shape
    vocab_width = vocab_weight.shape[1]
    out_rows, _, choices = cand_ids.shape
    pieces = feat // inner
    ratio = out_rows // rows
    mp_bits = bits_of(mp)
    pair, core = b // 2, b % 2
    pair_bits = bits_of(batch // 2)

    taken = lax.broadcasted_iota(jnp.int32, (rows, positions, 1), 1) == (accepted - 1)[:, None, None]
    chosen = jnp.sum(jnp.where(taken, hidden_states, 0).astype(jnp.float32), axis=1)
    chosen = chosen.astype(jnp.bfloat16)
    other = swap(chosen, "batch", lambda i: i ^ 1)
    chosen = jnp.concatenate(
        [jnp.where(core == 0, chosen, other), jnp.where(core == 0, other, chosen)], axis=0
    ).astype(jnp.float32)
    gain = lax.dynamic_slice_in_dim(norm_gain, m * feat, feat, 0)

    if pieces == 2:
        sent = lax.dynamic_slice_in_dim(chosen, core * inner, inner, 1)
        sent_gain = lax.dynamic_slice_in_dim(gain, core * inner, inner, 0)
    else:
        sent = lax.dynamic_slice_in_dim(chosen, core * rows, rows, 0)
        sent_gain = gain
    sent = (sent * sent_gain).astype(jnp.bfloat16)
    perm = []
    for i in range(batch):
        for j in range(mp):
            perm.append((i * mp + j, (j * pieces + i % pieces) * mp + ((i // pieces) ^ j)))
    head_first = (1 - core).astype(jnp.int32).reshape(1)
    head_then = core.astype(jnp.int32).reshape(1)
    part = feat // 2
    head_first = (1 - core).astype(jnp.int32).reshape(1)
    head_then = core.astype(jnp.int32).reshape(1)
    part = feat // 4
    firsts = [part * i for i in range(4)]
    weights_first = fetch(head_first, head_weight, firsts, part, [sent], HEAD_LIMIT)
    weights_then = []
    block = lax.ppermute(sent, ("batch", "mp"), perm)
    block, *weights_first = together(block, *weights_first)
    for bit in mp_bits:
        came = swap(block, "mp", lambda i: i ^ bit)
        if not weights_then:
            fetched = fetch(head_then, head_weight, firsts[:2], part, [block], HEAD_LIMIT)
            came, *weights_then = together(came, *fetched)
        block = jnp.concatenate([block, came], axis=0)

    square_sum = jnp.sum(chosen * chosen, axis=1, keepdims=True)
    for bit in mp_bits:
        square_sum = square_sum + swap(square_sum, "mp", lambda i: i ^ bit)
    row_scale = lax.rsqrt(square_sum / (mp * feat) + EPSILON)
    own_normed = (chosen * row_scale * gain).astype(jnp.bfloat16).astype(jnp.float32)

    spots = []
    for unit in range(batch):
        source = (m ^ (unit // pieces) ^ (b // pieces)) * pieces + unit % pieces
        spots.append(((source // 2) ^ pair) * 2 + source % 2)
    info = jnp.stack([core] + spots).astype(jnp.int32)
    send, *fetched = head_matmul(
        info, block, head_weight, weights_first, rows, jnp.bfloat16, firsts[2:]
    )
    weights_then = list(weights_then) + fetched
    came = swap(send, "batch", lambda i: i ^ 1)
    (keep,) = head_matmul(info, block, head_weight, weights_then, rows, jnp.float32, [])
    units = batch // 2
    share = feat // 2
    tall = 2 * rows
    orders = (pair_bits, pair_bits[::-1])
    total = keep + came.astype(jnp.float32)
    halves = [
        {u: total[u * tall : (u + 1) * tall, h * share : (h + 1) * share] for u in range(units)}
        for h in range(2)
    ]
    for step in range(len(pair_bits)):
        arrived = []
        for half, order in zip(halves, orders):
            leave = [u for u in half if u & order[step]]
            outbound = jnp.concatenate([half[u] for u in leave], axis=0).astype(jnp.bfloat16)
            arrived.append(swap(outbound, "batch", lambda i: i ^ (2 * order[step])))
        for h, order in enumerate(orders):
            stay = [u for u in halves[h] if not u & order[step]]
            halves[h] = {
                u: halves[h][u] + arrived[h][i * tall : (i + 1) * tall].astype(jnp.float32)
                for i, u in enumerate(stay)
            }
    bias = lax.dynamic_slice_in_dim(head_bias, core, 1, 0)
    before = jnp.concatenate([half[0] for half in halves], axis=1) * row_scale + bias
    residual = (own_normed + jax.nn.silu(before)).astype(jnp.bfloat16)
    filled = [residual[:, :share], residual[:, share:]]
    held = [[0], [0]]
    parts, others = [], []
    block = residual
    for step in reversed(range(len(pair_bits))):
        arrived = [
            swap(filled[h], "batch", lambda i: i ^ (2 * orders[h][step])) for h in range(2)
        ]
        for h in range(2):
            held[h] = held[h] + [u ^ orders[h][step] for u in held[h]]
        came = jnp.concatenate(arrived, axis=1)
        if step == 0:
            parts.append(block)
            others.append(swap(block, "batch", lambda i: i ^ 1))
            block = came
        else:
            block = jnp.concatenate([block, came], axis=0)
            filled = [block[:, :share], block[:, share:]]
    parts.append(block)
    others.append(swap(block, "batch", lambda i: i ^ 1))

    table = []
    for whose in (core, 1 - core):
        for unit in range(batch):
            for h in range(2):
                source = (pair ^ held[h][unit // 2]) * 2 + unit % 2
                table.append((((source // ratio) ^ m) * ratio + source % ratio) * heads + whose)
    all_rows = gather_rows(jnp.stack(table).astype(jnp.int32), parts + others, rows, 2)
    wanted = (cand_ids - b * vocab_width).reshape(ratio, rows, heads, choices)
    wanted = wanted.transpose(0, 2, 1, 3).reshape(out_rows * heads, choices)
    wanted = jnp.pad(wanted, ((0, 0), (0, LANES - choices)), constant_values=-1)

    unit_width = vocab_width // 8
    plan = [(0, 2), (2, 2), (4, 2), (6, 1), (7, 1)]
    plan = [(first * unit_width, count * unit_width) for first, count in plan]
    tile = widest(512, unit_width)
    blocks = len(plan)
    stages = [mp_bits if block % 2 == 0 else mp_bits[::-1] for block in range(blocks)]
    keeps, sends, arrivals = [], [], [[] for _ in plan]

    def begin(block, after):
        first, width = plan[block]
        order = sorted(range(mp), key=lambda g: place(g, stages[block]))
        keep, send = vocab_matmul(all_rows, vocab_weight, first, width, order, tile, after)
        keeps.append(keep)
        sends.append(send)
        arrivals[block].append(swap(send, "mp", lambda i: i ^ stages[block][0]))

    def go_on(block, after):
        keep = keeps[block]
        for bit in stages[block][1:]:
            while len(arrivals[block]) > 1:
                rest = arrivals[block].pop(0)
                keep = add_kept(keep, rest, tile)
            send = fold(keep, arrivals[block][-1], tile, after)
            arrivals[block].append(swap(send, "mp", lambda i: i ^ bit))
        keeps[block] = keep
        return send

    begin(0, [])
    begin(1, [sends[0]])
    begin(2, [sends[1]])
    last = go_on(0, [sends[2]])
    begin(3, [last])
    last = go_on(1, [sends[3]])
    begin(4, [last])
    lasts = [go_on(block, [sends[4]]) for block in (2, 3, 4)]
    joined = None
    for group in (range(0, 3), range(3, 5)):
        joined = finish(
            wanted,
            [(keeps[block], arrivals[block]) for block in group],
            tile,
            choices,
            plan[group[0]][0],
            vocab_width,
            joined,
            lasts[2:] if joined is None else [],
        )
    logits, stats = joined

    for bit in bits_of(batch):
        came = swap(stats, "batch", lambda i: i ^ bit)
        low = (1 - (b & bit) // bit).astype(jnp.int32).reshape(1)
        if 2 * bit < batch:
            stats = merge(low, stats, came)
    log_probs, path_scores = tail(
        low, stats, came, tree_paths.T, logits, out_rows, rows, choices
    )
    return (log_probs, path_scores)


def solution(mesh):
    return jax.shard_map(
        shards,
        mesh=mesh,
        in_specs=(
            P("batch", None, "mp"),
            P("batch"),
            P(),
            P(None, "batch", "mp"),
            P(None, "mp"),
            P("mp", "batch"),
            P("mp", None, None),
            P(),
        ),
        out_specs=(P("mp", None, "batch"), P("mp", None)),
        check_vma=False,
    )
```

```python
import functools

import jax
import jax.numpy as jnp
from jax import lax
from jax.experimental import pallas as pl
from jax.experimental.pallas import tpu as pltpu
from jax.sharding import PartitionSpec as P

EPSILON = 1e-05
MIB = 1024 * 1024
LANES = 128
CODE_BITS = 14
VMEM_LIMIT = 4 * MIB
HEAD_LIMIT = 24 * MIB
VOCAB_LIMIT = 24 * MIB


def together(*arrays):
    return lax.optimization_barrier(arrays)


def bits_of(count):
    return [1 << i for i in range(count.bit_length() - 1)]


def swap(array, axis, partner):
    return lax.ppermute(array, axis, [(i, partner(i)) for i in range(lax.axis_size(axis))])


def place(index, stages):
    spot = 0
    for bit in stages:
        spot = 2 * spot + (index & bit) // bit
    return spot


def unplace(spot, stages):
    index = 0
    for step, bit in enumerate(stages[::-1]):
        index = index + ((spot >> step) & 1) * bit
    return index


def widest(limit, size):
    tile = min(limit, size)
    while size % tile:
        tile //= 2
    return tile


VMEM = pl.BlockSpec(memory_space=pltpu.VMEM)
ANY = pl.BlockSpec(memory_space=pl.ANY)
WAYS = 4


def copy_groups(source, targets, sems, firsts):
    groups = []
    for index, target in enumerate(targets):
        depth, width = target.shape
        share, tile = depth // WAYS, widest(512, width)
        for step in range(width // tile):
            groups.append(
                [
                    pltpu.make_async_copy(
                        source.at[pl.ds(way * share, share), pl.ds(firsts[index] + step * tile, tile)],
                        target.at[pl.ds(way * share, share), pl.ds(step * tile, tile)],
                        sems.at[index, step, way],
                    )
                    for way in range(WAYS)
                ]
            )
    return groups


def group_sems(count, width):
    return pltpu.SemaphoreType.DMA((max(1, count), width // widest(512, width), WAYS))


def stream(source, held, sems, first, tile):
    depth, width = held.shape
    share = depth // WAYS

    def copies(n):
        at = n * tile if isinstance(n, int) else pl.multiple_of(n * tile, tile)
        return [
            pltpu.make_async_copy(
                source.at[pl.ds(way * share, share), pl.ds(first + at, tile)],
                held.at[pl.ds(way * share, share), pl.ds(at, tile)],
                sems.at[n, way],
            )
            for way in range(WAYS)
        ]

    def begin(n, carry):
        for copy in copies(n):
            copy.start()
        return carry

    lax.fori_loop(0, width // tile, begin, 0)

    def wait(n):
        for copy in copies(n):
            copy.wait()

    return wait


def start_group(group):
    for copy in group:
        copy.start()


def wait_groups(groups):
    for group in groups:
        for copy in group:
            copy.wait()


def fetch_body(info, weight, *refs, firsts):
    targets, sems = refs[-1 - len(firsts) : -1], refs[-1]
    source = weight.at[info[0]] if len(weight.shape) == 3 else weight
    groups = copy_groups(source, targets, sems, firsts)
    for group in groups:
        start_group(group)
    wait_groups(groups)


def fetch(info, weight, firsts, width, after, limit=VMEM_LIMIT):
    depth = weight.shape[-2]
    return pl.pallas_call(
        functools.partial(fetch_body, firsts=firsts),
        in_specs=[pl.BlockSpec(memory_space=pltpu.SMEM), ANY] + [ANY] * len(after),
        out_specs=[VMEM] * len(firsts),
        out_shape=[jax.ShapeDtypeStruct((depth, width), weight.dtype)] * len(firsts),
        scratch_shapes=[group_sems(len(firsts), width)],
        compiler_params=pltpu.CompilerParams(vmem_limit_bytes=limit),
        cost_estimate=pl.CostEstimate(
            flops=700 * depth * width * len(firsts), bytes_accessed=0, transcendentals=0
        ),
    )(info, weight, *after)


def head_body(info, came, *refs, height, tile, streams):
    if streams:
        source, out, rows, held, sems = refs
        wait = stream(source.at[info[0]], held, sems, 0, tile)
        weights = [held]
    else:
        weights, (out, rows) = refs[:-2], refs[-2:]
    for unit in range(came.shape[0] // height):
        start = pl.multiple_of(info[1 + unit] * height, height)
        rows[pl.ds(start, height), :] = came[unit * height : (unit + 1) * height, :]
    first = 0
    for weight in weights:
        width = weight.shape[1]

        def step(n, carry, weight=weight, first=first):
            at = pl.multiple_of(n * tile, tile)
            if streams:
                wait(n)
            total = jnp.dot(
                rows[...], weight[:, pl.ds(at, tile)], preferred_element_type=jnp.float32
            )
            out[:, pl.ds(pl.multiple_of(first + at, tile), tile)] = total.astype(out.dtype)
            return carry

        lax.fori_loop(0, width // tile, step, 0)
        first += width


def head_matmul(info, came, weights, height, out_type):
    count, depth = came.shape
    streams = not isinstance(weights, list)
    if streams:
        width = weights.shape[2]
        weights, weight_spec = [weights], ANY
    else:
        width = sum(weight.shape[1] for weight in weights)
        weight_spec = VMEM
    tile = widest(512, width // 4)
    scratch = [pltpu.VMEM((count, depth), jnp.bfloat16)]
    if streams:
        scratch.append(pltpu.VMEM((depth, width), jnp.bfloat16))
        scratch.append(pltpu.SemaphoreType.DMA((width // tile, WAYS)))
    return pl.pallas_call(
        functools.partial(head_body, height=height, tile=tile, streams=streams),
        in_specs=[pl.BlockSpec(memory_space=pltpu.SMEM), VMEM] + [weight_spec] * len(weights),
        out_specs=VMEM,
        out_shape=jax.ShapeDtypeStruct((count, width), out_type),
        scratch_shapes=scratch,
        compiler_params=pltpu.CompilerParams(
            vmem_limit_bytes=HEAD_LIMIT if streams else VMEM_LIMIT
        ),
        cost_estimate=pl.CostEstimate(
            flops=2 * count * depth * width, bytes_accessed=2 * depth * width, transcendentals=0
        ),
    )(info, came, *weights)


def encode(value):
    top = jnp.max(jnp.abs(value), axis=1, keepdims=True)
    power = jnp.floor(jnp.log2(jnp.maximum(top, 1e-30))) + 1.0
    code = jnp.floor(value * jnp.exp2(CODE_BITS - power) + 0.5)
    return code.astype(jnp.int32).astype(jnp.int16), power


def decode(code, power):
    return code.astype(jnp.int32).astype(jnp.float32) * jnp.exp2(power - CODE_BITS)


def marks_of(powers, height):
    lane = lax.broadcasted_iota(jnp.int32, (height, LANES), 1)
    marks = jnp.zeros((height, LANES), jnp.float32)
    for index, power in enumerate(powers):
        marks = jnp.where(lane == index, power, marks)
    return marks.astype(jnp.int32).astype(jnp.int16)


def gather_body(spots, *refs, height, halves):
    parts, rows = refs[:-1], refs[-1]
    share = rows.shape[1] // halves
    unit = 0
    for part in parts:
        for block in range(part.shape[0] // height):
            for half in range(halves):
                start = pl.multiple_of(spots[unit] * height, height)
                columns = slice(half * share, (half + 1) * share)
                rows[pl.ds(start, height), columns] = part[
                    block * height : (block + 1) * height, columns
                ]
                unit += 1


def gather_rows(spots, parts, height, halves):
    count = sum(p.shape[0] for p in parts)
    return pl.pallas_call(
        functools.partial(gather_body, height=height, halves=halves),
        in_specs=[pl.BlockSpec(memory_space=pltpu.SMEM)] + [VMEM] * len(parts),
        out_specs=VMEM,
        out_shape=jax.ShapeDtypeStruct((count, parts[0].shape[1]), parts[0].dtype),
        compiler_params=pltpu.CompilerParams(vmem_limit_bytes=VMEM_LIMIT),
    )(spots, *parts)


def vocab_body(rows, source, *refs, order, tile, first, waits):
    keep, send, held, powers, sems = refs[waits:]
    wait = stream(source, held, sems, first, tile)
    height = rows.shape[0] // len(order)
    half = len(order) // 2
    width = held.shape[1]
    lane = lax.broadcasted_iota(jnp.int32, powers.shape, 1)
    powers[...] = jnp.zeros_like(powers)

    def step(n, carry):
        at = pl.ds(pl.multiple_of(n * tile, tile), tile)
        wait(n)
        total = jnp.dot(rows[...], held[:, at], preferred_element_type=jnp.float32)
        sorted_rows = [total[g * height : (g + 1) * height] for g in order]
        for spot, value in enumerate(sorted_rows[:half]):
            keep[spot * height : (spot + 1) * height, at] = value
        code, power = encode(jnp.concatenate(sorted_rows[half:], axis=0))
        send[:, at] = code
        powers[...] = jnp.where(lane == n, power, powers[...])
        return carry

    lax.fori_loop(0, width // tile, step, 0)
    send[:, width:] = powers[...].astype(jnp.int32).astype(jnp.int16)


def vocab_matmul(rows, vocab_weight, first, width, order, tile, after):
    depth = vocab_weight.shape[0]
    count = rows.shape[0]
    half = count // 2
    return pl.pallas_call(
        functools.partial(vocab_body, order=order, tile=tile, first=first, waits=len(after)),
        in_specs=[VMEM] + [ANY] * (1 + len(after)),
        out_specs=[VMEM] * 2,
        out_shape=[
            jax.ShapeDtypeStruct((half, width), jnp.float32),
            jax.ShapeDtypeStruct((half, width + LANES), jnp.int16),
        ],
        scratch_shapes=[
            pltpu.VMEM((depth, width), jnp.bfloat16),
            pltpu.VMEM((half, LANES), jnp.float32),
            pltpu.SemaphoreType.DMA((width // tile, WAYS)),
        ],
        compiler_params=pltpu.CompilerParams(vmem_limit_bytes=VOCAB_LIMIT),
        cost_estimate=pl.CostEstimate(
            flops=2 * count * depth * width, bytes_accessed=2 * depth * width, transcendentals=0
        ),
    )(rows, vocab_weight, *after)


def fold_body(keep, came, *refs, tile):
    send = refs[-1]
    half = send.shape[0]
    width = keep.shape[1]
    for row in range(half, 2 * half, 16):
        here, there = slice(row, row + 16), slice(row - half, row - half + 16)
        marks = came[here, width:].astype(jnp.int32).astype(jnp.float32)
        powers = []
        for step in range(width // tile):
            block = slice(step * tile, (step + 1) * tile)
            value = keep[here, block] + decode(came[here, block], marks[:, step : step + 1])
            code, power = encode(value)
            send[there, block] = code
            powers.append(power)
        send[there, width:] = marks_of(powers, 16)


def fold(keep, came, tile, after):
    rows, width = keep.shape
    return pl.pallas_call(
        functools.partial(fold_body, tile=tile),
        in_specs=[VMEM] * 2 + [ANY] * len(after),
        out_specs=VMEM,
        out_shape=jax.ShapeDtypeStruct((rows // 2, width + LANES), jnp.int16),
        compiler_params=pltpu.CompilerParams(vmem_limit_bytes=VMEM_LIMIT),
    )(keep, came, *after)


def add_body(keep, came, out, *, tile):
    half, width = out.shape
    for row in range(0, half, 16):
        here = slice(row, row + 16)
        marks = came[here, width:].astype(jnp.int32).astype(jnp.float32)
        for step in range(width // tile):
            block = slice(step * tile, (step + 1) * tile)
            out[here, block] = keep[here, block] + decode(came[here, block], marks[:, step : step + 1])


def add_kept(keep, came, tile):
    rows, width = keep.shape
    return pl.pallas_call(
        functools.partial(add_body, tile=tile),
        in_specs=[VMEM] * 2,
        out_specs=VMEM,
        out_shape=jax.ShapeDtypeStruct((rows // 2, width), jnp.float32),
        compiler_params=pltpu.CompilerParams(vmem_limit_bytes=VMEM_LIMIT),
    )(keep, came)


def merge_rows(one, two):
    peak = jnp.maximum(one[:, :1], two[:, :1])
    lane = lax.broadcasted_iota(jnp.int32, one.shape, 1)
    factor_one = jnp.where(lane == 1, jnp.exp(one[:, :1] - peak), 1.0)
    factor_two = jnp.where(lane == 1, jnp.exp(two[:, :1] - peak), 1.0)
    return jnp.where(lane == 0, peak, one * factor_one + two * factor_two)


def finish_body(wanted, *refs, tile, choices, first, counts, earlier):
    blocks = []
    for count in counts:
        blocks.append((refs[0], refs[1 : 1 + count]))
        refs = refs[1 + count :]
    before = refs[0] if earlier else None
    total_logits, stats, logits, sems = refs[-4:]
    rows, width = logits.shape
    height = 16
    lane = lax.broadcasted_iota(jnp.int32, (height, LANES), 1)
    copies = []
    for index, row in enumerate(range(0, rows, height)):
        here = slice(row, row + height)
        ids = wanted[here, :] - first
        columns = [jnp.broadcast_to(ids[:, k : k + 1], (height, LANES)) for k in range(choices)]
        peak = None
        picks = [None] * choices
        start = 0
        for keep, arrivals in blocks:
            wide = keep.shape[1]
            marks = [came[here, wide:].astype(jnp.int32).astype(jnp.float32) for came in arrivals]
            for step in range(wide // tile):
                block = slice(step * tile, (step + 1) * tile)
                value = keep[here, block]
                for came, mark in zip(arrivals, marks):
                    value = value + decode(came[here, block], mark[:, step : step + 1])
                logits[here, start : start + tile] = value
                for part in range(tile // LANES):
                    piece = value[:, part * LANES : (part + 1) * LANES]
                    at = lane + (start + part * LANES)
                    peak = piece if peak is None else jnp.maximum(peak, piece)
                    for k in range(choices):
                        term = jnp.where(at == columns[k], piece, 0.0)
                        picks[k] = term if picks[k] is None else picks[k] + term
                start += tile
        copies.append(
            pltpu.make_async_copy(
                logits.at[pl.ds(row, height), :],
                total_logits.at[pl.ds(row, height), pl.ds(first, width)],
                sems.at[index],
            )
        )
        copies[-1].start()
        peak = jnp.max(peak, axis=1, keepdims=True)
        total = None
        for part in range(width // LANES):
            term = jnp.exp(logits[here, part * LANES : (part + 1) * LANES] - peak)
            total = term if total is None else total + term
        out = jnp.where(lane == 0, peak, jnp.zeros((height, LANES), jnp.float32))
        for k, item in enumerate([total] + picks):
            out = jnp.where(lane == k + 1, jnp.sum(item, axis=1, keepdims=True), out)
        stats[here, :] = out if before is None else merge_rows(before[here, :], out)
    for copy in copies:
        copy.wait()


def finish(wanted, blocks, tile, choices, first, vocab_width, earlier, after):
    rows = wanted.shape[0]
    width = sum(keep.shape[1] for keep, _ in blocks)
    operands = [wanted]
    for keep, arrivals in blocks:
        operands += [keep, *arrivals]
    operands += [earlier[1]] if earlier else []
    buffer = [earlier[0]] if earlier else []
    return pl.pallas_call(
        functools.partial(
            finish_body,
            tile=tile,
            choices=choices,
            first=first,
            counts=[len(arrivals) for _, arrivals in blocks],
            earlier=bool(earlier),
        ),
        in_specs=[VMEM] * len(operands) + [ANY] * len(buffer + after),
        out_specs=[ANY, VMEM],
        out_shape=[
            jax.ShapeDtypeStruct((rows, vocab_width), jnp.float32),
            jax.ShapeDtypeStruct((rows, LANES), jnp.float32),
        ],
        scratch_shapes=[
            pltpu.VMEM((rows, width), jnp.float32),
            pltpu.SemaphoreType.DMA((rows // 16,)),
        ],
        input_output_aliases={len(operands): 0} if earlier else {},
        compiler_params=pltpu.CompilerParams(vmem_limit_bytes=VOCAB_LIMIT),
    )(*operands, *buffer, *after)


def merge_body(low, own, came, out):
    first = jnp.where(low[0] == 1, own[...], came[...])
    second = jnp.where(low[0] == 1, came[...], own[...])
    out[...] = merge_rows(first, second)


def merge(low, own, came):
    return pl.pallas_call(
        merge_body,
        in_specs=[pl.BlockSpec(memory_space=pltpu.SMEM), VMEM, VMEM],
        out_specs=VMEM,
        out_shape=jax.ShapeDtypeStruct(own.shape, own.dtype),
        compiler_params=pltpu.CompilerParams(vmem_limit_bytes=VMEM_LIMIT),
    )(low, own, came)


def tail_body(low, own, came, tree, logits, log_probs, scores, stats, *, heads, height, choices):
    merge_body(low, own, came, stats)
    blocks = log_probs.shape[0] // height
    paths = scores.shape[1]
    width = logits.shape[1]
    tile = widest(1024, width)
    for block in range(blocks):
        there = slice(block * height, (block + 1) * height)
        score = jnp.zeros((height, paths), jnp.float32)
        for head in range(heads):
            row = (block * heads + head) * height
            here = slice(row, row + height)
            normalizer = stats[here, 0:1] + jnp.log(stats[here, 1:2])
            for at in range(0, width, tile):
                log_probs[there, head, at : at + tile] = logits[here, at : at + tile] - normalizer
            found = jnp.zeros((height, paths), jnp.float32)
            for k in range(choices):
                picked = stats[here, 2 + k : 3 + k] - normalizer
                found = jnp.where(tree[head : head + 1, :] == k, picked, found)
            score = score + found
        scores[there, :] = score


def tail(low, own, came, tree, logits, out_rows, height, choices):
    heads, paths = tree.shape
    return pl.pallas_call(
        functools.partial(tail_body, heads=heads, height=height, choices=choices),
        in_specs=[pl.BlockSpec(memory_space=pltpu.SMEM)] + [VMEM] * 4,
        out_specs=[VMEM] * 2,
        out_shape=[
            jax.ShapeDtypeStruct((out_rows, heads, logits.shape[1]), jnp.float32),
            jax.ShapeDtypeStruct((out_rows, paths), jnp.float32),
        ],
        scratch_shapes=[pltpu.VMEM(own.shape, own.dtype)],
        compiler_params=pltpu.CompilerParams(vmem_limit_bytes=VMEM_LIMIT),
    )(low, own, came, tree, logits)


def shards(
    hidden_states, accepted, norm_gain, head_weight, head_bias, vocab_weight, cand_ids, tree_paths
):
    batch, mp = lax.axis_size("batch"), lax.axis_size("mp")
    b, m = lax.axis_index("batch"), lax.axis_index("mp")
    rows, positions, feat = hidden_states.shape
    heads, inner, _ = head_weight.shape
    vocab_width = vocab_weight.shape[1]
    out_rows, _, choices = cand_ids.shape
    pieces = feat // inner
    ratio = out_rows // rows
    mp_bits = bits_of(mp)
    pair, core = b // 2, b % 2
    pair_bits = bits_of(batch // 2)

    taken = lax.broadcasted_iota(jnp.int32, (rows, positions, 1), 1) == (accepted - 1)[:, None, None]
    chosen = jnp.sum(jnp.where(taken, hidden_states, 0).astype(jnp.float32), axis=1)
    chosen = chosen.astype(jnp.bfloat16)
    other = swap(chosen, "batch", lambda i: i ^ 1)
    chosen = jnp.concatenate(
        [jnp.where(core == 0, chosen, other), jnp.where(core == 0, other, chosen)], axis=0
    ).astype(jnp.float32)
    gain = lax.dynamic_slice_in_dim(norm_gain, m * feat, feat, 0)

    if pieces == 2:
        sent = lax.dynamic_slice_in_dim(chosen, core * inner, inner, 1)
        sent_gain = lax.dynamic_slice_in_dim(gain, core * inner, inner, 0)
    else:
        sent = lax.dynamic_slice_in_dim(chosen, core * rows, rows, 0)
        sent_gain = gain
    sent = (sent * sent_gain).astype(jnp.bfloat16)
    perm = []
    for i in range(batch):
        for j in range(mp):
            perm.append((i * mp + j, (j * pieces + i % pieces) * mp + ((i // pieces) ^ j)))
    head_first = (1 - core).astype(jnp.int32).reshape(1)
    part = feat // 2
    head_first = (1 - core).astype(jnp.int32).reshape(1)
    part = feat // 4
    firsts = [part * i for i in range(4)]
    weights_first = fetch(head_first, head_weight, firsts, part, [sent], HEAD_LIMIT)
    block = lax.ppermute(sent, ("batch", "mp"), perm)
    block, *weights_first = together(block, *weights_first)
    for bit in mp_bits:
        block = jnp.concatenate([block, swap(block, "mp", lambda i: i ^ bit)], axis=0)

    square_sum = jnp.sum(chosen * chosen, axis=1, keepdims=True)
    for bit in mp_bits:
        square_sum = square_sum + swap(square_sum, "mp", lambda i: i ^ bit)
    row_scale = lax.rsqrt(square_sum / (mp * feat) + EPSILON)
    own_normed = (chosen * row_scale * gain).astype(jnp.bfloat16).astype(jnp.float32)

    spots = []
    for unit in range(batch):
        source = (m ^ (unit // pieces) ^ (b // pieces)) * pieces + unit % pieces
        spots.append(((source // 2) ^ pair) * 2 + source % 2)
    info = jnp.stack([core] + spots).astype(jnp.int32)
    send = head_matmul(info, block, weights_first, rows, jnp.bfloat16)
    came = swap(send, "batch", lambda i: i ^ 1)
    keep = head_matmul(info, block, head_weight, rows, jnp.float32)
    units = batch // 2
    share = feat // 2
    tall = 2 * rows
    orders = (pair_bits, pair_bits[::-1])
    total = keep + came.astype(jnp.float32)
    halves = [
        {u: total[u * tall : (u + 1) * tall, h * share : (h + 1) * share] for u in range(units)}
        for h in range(2)
    ]
    for step in range(len(pair_bits)):
        arrived = []
        for half, order in zip(halves, orders):
            leave = [u for u in half if u & order[step]]
            outbound = jnp.concatenate([half[u] for u in leave], axis=0).astype(jnp.bfloat16)
            arrived.append(swap(outbound, "batch", lambda i: i ^ (2 * order[step])))
        for h, order in enumerate(orders):
            stay = [u for u in halves[h] if not u & order[step]]
            halves[h] = {
                u: halves[h][u] + arrived[h][i * tall : (i + 1) * tall].astype(jnp.float32)
                for i, u in enumerate(stay)
            }
    bias = lax.dynamic_slice_in_dim(head_bias, core, 1, 0)
    before = jnp.concatenate([half[0] for half in halves], axis=1) * row_scale + bias
    residual = (own_normed + jax.nn.silu(before)).astype(jnp.bfloat16)
    filled = [residual[:, :share], residual[:, share:]]
    held = [[0], [0]]
    parts, others = [], []
    block = residual
    for step in reversed(range(len(pair_bits))):
        arrived = [
            swap(filled[h], "batch", lambda i: i ^ (2 * orders[h][step])) for h in range(2)
        ]
        for h in range(2):
            held[h] = held[h] + [u ^ orders[h][step] for u in held[h]]
        came = jnp.concatenate(arrived, axis=1)
        if step == 0:
            parts.append(block)
            others.append(swap(block, "batch", lambda i: i ^ 1))
            block = came
        else:
            block = jnp.concatenate([block, came], axis=0)
            filled = [block[:, :share], block[:, share:]]
    parts.append(block)
    others.append(swap(block, "batch", lambda i: i ^ 1))

    table = []
    for whose in (core, 1 - core):
        for unit in range(batch):
            for h in range(2):
                source = (pair ^ held[h][unit // 2]) * 2 + unit % 2
                table.append((((source // ratio) ^ m) * ratio + source % ratio) * heads + whose)
    all_rows = gather_rows(jnp.stack(table).astype(jnp.int32), parts + others, rows, 2)
    wanted = (cand_ids - b * vocab_width).reshape(ratio, rows, heads, choices)
    wanted = wanted.transpose(0, 2, 1, 3).reshape(out_rows * heads, choices)
    wanted = jnp.pad(wanted, ((0, 0), (0, LANES - choices)), constant_values=-1)

    unit_width = vocab_width // 8
    plan = [(0, 2), (2, 2), (4, 2), (6, 1), (7, 1)]
    plan = [(first * unit_width, count * unit_width) for first, count in plan]
    tile = widest(512, unit_width)
    blocks = len(plan)
    stages = [mp_bits if block % 2 == 0 else mp_bits[::-1] for block in range(blocks)]
    keeps, sends, arrivals = [], [], [[] for _ in plan]

    def begin(block, after):
        first, width = plan[block]
        order = sorted(range(mp), key=lambda g: place(g, stages[block]))
        keep, send = vocab_matmul(all_rows, vocab_weight, first, width, order, tile, after)
        keeps.append(keep)
        sends.append(send)
        arrivals[block].append(swap(send, "mp", lambda i: i ^ stages[block][0]))

    def go_on(block, after):
        keep = keeps[block]
        for bit in stages[block][1:]:
            while len(arrivals[block]) > 1:
                rest = arrivals[block].pop(0)
                keep = add_kept(keep, rest, tile)
            send = fold(keep, arrivals[block][-1], tile, after)
            arrivals[block].append(swap(send, "mp", lambda i: i ^ bit))
        keeps[block] = keep
        return send

    def finish_blocks(group, earlier, after):
        return finish(
            wanted,
            [(keeps[block], arrivals[block]) for block in group],
            tile,
            choices,
            plan[group[0]][0],
            vocab_width,
            earlier,
            after,
        )

    begin(0, [])
    begin(1, [sends[0]])
    begin(2, [sends[1]])
    last = go_on(0, [sends[2]])
    begin(3, [last])
    last = go_on(1, [sends[3]])
    begin(4, [last, arrivals[0][-1], arrivals[2][0], arrivals[3][0]])
    last = go_on(2, [sends[4]])
    last = go_on(3, [last])
    joined = finish_blocks((0, 1), None, [last])
    go_on(4, [joined[1]])
    joined = finish_blocks((2, 3, 4), joined, [])
    logits, stats = joined

    for bit in bits_of(batch):
        came = swap(stats, "batch", lambda i: i ^ bit)
        low = (1 - (b & bit) // bit).astype(jnp.int32).reshape(1)
        if 2 * bit < batch:
            stats = merge(low, stats, came)
    log_probs, path_scores = tail(
        low, stats, came, tree_paths.T, logits, out_rows, rows, choices
    )
    return (log_probs, path_scores)


def solution(mesh):
    return jax.shard_map(
        shards,
        mesh=mesh,
        in_specs=(
            P("batch", None, "mp"),
            P("batch"),
            P(),
            P(None, "batch", "mp"),
            P(None, "mp"),
            P("mp", "batch"),
            P("mp", None, None),
            P(),
        ),
        out_specs=(P("mp", None, "batch"), P("mp", None)),
        check_vma=False,
    )
```

```python
import functools

import jax
import jax.numpy as jnp
from jax import lax
from jax.experimental import pallas as pl
from jax.experimental.pallas import tpu as pltpu
from jax.sharding import PartitionSpec as P

EPSILON = 1e-05
MIB = 1024 * 1024
LANES = 128
CODE_BITS = 14
VMEM_LIMIT = 4 * MIB
VOCAB_LIMIT = 24 * MIB
FINISH_LIMIT = 10 * MIB


def bits_of(count):
    return [1 << i for i in range(count.bit_length() - 1)]


def swap(array, axis, partner):
    return lax.ppermute(array, axis, [(i, partner(i)) for i in range(lax.axis_size(axis))])


def place(index, stages):
    spot = 0
    for bit in stages:
        spot = 2 * spot + (index & bit) // bit
    return spot


def unplace(spot, stages):
    index = 0
    for step, bit in enumerate(stages[::-1]):
        index = index + ((spot >> step) & 1) * bit
    return index


def widest(limit, size):
    tile = min(limit, size)
    while size % tile:
        tile //= 2
    return tile


VMEM = pl.BlockSpec(memory_space=pltpu.VMEM)
ANY = pl.BlockSpec(memory_space=pl.ANY)
WAYS = 4
UNIT_COST = pl.CostEstimate(flops=1, bytes_accessed=1, transcendentals=0)


def stream(source, held, sems, first, tile):
    depth, width = held.shape
    share = depth // WAYS

    def copies(n):
        at = n * tile if isinstance(n, int) else pl.multiple_of(n * tile, tile)
        return [
            pltpu.make_async_copy(
                source.at[pl.ds(way * share, share), pl.ds(first + at, tile)],
                held.at[pl.ds(way * share, share), pl.ds(at, tile)],
                sems.at[n, way],
            )
            for way in range(WAYS)
        ]

    def begin(n, carry):
        for copy in copies(n):
            copy.start()
        return carry

    lax.fori_loop(0, width // tile, begin, 0)

    def wait(n):
        for copy in copies(n):
            copy.wait()

    return wait


def head_body(info, came, source, out, rows, held, sems, *, height, tile):
    wait = stream(source.at[info[0]], held, sems, 0, tile)
    for unit in range(came.shape[0] // height):
        start = pl.multiple_of(info[1 + unit] * height, height)
        rows[pl.ds(start, height), :] = came[unit * height : (unit + 1) * height, :]

    def step(n, carry):
        at = pl.ds(pl.multiple_of(n * tile, tile), tile)
        wait(n)
        total = jnp.dot(rows[...], held[:, at], preferred_element_type=jnp.float32)
        out[:, at] = total.astype(out.dtype)
        return carry

    lax.fori_loop(0, held.shape[1] // tile, step, 0)


def head_matmul(info, came, head_weight, height, out_type):
    count, depth = came.shape
    width = head_weight.shape[2]
    tile = widest(512, width // 2)
    return pl.pallas_call(
        functools.partial(head_body, height=height, tile=tile),
        in_specs=[pl.BlockSpec(memory_space=pltpu.SMEM), VMEM, ANY],
        out_specs=VMEM,
        out_shape=jax.ShapeDtypeStruct((count, width), out_type),
        scratch_shapes=[
            pltpu.VMEM((count, depth), jnp.bfloat16),
            pltpu.VMEM((depth, width), jnp.bfloat16),
            pltpu.SemaphoreType.DMA((width // tile, WAYS)),
        ],
        cost_estimate=UNIT_COST,
        compiler_params=pltpu.CompilerParams(vmem_limit_bytes=VOCAB_LIMIT),
    )(info, came, head_weight)


def encode(value):
    top = jnp.max(jnp.abs(value), axis=1, keepdims=True)
    power = jnp.floor(jnp.log2(jnp.maximum(top, 1e-30))) + 1.0
    code = jnp.floor(value * jnp.exp2(CODE_BITS - power) + 0.5)
    return code.astype(jnp.int32).astype(jnp.int16), power


def decode(code, power):
    return code.astype(jnp.int32).astype(jnp.float32) * jnp.exp2(power - CODE_BITS)


def marks_of(powers, height):
    lane = lax.broadcasted_iota(jnp.int32, (height, LANES), 1)
    marks = jnp.zeros((height, LANES), jnp.float32)
    for index, power in enumerate(powers):
        marks = jnp.where(lane == index, power, marks)
    return marks.astype(jnp.int32).astype(jnp.int16)


def gather_body(spots, *refs, height, halves):
    parts, rows = refs[:-1], refs[-1]
    share = rows.shape[1] // halves
    unit = 0
    for part in parts:
        for block in range(part.shape[0] // height):
            for half in range(halves):
                start = pl.multiple_of(spots[unit] * height, height)
                columns = slice(half * share, (half + 1) * share)
                rows[pl.ds(start, height), columns] = part[
                    block * height : (block + 1) * height, columns
                ]
                unit += 1


def gather_rows(spots, parts, height, halves):
    count = sum(p.shape[0] for p in parts)
    return pl.pallas_call(
        functools.partial(gather_body, height=height, halves=halves),
        in_specs=[pl.BlockSpec(memory_space=pltpu.SMEM)] + [VMEM] * len(parts),
        out_specs=VMEM,
        out_shape=jax.ShapeDtypeStruct((count, parts[0].shape[1]), parts[0].dtype),
        cost_estimate=UNIT_COST,
        compiler_params=pltpu.CompilerParams(vmem_limit_bytes=VMEM_LIMIT),
    )(spots, *parts)


def vocab_body(rows, source, *refs, order, tile, first, waits):
    keep, send, held, powers, sems = refs[waits:]
    wait = stream(source, held, sems, first, tile)
    height = rows.shape[0] // len(order)
    half = len(order) // 2
    width = held.shape[1]
    lane = lax.broadcasted_iota(jnp.int32, powers.shape, 1)
    powers[...] = jnp.zeros_like(powers)

    def step(n, carry):
        at = pl.ds(pl.multiple_of(n * tile, tile), tile)
        wait(n)
        total = jnp.dot(rows[...], held[:, at], preferred_element_type=jnp.float32)
        sorted_rows = [total[g * height : (g + 1) * height] for g in order]
        for spot, value in enumerate(sorted_rows[:half]):
            keep[spot * height : (spot + 1) * height, at] = value
        code, power = encode(jnp.concatenate(sorted_rows[half:], axis=0))
        send[:, at] = code
        powers[...] = jnp.where(lane == n, power, powers[...])
        return carry

    lax.fori_loop(0, width // tile, step, 0)
    send[:, width:] = powers[...].astype(jnp.int32).astype(jnp.int16)


def vocab_matmul(rows, vocab_weight, first, width, order, tile, after):
    depth = vocab_weight.shape[0]
    count = rows.shape[0]
    half = count // 2
    return pl.pallas_call(
        functools.partial(vocab_body, order=order, tile=tile, first=first, waits=len(after)),
        in_specs=[VMEM] + [ANY] * (1 + len(after)),
        out_specs=[VMEM] * 2,
        out_shape=[
            jax.ShapeDtypeStruct((half, width), jnp.float32),
            jax.ShapeDtypeStruct((half, width + LANES), jnp.int16),
        ],
        scratch_shapes=[
            pltpu.VMEM((depth, width), jnp.bfloat16),
            pltpu.VMEM((half, LANES), jnp.float32),
            pltpu.SemaphoreType.DMA((width // tile, WAYS)),
        ],
        compiler_params=pltpu.CompilerParams(vmem_limit_bytes=VOCAB_LIMIT),
        cost_estimate=UNIT_COST,
    )(rows, vocab_weight, *after)


def fold_body(keep, came, *refs, tile):
    send = refs[-1]
    half = send.shape[0]
    width = keep.shape[1]
    for row in range(half, 2 * half, 16):
        here, there = slice(row, row + 16), slice(row - half, row - half + 16)
        marks = came[here, width:].astype(jnp.int32).astype(jnp.float32)
        powers = []
        for step in range(width // tile):
            block = slice(step * tile, (step + 1) * tile)
            value = keep[here, block] + decode(came[here, block], marks[:, step : step + 1])
            code, power = encode(value)
            send[there, block] = code
            powers.append(power)
        send[there, width:] = marks_of(powers, 16)


def fold(keep, came, tile, after):
    rows, width = keep.shape
    return pl.pallas_call(
        functools.partial(fold_body, tile=tile),
        in_specs=[VMEM] * 2 + [ANY] * len(after),
        out_specs=VMEM,
        out_shape=jax.ShapeDtypeStruct((rows // 2, width + LANES), jnp.int16),
        cost_estimate=UNIT_COST,
        compiler_params=pltpu.CompilerParams(vmem_limit_bytes=VMEM_LIMIT),
    )(keep, came, *after)


def add_body(keep, came, out, *, tile):
    half, width = out.shape
    for row in range(0, half, 16):
        here = slice(row, row + 16)
        marks = came[here, width:].astype(jnp.int32).astype(jnp.float32)
        for step in range(width // tile):
            block = slice(step * tile, (step + 1) * tile)
            out[here, block] = keep[here, block] + decode(came[here, block], marks[:, step : step + 1])


def add_kept(keep, came, tile):
    rows, width = keep.shape
    return pl.pallas_call(
        functools.partial(add_body, tile=tile),
        in_specs=[VMEM] * 2,
        out_specs=VMEM,
        out_shape=jax.ShapeDtypeStruct((rows // 2, width), jnp.float32),
        cost_estimate=UNIT_COST,
        compiler_params=pltpu.CompilerParams(vmem_limit_bytes=VMEM_LIMIT),
    )(keep, came)


def merge_rows(one, two):
    peak = jnp.maximum(one[:, :1], two[:, :1])
    lane = lax.broadcasted_iota(jnp.int32, one.shape, 1)
    factor_one = jnp.where(lane == 1, jnp.exp(one[:, :1] - peak), 1.0)
    factor_two = jnp.where(lane == 1, jnp.exp(two[:, :1] - peak), 1.0)
    return jnp.where(lane == 0, peak, one * factor_one + two * factor_two)


def finish_body(wanted, *refs, tile, choices, first, counts, earlier):
    blocks = []
    for count in counts:
        blocks.append((refs[0], refs[1 : 1 + count]))
        refs = refs[1 + count :]
    before = refs[0] if earlier else None
    total_logits, stats, logits, sems = refs[-4:]
    rows, width = logits.shape
    height = 16
    lane = lax.broadcasted_iota(jnp.int32, (height, LANES), 1)
    copies = []
    for index, row in enumerate(range(0, rows, height)):
        here = slice(row, row + height)
        ids = wanted[here, :] - first
        columns = [jnp.broadcast_to(ids[:, k : k + 1], (height, LANES)) for k in range(choices)]
        peak = None
        picks = [None] * choices
        start = 0
        for keep, arrivals in blocks:
            wide = keep.shape[1]
            marks = [came[here, wide:].astype(jnp.int32).astype(jnp.float32) for came in arrivals]
            for step in range(wide // tile):
                block = slice(step * tile, (step + 1) * tile)
                value = keep[here, block]
                for came, mark in zip(arrivals, marks):
                    value = value + decode(came[here, block], mark[:, step : step + 1])
                logits[here, start : start + tile] = value
                for part in range(tile // LANES):
                    piece = value[:, part * LANES : (part + 1) * LANES]
                    at = lane + (start + part * LANES)
                    peak = piece if peak is None else jnp.maximum(peak, piece)
                    for k in range(choices):
                        term = jnp.where(at == columns[k], piece, 0.0)
                        picks[k] = term if picks[k] is None else picks[k] + term
                start += tile
        copies.append(
            pltpu.make_async_copy(
                logits.at[pl.ds(row, height), :],
                total_logits.at[pl.ds(row, height), pl.ds(first, width)],
                sems.at[index],
            )
        )
        copies[-1].start()
        peak = jnp.max(peak, axis=1, keepdims=True)
        total = None
        for part in range(width // LANES):
            term = jnp.exp(logits[here, part * LANES : (part + 1) * LANES] - peak)
            total = term if total is None else total + term
        out = jnp.where(lane == 0, peak, jnp.zeros((height, LANES), jnp.float32))
        for k, item in enumerate([total] + picks):
            out = jnp.where(lane == k + 1, jnp.sum(item, axis=1, keepdims=True), out)
        stats[here, :] = out if before is None else merge_rows(before[here, :], out)
    for copy in copies:
        copy.wait()


def finish(wanted, blocks, tile, choices, first, vocab_width, earlier, after):
    rows = wanted.shape[0]
    width = sum(keep.shape[1] for keep, _ in blocks)
    operands = [wanted]
    for keep, arrivals in blocks:
        operands += [keep, *arrivals]
    operands += [earlier[1]] if earlier else []
    buffer = [earlier[0]] if earlier else []
    return pl.pallas_call(
        functools.partial(
            finish_body,
            tile=tile,
            choices=choices,
            first=first,
            counts=[len(arrivals) for _, arrivals in blocks],
            earlier=bool(earlier),
        ),
        in_specs=[VMEM] * len(operands) + [ANY] * len(buffer + after),
        out_specs=[ANY, VMEM],
        out_shape=[
            jax.ShapeDtypeStruct((rows, vocab_width), jnp.float32),
            jax.ShapeDtypeStruct((rows, LANES), jnp.float32),
        ],
        scratch_shapes=[
            pltpu.VMEM((rows, width), jnp.float32),
            pltpu.SemaphoreType.DMA((rows // 16,)),
        ],
        input_output_aliases={len(operands): 0} if earlier else {},
        cost_estimate=UNIT_COST,
        compiler_params=pltpu.CompilerParams(vmem_limit_bytes=FINISH_LIMIT),
    )(*operands, *buffer, *after)


def merge_body(low, own, came, out):
    first = jnp.where(low[0] == 1, own[...], came[...])
    second = jnp.where(low[0] == 1, came[...], own[...])
    out[...] = merge_rows(first, second)


def merge(low, own, came):
    return pl.pallas_call(
        merge_body,
        in_specs=[pl.BlockSpec(memory_space=pltpu.SMEM), VMEM, VMEM],
        out_specs=VMEM,
        out_shape=jax.ShapeDtypeStruct(own.shape, own.dtype),
        cost_estimate=UNIT_COST,
        compiler_params=pltpu.CompilerParams(vmem_limit_bytes=VMEM_LIMIT),
    )(low, own, came)


def tail_body(low, own, came, tree, logits, log_probs, scores, stats, *, heads, height, choices):
    merge_body(low, own, came, stats)
    blocks = log_probs.shape[0] // height
    paths = scores.shape[1]
    width = logits.shape[1]
    tile = widest(1024, width)
    for block in range(blocks):
        there = slice(block * height, (block + 1) * height)
        score = jnp.zeros((height, paths), jnp.float32)
        for head in range(heads):
            row = (block * heads + head) * height
            here = slice(row, row + height)
            normalizer = stats[here, 0:1] + jnp.log(stats[here, 1:2])
            for at in range(0, width, tile):
                log_probs[there, head, at : at + tile] = logits[here, at : at + tile] - normalizer
            found = jnp.zeros((height, paths), jnp.float32)
            for k in range(choices):
                picked = stats[here, 2 + k : 3 + k] - normalizer
                found = jnp.where(tree[head : head + 1, :] == k, picked, found)
            score = score + found
        scores[there, :] = score


def tail(low, own, came, tree, logits, out_rows, height, choices):
    heads, paths = tree.shape
    return pl.pallas_call(
        functools.partial(tail_body, heads=heads, height=height, choices=choices),
        in_specs=[pl.BlockSpec(memory_space=pltpu.SMEM)] + [VMEM] * 4,
        out_specs=[VMEM] * 2,
        out_shape=[
            jax.ShapeDtypeStruct((out_rows, heads, logits.shape[1]), jnp.float32),
            jax.ShapeDtypeStruct((out_rows, paths), jnp.float32),
        ],
        scratch_shapes=[pltpu.VMEM(own.shape, own.dtype)],
        cost_estimate=UNIT_COST,
        compiler_params=pltpu.CompilerParams(vmem_limit_bytes=VMEM_LIMIT),
    )(low, own, came, tree, logits)


def shards(
    hidden_states, accepted, norm_gain, head_weight, head_bias, vocab_weight, cand_ids, tree_paths
):
    batch, mp = lax.axis_size("batch"), lax.axis_size("mp")
    b, m = lax.axis_index("batch"), lax.axis_index("mp")
    rows, positions, feat = hidden_states.shape
    heads, inner, _ = head_weight.shape
    vocab_width = vocab_weight.shape[1]
    out_rows, _, choices = cand_ids.shape
    pieces = feat // inner
    ratio = out_rows // rows
    mp_bits = bits_of(mp)
    pair, core = b // 2, b % 2
    pair_bits = bits_of(batch // 2)

    taken = lax.broadcasted_iota(jnp.int32, (rows, positions, 1), 1) == (accepted - 1)[:, None, None]
    chosen = jnp.sum(jnp.where(taken, hidden_states, 0).astype(jnp.float32), axis=1)
    chosen = chosen.astype(jnp.bfloat16)
    other = swap(chosen, "batch", lambda i: i ^ 1)
    chosen = jnp.concatenate(
        [jnp.where(core == 0, chosen, other), jnp.where(core == 0, other, chosen)], axis=0
    ).astype(jnp.float32)
    gain = lax.dynamic_slice_in_dim(norm_gain, m * feat, feat, 0)

    if pieces == 2:
        sent = lax.dynamic_slice_in_dim(chosen, core * inner, inner, 1)
        sent_gain = lax.dynamic_slice_in_dim(gain, core * inner, inner, 0)
    else:
        sent = lax.dynamic_slice_in_dim(chosen, core * rows, rows, 0)
        sent_gain = gain
    sent = (sent * sent_gain).astype(jnp.bfloat16)
    perm = []
    for i in range(batch):
        for j in range(mp):
            perm.append((i * mp + j, (j * pieces + i % pieces) * mp + ((i // pieces) ^ j)))
    block = lax.ppermute(sent, ("batch", "mp"), perm)
    for bit in mp_bits:
        block = jnp.concatenate([block, swap(block, "mp", lambda i: i ^ bit)], axis=0)

    square_sum = jnp.sum(chosen * chosen, axis=1, keepdims=True)
    for bit in mp_bits:
        square_sum = square_sum + swap(square_sum, "mp", lambda i: i ^ bit)
    row_scale = lax.rsqrt(square_sum / (mp * feat) + EPSILON)
    own_normed = (chosen * row_scale * gain).astype(jnp.bfloat16).astype(jnp.float32)

    spots = []
    for unit in range(batch):
        source = (m ^ (unit // pieces) ^ (b // pieces)) * pieces + unit % pieces
        spots.append(((source // 2) ^ pair) * 2 + source % 2)
    first = jnp.stack([1 - core] + spots).astype(jnp.int32)
    then = jnp.stack([core] + spots).astype(jnp.int32)
    send = head_matmul(first, block, head_weight, rows, jnp.bfloat16)
    came = swap(send, "batch", lambda i: i ^ 1)
    keep = head_matmul(then, block, head_weight, rows, jnp.float32)
    units = batch // 2
    share = feat // 2
    tall = 2 * rows
    orders = (pair_bits, pair_bits[::-1])
    total = keep + came.astype(jnp.float32)
    halves = [
        {u: total[u * tall : (u + 1) * tall, h * share : (h + 1) * share] for u in range(units)}
        for h in range(2)
    ]
    for step in range(len(pair_bits)):
        arrived = []
        for half, order in zip(halves, orders):
            leave = [u for u in half if u & order[step]]
            outbound = jnp.concatenate([half[u] for u in leave], axis=0).astype(jnp.bfloat16)
            arrived.append(swap(outbound, "batch", lambda i: i ^ (2 * order[step])))
        for h, order in enumerate(orders):
            stay = [u for u in halves[h] if not u & order[step]]
            halves[h] = {
                u: halves[h][u] + arrived[h][i * tall : (i + 1) * tall].astype(jnp.float32)
                for i, u in enumerate(stay)
            }
    bias = lax.dynamic_slice_in_dim(head_bias, core, 1, 0)
    before = jnp.concatenate([half[0] for half in halves], axis=1) * row_scale + bias
    residual = (own_normed + jax.nn.silu(before)).astype(jnp.bfloat16)
    filled = [residual[:, :share], residual[:, share:]]
    held = [[0], [0]]
    parts, others = [], []
    block = residual
    for step in reversed(range(len(pair_bits))):
        arrived = [
            swap(filled[h], "batch", lambda i: i ^ (2 * orders[h][step])) for h in range(2)
        ]
        for h in range(2):
            held[h] = held[h] + [u ^ orders[h][step] for u in held[h]]
        came = jnp.concatenate(arrived, axis=1)
        if step == 0:
            parts.append(block)
            others.append(swap(block, "batch", lambda i: i ^ 1))
            block = came
        else:
            block = jnp.concatenate([block, came], axis=0)
            filled = [block[:, :share], block[:, share:]]
    parts.append(block)
    others.append(swap(block, "batch", lambda i: i ^ 1))

    table = []
    for whose in (core, 1 - core):
        for unit in range(batch):
            for h in range(2):
                source = (pair ^ held[h][unit // 2]) * 2 + unit % 2
                table.append((((source // ratio) ^ m) * ratio + source % ratio) * heads + whose)
    all_rows = gather_rows(jnp.stack(table).astype(jnp.int32), parts + others, rows, 2)
    wanted = (cand_ids - b * vocab_width).reshape(ratio, rows, heads, choices)
    wanted = wanted.transpose(0, 2, 1, 3).reshape(out_rows * heads, choices)
    wanted = jnp.pad(wanted, ((0, 0), (0, LANES - choices)), constant_values=-1)

    unit_width = vocab_width // 8
    plan = [(0, 1), (1, 2), (3, 2), (5, 2), (7, 1)]
    plan = [(first * unit_width, count * unit_width) for first, count in plan]
    tile = widest(512, unit_width)
    blocks = len(plan)
    stages = [mp_bits if block % 2 == 0 else mp_bits[::-1] for block in range(blocks)]
    keeps, sends, arrivals = [], [], [[] for _ in plan]

    def begin(block, after):
        first, width = plan[block]
        order = sorted(range(mp), key=lambda g: place(g, stages[block]))
        keep, send = vocab_matmul(all_rows, vocab_weight, first, width, order, tile, after)
        keeps.append(keep)
        sends.append(send)
        arrivals[block].append(swap(send, "mp", lambda i: i ^ stages[block][0]))

    def go_on(block, after):
        keep = keeps[block]
        for bit in stages[block][1:]:
            while len(arrivals[block]) > 1:
                rest = arrivals[block].pop(0)
                keep = add_kept(keep, rest, tile)
            send = fold(keep, arrivals[block][-1], tile, after)
            arrivals[block].append(swap(send, "mp", lambda i: i ^ bit))
        keeps[block] = keep
        return send

    def finish_blocks(group, earlier, after):
        return finish(
            wanted,
            [(keeps[block], arrivals[block]) for block in group],
            tile,
            choices,
            plan[group[0]][0],
            vocab_width,
            earlier,
            after,
        )

    begin(0, [])
    begin(1, [sends[0]])
    begin(2, [sends[1]])
    last = go_on(0, [sends[2]])
    begin(3, [last])
    last = go_on(1, [sends[3]])
    begin(4, [last, arrivals[2][0]])
    last = go_on(2, [sends[4], arrivals[0][-1]])
    joined = finish_blocks((0, 1), None, [last])
    last = go_on(3, [joined[1]])
    last = go_on(4, [last])
    joined = finish_blocks((2,), joined, [last])
    joined = finish_blocks((3, 4), joined, [])
    logits, stats = joined

    for bit in bits_of(batch):
        came = swap(stats, "batch", lambda i: i ^ bit)
        low = (1 - (b & bit) // bit).astype(jnp.int32).reshape(1)
        if 2 * bit < batch:
            stats = merge(low, stats, came)
    log_probs, path_scores = tail(
        low, stats, came, tree_paths.T, logits, out_rows, rows, choices
    )
    return (log_probs, path_scores)


def solution(mesh):
    return jax.shard_map(
        shards,
        mesh=mesh,
        in_specs=(
            P("batch", None, "mp"),
            P("batch"),
            P(),
            P(None, "batch", "mp"),
            P(None, "mp"),
            P("mp", "batch"),
            P("mp", None, None),
            P(),
        ),
        out_specs=(P("mp", None, "batch"), P("mp", None)),
        check_vma=False,
    )
```

```python
import functools

import jax
import jax.numpy as jnp
from jax import lax
from jax.experimental import pallas as pl
from jax.experimental.pallas import tpu as pltpu
from jax.sharding import PartitionSpec as P

EPSILON = 1e-05
MIB = 1024 * 1024
LANES = 128
CODE_BITS = 14
VMEM_LIMIT = 4 * MIB
VOCAB_LIMIT = 24 * MIB
FINISH_LIMIT = 10 * MIB


def bits_of(count):
    return [1 << i for i in range(count.bit_length() - 1)]


def swap(array, axis, partner):
    return lax.ppermute(array, axis, [(i, partner(i)) for i in range(lax.axis_size(axis))])


def place(index, stages):
    spot = 0
    for bit in stages:
        spot = 2 * spot + (index & bit) // bit
    return spot


def unplace(spot, stages):
    index = 0
    for step, bit in enumerate(stages[::-1]):
        index = index + ((spot >> step) & 1) * bit
    return index


def widest(limit, size):
    tile = min(limit, size)
    while size % tile:
        tile //= 2
    return tile


VMEM = pl.BlockSpec(memory_space=pltpu.VMEM)
ANY = pl.BlockSpec(memory_space=pl.ANY)
WAYS = 4
UNIT_COST = pl.CostEstimate(flops=1, bytes_accessed=1, transcendentals=0)


def stream(source, held, sems, first, tile):
    depth, width = held.shape
    share = depth // WAYS

    def copies(n):
        at = n * tile if isinstance(n, int) else pl.multiple_of(n * tile, tile)
        return [
            pltpu.make_async_copy(
                source.at[pl.ds(way * share, share), pl.ds(first + at, tile)],
                held.at[pl.ds(way * share, share), pl.ds(at, tile)],
                sems.at[n, way],
            )
            for way in range(WAYS)
        ]

    def begin(n, carry):
        for copy in copies(n):
            copy.start()
        return carry

    lax.fori_loop(0, width // tile, begin, 0)

    def wait(n):
        for copy in copies(n):
            copy.wait()

    return wait


def head_body(info, came, source, out, rows, held, sems, *, height, tile):
    wait = stream(source.at[info[0]], held, sems, 0, tile)
    for unit in range(came.shape[0] // height):
        start = pl.multiple_of(info[1 + unit] * height, height)
        rows[pl.ds(start, height), :] = came[unit * height : (unit + 1) * height, :]

    def step(n, carry):
        at = pl.ds(pl.multiple_of(n * tile, tile), tile)
        wait(n)
        total = jnp.dot(rows[...], held[:, at], preferred_element_type=jnp.float32)
        out[:, at] = total.astype(out.dtype)
        return carry

    lax.fori_loop(0, held.shape[1] // tile, step, 0)


def head_matmul(info, came, head_weight, height, out_type):
    count, depth = came.shape
    width = head_weight.shape[2]
    tile = widest(512, width // 2)
    return pl.pallas_call(
        functools.partial(head_body, height=height, tile=tile),
        in_specs=[pl.BlockSpec(memory_space=pltpu.SMEM), VMEM, ANY],
        out_specs=VMEM,
        out_shape=jax.ShapeDtypeStruct((count, width), out_type),
        scratch_shapes=[
            pltpu.VMEM((count, depth), jnp.bfloat16),
            pltpu.VMEM((depth, width), jnp.bfloat16),
            pltpu.SemaphoreType.DMA((width // tile, WAYS)),
        ],
        cost_estimate=UNIT_COST,
        compiler_params=pltpu.CompilerParams(vmem_limit_bytes=VOCAB_LIMIT),
    )(info, came, head_weight)


def encode(value):
    top = jnp.max(jnp.abs(value), axis=1, keepdims=True)
    power = jnp.floor(jnp.log2(jnp.maximum(top, 1e-30))) + 1.0
    code = jnp.floor(value * jnp.exp2(CODE_BITS - power) + 0.5)
    return code.astype(jnp.int32).astype(jnp.int16), power


def decode(code, power):
    return code.astype(jnp.int32).astype(jnp.float32) * jnp.exp2(power - CODE_BITS)


def marks_of(powers, height):
    lane = lax.broadcasted_iota(jnp.int32, (height, LANES), 1)
    marks = jnp.zeros((height, LANES), jnp.float32)
    for index, power in enumerate(powers):
        marks = jnp.where(lane == index, power, marks)
    return marks.astype(jnp.int32).astype(jnp.int16)


def gather_body(spots, *refs, height, halves):
    parts, rows = refs[:-1], refs[-1]
    share = rows.shape[1] // halves
    unit = 0
    for part in parts:
        for block in range(part.shape[0] // height):
            for half in range(halves):
                start = pl.multiple_of(spots[unit] * height, height)
                columns = slice(half * share, (half + 1) * share)
                rows[pl.ds(start, height), columns] = part[
                    block * height : (block + 1) * height, columns
                ]
                unit += 1


def gather_rows(spots, parts, height, halves):
    count = sum(p.shape[0] for p in parts)
    return pl.pallas_call(
        functools.partial(gather_body, height=height, halves=halves),
        in_specs=[pl.BlockSpec(memory_space=pltpu.SMEM)] + [VMEM] * len(parts),
        out_specs=VMEM,
        out_shape=jax.ShapeDtypeStruct((count, parts[0].shape[1]), parts[0].dtype),
        cost_estimate=UNIT_COST,
        compiler_params=pltpu.CompilerParams(vmem_limit_bytes=VMEM_LIMIT),
    )(spots, *parts)


def vocab_body(rows, source, *refs, order, tile, first, waits):
    stay, go, send, held, powers, sems = refs[waits:]
    wait = stream(source, held, sems, first, tile)
    height = rows.shape[0] // len(order)
    half = len(order) // 2
    width = held.shape[1]
    lane = lax.broadcasted_iota(jnp.int32, powers.shape, 1)
    powers[...] = jnp.zeros_like(powers)

    def step(n, carry):
        at = pl.ds(pl.multiple_of(n * tile, tile), tile)
        wait(n)
        total = jnp.dot(rows[...], held[:, at], preferred_element_type=jnp.float32)
        sorted_rows = [total[g * height : (g + 1) * height] for g in order]
        stay[:, at] = jnp.concatenate(sorted_rows[: half // 2], axis=0)
        go[:, at] = jnp.concatenate(sorted_rows[half // 2 : half], axis=0)
        code, power = encode(jnp.concatenate(sorted_rows[half:], axis=0))
        send[:, at] = code
        powers[...] = jnp.where(lane == n, power, powers[...])
        return carry

    lax.fori_loop(0, width // tile, step, 0)
    send[:, width:] = powers[...].astype(jnp.int32).astype(jnp.int16)


def vocab_matmul(rows, vocab_weight, first, width, order, tile, after):
    depth = vocab_weight.shape[0]
    count = rows.shape[0]
    half = count // 2
    return pl.pallas_call(
        functools.partial(vocab_body, order=order, tile=tile, first=first, waits=len(after)),
        in_specs=[VMEM] + [ANY] * (1 + len(after)),
        out_specs=[VMEM] * 3,
        out_shape=[
            jax.ShapeDtypeStruct((half // 2, width), jnp.float32),
            jax.ShapeDtypeStruct((half // 2, width), jnp.float32),
            jax.ShapeDtypeStruct((half, width + LANES), jnp.int16),
        ],
        scratch_shapes=[
            pltpu.VMEM((depth, width), jnp.bfloat16),
            pltpu.VMEM((half, LANES), jnp.float32),
            pltpu.SemaphoreType.DMA((width // tile, WAYS)),
        ],
        compiler_params=pltpu.CompilerParams(vmem_limit_bytes=VOCAB_LIMIT),
        cost_estimate=UNIT_COST,
    )(rows, vocab_weight, *after)


def fold_body(keep, came, *refs, tile):
    send = refs[-1]
    half = send.shape[0]
    width = keep.shape[1]
    skip = keep.shape[0] - half
    for row in range(half, 2 * half, 16):
        here, there = slice(row, row + 16), slice(row - half, row - half + 16)
        held = slice(row - half + skip, row - half + skip + 16)
        marks = came[here, width:].astype(jnp.int32).astype(jnp.float32)
        powers = []
        for step in range(width // tile):
            block = slice(step * tile, (step + 1) * tile)
            value = keep[held, block] + decode(came[here, block], marks[:, step : step + 1])
            code, power = encode(value)
            send[there, block] = code
            powers.append(power)
        send[there, width:] = marks_of(powers, 16)


def fold(keep, came, tile, after):
    rows, width = came.shape[0], keep.shape[1]
    return pl.pallas_call(
        functools.partial(fold_body, tile=tile),
        in_specs=[VMEM] * 2 + [ANY] * len(after),
        out_specs=VMEM,
        out_shape=jax.ShapeDtypeStruct((rows // 2, width + LANES), jnp.int16),
        cost_estimate=UNIT_COST,
        compiler_params=pltpu.CompilerParams(vmem_limit_bytes=VMEM_LIMIT),
    )(keep, came, *after)


def add_body(keep, came, out, *, tile):
    half, width = out.shape
    for row in range(0, half, 16):
        here = slice(row, row + 16)
        marks = came[here, width:].astype(jnp.int32).astype(jnp.float32)
        for step in range(width // tile):
            block = slice(step * tile, (step + 1) * tile)
            out[here, block] = keep[here, block] + decode(came[here, block], marks[:, step : step + 1])


def add_kept(keep, came, tile):
    rows, width = came.shape[0], keep.shape[1]
    return pl.pallas_call(
        functools.partial(add_body, tile=tile),
        in_specs=[VMEM] * 2,
        out_specs=VMEM,
        out_shape=jax.ShapeDtypeStruct((rows // 2, width), jnp.float32),
        cost_estimate=UNIT_COST,
        compiler_params=pltpu.CompilerParams(vmem_limit_bytes=VMEM_LIMIT),
    )(keep, came)


def merge_rows(one, two):
    peak = jnp.maximum(one[:, :1], two[:, :1])
    lane = lax.broadcasted_iota(jnp.int32, one.shape, 1)
    factor_one = jnp.where(lane == 1, jnp.exp(one[:, :1] - peak), 1.0)
    factor_two = jnp.where(lane == 1, jnp.exp(two[:, :1] - peak), 1.0)
    return jnp.where(lane == 0, peak, one * factor_one + two * factor_two)


def finish_body(wanted, *refs, tile, choices, first, counts, earlier):
    blocks = []
    for count in counts:
        blocks.append((refs[0], refs[1 : 1 + count]))
        refs = refs[1 + count :]
    before = refs[0] if earlier else None
    total_logits, stats, logits, sems = refs[-4:]
    rows, width = logits.shape
    height = 16
    lane = lax.broadcasted_iota(jnp.int32, (height, LANES), 1)
    copies = []
    for index, row in enumerate(range(0, rows, height)):
        here = slice(row, row + height)
        ids = wanted[here, :] - first
        columns = [jnp.broadcast_to(ids[:, k : k + 1], (height, LANES)) for k in range(choices)]
        peak = None
        picks = [None] * choices
        start = 0
        for keep, arrivals in blocks:
            wide = keep.shape[1]
            marks = [came[here, wide:].astype(jnp.int32).astype(jnp.float32) for came in arrivals]
            for step in range(wide // tile):
                block = slice(step * tile, (step + 1) * tile)
                value = keep[here, block]
                for came, mark in zip(arrivals, marks):
                    value = value + decode(came[here, block], mark[:, step : step + 1])
                logits[here, start : start + tile] = value
                for part in range(tile // LANES):
                    piece = value[:, part * LANES : (part + 1) * LANES]
                    at = lane + (start + part * LANES)
                    peak = piece if peak is None else jnp.maximum(peak, piece)
                    for k in range(choices):
                        term = jnp.where(at == columns[k], piece, 0.0)
                        picks[k] = term if picks[k] is None else picks[k] + term
                start += tile
        copies.append(
            pltpu.make_async_copy(
                logits.at[pl.ds(row, height), :],
                total_logits.at[pl.ds(row, height), pl.ds(first, width)],
                sems.at[index],
            )
        )
        copies[-1].start()
        peak = jnp.max(peak, axis=1, keepdims=True)
        total = None
        for part in range(width // LANES):
            term = jnp.exp(logits[here, part * LANES : (part + 1) * LANES] - peak)
            total = term if total is None else total + term
        out = jnp.where(lane == 0, peak, jnp.zeros((height, LANES), jnp.float32))
        for k, item in enumerate([total] + picks):
            out = jnp.where(lane == k + 1, jnp.sum(item, axis=1, keepdims=True), out)
        stats[here, :] = out if before is None else merge_rows(before[here, :], out)
    for copy in copies:
        copy.wait()


def finish(wanted, blocks, tile, choices, first, vocab_width, earlier, after):
    rows = wanted.shape[0]
    width = sum(keep.shape[1] for keep, _ in blocks)
    operands = [wanted]
    for keep, arrivals in blocks:
        operands += [keep, *arrivals]
    operands += [earlier[1]] if earlier else []
    buffer = [earlier[0]] if earlier else []
    return pl.pallas_call(
        functools.partial(
            finish_body,
            tile=tile,
            choices=choices,
            first=first,
            counts=[len(arrivals) for _, arrivals in blocks],
            earlier=bool(earlier),
        ),
        in_specs=[VMEM] * len(operands) + [ANY] * len(buffer + after),
        out_specs=[ANY, VMEM],
        out_shape=[
            jax.ShapeDtypeStruct((rows, vocab_width), jnp.float32),
            jax.ShapeDtypeStruct((rows, LANES), jnp.float32),
        ],
        scratch_shapes=[
            pltpu.VMEM((rows, width), jnp.float32),
            pltpu.SemaphoreType.DMA((rows // 16,)),
        ],
        input_output_aliases={len(operands): 0} if earlier else {},
        cost_estimate=UNIT_COST,
        compiler_params=pltpu.CompilerParams(vmem_limit_bytes=FINISH_LIMIT),
    )(*operands, *buffer, *after)


def merge_body(low, own, came, out):
    first = jnp.where(low[0] == 1, own[...], came[...])
    second = jnp.where(low[0] == 1, came[...], own[...])
    out[...] = merge_rows(first, second)


def merge(low, own, came):
    return pl.pallas_call(
        merge_body,
        in_specs=[pl.BlockSpec(memory_space=pltpu.SMEM), VMEM, VMEM],
        out_specs=VMEM,
        out_shape=jax.ShapeDtypeStruct(own.shape, own.dtype),
        cost_estimate=UNIT_COST,
        compiler_params=pltpu.CompilerParams(vmem_limit_bytes=VMEM_LIMIT),
    )(low, own, came)


def tail_body(low, own, came, tree, logits, log_probs, scores, stats, *, heads, height, choices):
    merge_body(low, own, came, stats)
    blocks = log_probs.shape[0] // height
    paths = scores.shape[1]
    width = logits.shape[1]
    tile = widest(1024, width)
    for block in range(blocks):
        there = slice(block * height, (block + 1) * height)
        score = jnp.zeros((height, paths), jnp.float32)
        for head in range(heads):
            row = (block * heads + head) * height
            here = slice(row, row + height)
            normalizer = stats[here, 0:1] + jnp.log(stats[here, 1:2])
            for at in range(0, width, tile):
                log_probs[there, head, at : at + tile] = logits[here, at : at + tile] - normalizer
            found = jnp.zeros((height, paths), jnp.float32)
            for k in range(choices):
                picked = stats[here, 2 + k : 3 + k] - normalizer
                found = jnp.where(tree[head : head + 1, :] == k, picked, found)
            score = score + found
        scores[there, :] = score


def tail(low, own, came, tree, logits, out_rows, height, choices):
    heads, paths = tree.shape
    return pl.pallas_call(
        functools.partial(tail_body, heads=heads, height=height, choices=choices),
        in_specs=[pl.BlockSpec(memory_space=pltpu.SMEM)] + [VMEM] * 4,
        out_specs=[VMEM] * 2,
        out_shape=[
            jax.ShapeDtypeStruct((out_rows, heads, logits.shape[1]), jnp.float32),
            jax.ShapeDtypeStruct((out_rows, paths), jnp.float32),
        ],
        scratch_shapes=[pltpu.VMEM(own.shape, own.dtype)],
        cost_estimate=UNIT_COST,
        compiler_params=pltpu.CompilerParams(vmem_limit_bytes=VMEM_LIMIT),
    )(low, own, came, tree, logits)


def shards(
    hidden_states, accepted, norm_gain, head_weight, head_bias, vocab_weight, cand_ids, tree_paths
):
    batch, mp = lax.axis_size("batch"), lax.axis_size("mp")
    b, m = lax.axis_index("batch"), lax.axis_index("mp")
    rows, positions, feat = hidden_states.shape
    heads, inner, _ = head_weight.shape
    vocab_width = vocab_weight.shape[1]
    out_rows, _, choices = cand_ids.shape
    pieces = feat // inner
    ratio = out_rows // rows
    mp_bits = bits_of(mp)
    pair, core = b // 2, b % 2
    pair_bits = bits_of(batch // 2)

    taken = lax.broadcasted_iota(jnp.int32, (rows, positions, 1), 1) == (accepted - 1)[:, None, None]
    chosen = jnp.sum(jnp.where(taken, hidden_states, 0).astype(jnp.float32), axis=1)
    chosen = chosen.astype(jnp.bfloat16)
    other = swap(chosen, "batch", lambda i: i ^ 1)
    chosen = jnp.concatenate(
        [jnp.where(core == 0, chosen, other), jnp.where(core == 0, other, chosen)], axis=0
    ).astype(jnp.float32)
    gain = lax.dynamic_slice_in_dim(norm_gain, m * feat, feat, 0)

    if pieces == 2:
        sent = lax.dynamic_slice_in_dim(chosen, core * inner, inner, 1)
        sent_gain = lax.dynamic_slice_in_dim(gain, core * inner, inner, 0)
    else:
        sent = lax.dynamic_slice_in_dim(chosen, core * rows, rows, 0)
        sent_gain = gain
    sent = (sent * sent_gain).astype(jnp.bfloat16)
    perm = []
    for i in range(batch):
        for j in range(mp):
            perm.append((i * mp + j, (j * pieces + i % pieces) * mp + ((i // pieces) ^ j)))
    block = lax.ppermute(sent, ("batch", "mp"), perm)
    for bit in mp_bits:
        block = jnp.concatenate([block, swap(block, "mp", lambda i: i ^ bit)], axis=0)

    square_sum = jnp.sum(chosen * chosen, axis=1, keepdims=True)
    for bit in mp_bits:
        square_sum = square_sum + swap(square_sum, "mp", lambda i: i ^ bit)
    row_scale = lax.rsqrt(square_sum / (mp * feat) + EPSILON)
    own_normed = (chosen * row_scale * gain).astype(jnp.bfloat16).astype(jnp.float32)

    spots = []
    for unit in range(batch):
        source = (m ^ (unit // pieces) ^ (b // pieces)) * pieces + unit % pieces
        spots.append(((source // 2) ^ pair) * 2 + source % 2)
    first = jnp.stack([1 - core] + spots).astype(jnp.int32)
    then = jnp.stack([core] + spots).astype(jnp.int32)
    send = head_matmul(first, block, head_weight, rows, jnp.bfloat16)
    came = swap(send, "batch", lambda i: i ^ 1)
    keep = head_matmul(then, block, head_weight, rows, jnp.float32)
    units = batch // 2
    share = feat // 2
    tall = 2 * rows
    orders = (pair_bits, pair_bits[::-1])
    total = keep + came.astype(jnp.float32)
    halves = [
        {u: total[u * tall : (u + 1) * tall, h * share : (h + 1) * share] for u in range(units)}
        for h in range(2)
    ]
    for step in range(len(pair_bits)):
        arrived = []
        for half, order in zip(halves, orders):
            leave = [u for u in half if u & order[step]]
            outbound = jnp.concatenate([half[u] for u in leave], axis=0).astype(jnp.bfloat16)
            arrived.append(swap(outbound, "batch", lambda i: i ^ (2 * order[step])))
        for h, order in enumerate(orders):
            stay = [u for u in halves[h] if not u & order[step]]
            halves[h] = {
                u: halves[h][u] + arrived[h][i * tall : (i + 1) * tall].astype(jnp.float32)
                for i, u in enumerate(stay)
            }
    bias = lax.dynamic_slice_in_dim(head_bias, core, 1, 0)
    before = jnp.concatenate([half[0] for half in halves], axis=1) * row_scale + bias
    residual = (own_normed + jax.nn.silu(before)).astype(jnp.bfloat16)
    filled = [residual[:, :share], residual[:, share:]]
    held = [[0], [0]]
    parts, others = [], []
    block = residual
    for step in reversed(range(len(pair_bits))):
        arrived = [
            swap(filled[h], "batch", lambda i: i ^ (2 * orders[h][step])) for h in range(2)
        ]
        for h in range(2):
            held[h] = held[h] + [u ^ orders[h][step] for u in held[h]]
        came = jnp.concatenate(arrived, axis=1)
        if step == 0:
            parts.append(block)
            others.append(swap(block, "batch", lambda i: i ^ 1))
            block = came
        else:
            block = jnp.concatenate([block, came], axis=0)
            filled = [block[:, :share], block[:, share:]]
    parts.append(block)
    others.append(swap(block, "batch", lambda i: i ^ 1))

    table = []
    for whose in (core, 1 - core):
        for unit in range(batch):
            for h in range(2):
                source = (pair ^ held[h][unit // 2]) * 2 + unit % 2
                table.append((((source // ratio) ^ m) * ratio + source % ratio) * heads + whose)
    all_rows = gather_rows(jnp.stack(table).astype(jnp.int32), parts + others, rows, 2)
    wanted = (cand_ids - b * vocab_width).reshape(ratio, rows, heads, choices)
    wanted = wanted.transpose(0, 2, 1, 3).reshape(out_rows * heads, choices)
    wanted = jnp.pad(wanted, ((0, 0), (0, LANES - choices)), constant_values=-1)

    unit_width = vocab_width // 8
    plan = [(0, 1), (1, 2), (3, 2), (5, 2), (7, 1)]
    plan = [(first * unit_width, count * unit_width) for first, count in plan]
    tile = widest(512, unit_width)
    blocks = len(plan)
    stages = [mp_bits if block % 2 == 0 else mp_bits[::-1] for block in range(blocks)]
    keeps, goes, sends, arrivals = [], [], [], [[] for _ in plan]

    def begin(block, after):
        first, width = plan[block]
        order = sorted(range(mp), key=lambda g: place(g, stages[block]))
        stay, go, send = vocab_matmul(all_rows, vocab_weight, first, width, order, tile, after)
        keeps.append(stay)
        goes.append(go)
        sends.append(send)
        arrivals[block].append(swap(send, "mp", lambda i: i ^ stages[block][0]))

    def go_on(block, after):
        keep, go = keeps[block], goes[block]
        for bit in stages[block][1:]:
            while len(arrivals[block]) > 1:
                rest = arrivals[block].pop(0)
                keep = go = add_kept(keep, rest, tile)
            send = fold(go, arrivals[block][-1], tile, after)
            arrivals[block].append(swap(send, "mp", lambda i: i ^ bit))
        keeps[block] = keep
        return send

    def finish_blocks(group, earlier, after):
        return finish(
            wanted,
            [(keeps[block], arrivals[block]) for block in group],
            tile,
            choices,
            plan[group[0]][0],
            vocab_width,
            earlier,
            after,
        )

    begin(0, [])
    begin(1, [sends[0]])
    begin(2, [sends[1]])
    last = go_on(0, [sends[2]])
    begin(3, [last])
    last = go_on(1, [sends[3]])
    begin(4, [last, arrivals[2][0]])
    last = go_on(2, [sends[4]])
    joined = finish_blocks((0, 1), None, [last])
    last = go_on(3, [joined[1]])
    last = go_on(4, [last])
    joined = finish_blocks((2,), joined, [last])
    joined = finish_blocks((3, 4), joined, [])
    logits, stats = joined

    for bit in bits_of(batch):
        came = swap(stats, "batch", lambda i: i ^ bit)
        low = (1 - (b & bit) // bit).astype(jnp.int32).reshape(1)
        if 2 * bit < batch:
            stats = merge(low, stats, came)
    log_probs, path_scores = tail(
        low, stats, came, tree_paths.T, logits, out_rows, rows, choices
    )
    return (log_probs, path_scores)


def solution(mesh):
    return jax.shard_map(
        shards,
        mesh=mesh,
        in_specs=(
            P("batch", None, "mp"),
            P("batch"),
            P(),
            P(None, "batch", "mp"),
            P(None, "mp"),
            P("mp", "batch"),
            P("mp", None, None),
            P(),
        ),
        out_specs=(P("mp", None, "batch"), P("mp", None)),
        check_vma=False,
    )
```

```python
import functools

import jax
import jax.numpy as jnp
from jax import lax
from jax.experimental import pallas as pl
from jax.experimental.pallas import tpu as pltpu
from jax.sharding import PartitionSpec as P

EPSILON = 1e-05
MIB = 1024 * 1024
LANES = 128
CODE_BITS = 14
VMEM_LIMIT = 4 * MIB
VOCAB_LIMIT = 24 * MIB
FINISH_LIMIT = 10 * MIB


def bits_of(count):
    return [1 << i for i in range(count.bit_length() - 1)]


def swap(array, axis, partner):
    return lax.ppermute(array, axis, [(i, partner(i)) for i in range(lax.axis_size(axis))])


def place(index, stages):
    spot = 0
    for bit in stages:
        spot = 2 * spot + (index & bit) // bit
    return spot


def unplace(spot, stages):
    index = 0
    for step, bit in enumerate(stages[::-1]):
        index = index + ((spot >> step) & 1) * bit
    return index


def widest(limit, size):
    tile = min(limit, size)
    while size % tile:
        tile //= 2
    return tile


VMEM = pl.BlockSpec(memory_space=pltpu.VMEM)
ANY = pl.BlockSpec(memory_space=pl.ANY)
WAYS = 4
UNIT_COST = pl.CostEstimate(flops=1, bytes_accessed=1, transcendentals=0)


def stream(source, held, sems, first, tile):
    depth, width = held.shape
    share = depth // WAYS

    def copies(n):
        at = n * tile if isinstance(n, int) else pl.multiple_of(n * tile, tile)
        return [
            pltpu.make_async_copy(
                source.at[pl.ds(way * share, share), pl.ds(first + at, tile)],
                held.at[pl.ds(way * share, share), pl.ds(at, tile)],
                sems.at[n, way],
            )
            for way in range(WAYS)
        ]

    def begin(n, carry):
        for copy in copies(n):
            copy.start()
        return carry

    lax.fori_loop(0, width // tile, begin, 0)

    def wait(n):
        for copy in copies(n):
            copy.wait()

    return wait


def head_body(info, came, source, out, rows, held, sems, *, height, tile):
    wait = stream(source.at[info[0]], held, sems, 0, tile)
    for unit in range(came.shape[0] // height):
        start = pl.multiple_of(info[1 + unit] * height, height)
        rows[pl.ds(start, height), :] = came[unit * height : (unit + 1) * height, :]

    def step(n, carry):
        at = pl.ds(pl.multiple_of(n * tile, tile), tile)
        wait(n)
        total = jnp.dot(rows[...], held[:, at], preferred_element_type=jnp.float32)
        out[:, at] = total.astype(out.dtype)
        return carry

    lax.fori_loop(0, held.shape[1] // tile, step, 0)


def head_matmul(info, came, head_weight, height, out_type):
    count, depth = came.shape
    width = head_weight.shape[2]
    tile = widest(512, width // 2)
    return pl.pallas_call(
        functools.partial(head_body, height=height, tile=tile),
        in_specs=[pl.BlockSpec(memory_space=pltpu.SMEM), VMEM, ANY],
        out_specs=VMEM,
        out_shape=jax.ShapeDtypeStruct((count, width), out_type),
        scratch_shapes=[
            pltpu.VMEM((count, depth), jnp.bfloat16),
            pltpu.VMEM((depth, width), jnp.bfloat16),
            pltpu.SemaphoreType.DMA((width // tile, WAYS)),
        ],
        cost_estimate=UNIT_COST,
        compiler_params=pltpu.CompilerParams(vmem_limit_bytes=VOCAB_LIMIT),
    )(info, came, head_weight)


def encode(value):
    top = jnp.max(jnp.abs(value), axis=1, keepdims=True)
    power = jnp.floor(jnp.log2(jnp.maximum(top, 1e-30))) + 1.0
    code = jnp.floor(value * jnp.exp2(CODE_BITS - power) + 0.5)
    return code.astype(jnp.int32).astype(jnp.int16), power


def decode(code, power):
    return code.astype(jnp.int32).astype(jnp.float32) * jnp.exp2(power - CODE_BITS)


def marks_of(powers, height):
    lane = lax.broadcasted_iota(jnp.int32, (height, LANES), 1)
    marks = jnp.zeros((height, LANES), jnp.float32)
    for index, power in enumerate(powers):
        marks = jnp.where(lane == index, power, marks)
    return marks.astype(jnp.int32).astype(jnp.int16)


def gather_body(spots, *refs, height, halves):
    parts, rows = refs[:-1], refs[-1]
    share = rows.shape[1] // halves
    unit = 0
    for part in parts:
        for block in range(part.shape[0] // height):
            for half in range(halves):
                start = pl.multiple_of(spots[unit] * height, height)
                columns = slice(half * share, (half + 1) * share)
                rows[pl.ds(start, height), columns] = part[
                    block * height : (block + 1) * height, columns
                ]
                unit += 1


def gather_rows(spots, parts, height, halves):
    count = sum(p.shape[0] for p in parts)
    return pl.pallas_call(
        functools.partial(gather_body, height=height, halves=halves),
        in_specs=[pl.BlockSpec(memory_space=pltpu.SMEM)] + [VMEM] * len(parts),
        out_specs=VMEM,
        out_shape=jax.ShapeDtypeStruct((count, parts[0].shape[1]), parts[0].dtype),
        cost_estimate=UNIT_COST,
        compiler_params=pltpu.CompilerParams(vmem_limit_bytes=VMEM_LIMIT),
    )(spots, *parts)


def vocab_body(rows, source, *refs, order, tile, first, waits):
    stay, go, send, held, powers, sems = refs[waits:]
    part = widest(256, tile)
    wait = stream(source, held, sems, first, part)
    height = rows.shape[0] // len(order)
    half = len(order) // 2
    width = held.shape[1]
    lane = lax.broadcasted_iota(jnp.int32, powers.shape, 1)
    powers[...] = jnp.zeros_like(powers)

    def step(n, carry):
        at = pl.ds(pl.multiple_of(n * tile, tile), tile)
        terms = []
        for index in range(tile // part):
            wait(n * (tile // part) + index)
            columns = pl.ds(pl.multiple_of(n * tile + index * part, part), part)
            terms.append(
                jnp.dot(rows[...], held[:, columns], preferred_element_type=jnp.float32)
            )
        total = jnp.concatenate(terms, axis=1)
        sorted_rows = [total[g * height : (g + 1) * height] for g in order]
        stay[:, at] = jnp.concatenate(sorted_rows[: half // 2], axis=0)
        go[:, at] = jnp.concatenate(sorted_rows[half // 2 : half], axis=0)
        code, power = encode(jnp.concatenate(sorted_rows[half:], axis=0))
        send[:, at] = code
        powers[...] = jnp.where(lane == n, power, powers[...])
        return carry

    lax.fori_loop(0, width // tile, step, 0)
    send[:, width:] = powers[...].astype(jnp.int32).astype(jnp.int16)


def vocab_matmul(rows, vocab_weight, first, width, order, tile, after):
    depth = vocab_weight.shape[0]
    count = rows.shape[0]
    half = count // 2
    return pl.pallas_call(
        functools.partial(vocab_body, order=order, tile=tile, first=first, waits=len(after)),
        in_specs=[VMEM] + [ANY] * (1 + len(after)),
        out_specs=[VMEM] * 3,
        out_shape=[
            jax.ShapeDtypeStruct((half // 2, width), jnp.float32),
            jax.ShapeDtypeStruct((half // 2, width), jnp.float32),
            jax.ShapeDtypeStruct((half, width + LANES), jnp.int16),
        ],
        scratch_shapes=[
            pltpu.VMEM((depth, width), jnp.bfloat16),
            pltpu.VMEM((half, LANES), jnp.float32),
            pltpu.SemaphoreType.DMA((width // widest(256, tile), WAYS)),
        ],
        compiler_params=pltpu.CompilerParams(vmem_limit_bytes=VOCAB_LIMIT),
        cost_estimate=UNIT_COST,
    )(rows, vocab_weight, *after)


def fold_body(keep, came, *refs, tile):
    send = refs[-1]
    half = send.shape[0]
    width = keep.shape[1]
    skip = keep.shape[0] - half
    for row in range(half, 2 * half, 16):
        here, there = slice(row, row + 16), slice(row - half, row - half + 16)
        held = slice(row - half + skip, row - half + skip + 16)
        marks = came[here, width:].astype(jnp.int32).astype(jnp.float32)
        powers = []
        for step in range(width // tile):
            block = slice(step * tile, (step + 1) * tile)
            value = keep[held, block] + decode(came[here, block], marks[:, step : step + 1])
            code, power = encode(value)
            send[there, block] = code
            powers.append(power)
        send[there, width:] = marks_of(powers, 16)


def fold(keep, came, tile, after):
    rows, width = came.shape[0], keep.shape[1]
    return pl.pallas_call(
        functools.partial(fold_body, tile=tile),
        in_specs=[VMEM] * 2 + [ANY] * len(after),
        out_specs=VMEM,
        out_shape=jax.ShapeDtypeStruct((rows // 2, width + LANES), jnp.int16),
        cost_estimate=UNIT_COST,
        compiler_params=pltpu.CompilerParams(vmem_limit_bytes=VMEM_LIMIT),
    )(keep, came, *after)


def add_body(keep, came, out, *, tile):
    half, width = out.shape
    for row in range(0, half, 16):
        here = slice(row, row + 16)
        marks = came[here, width:].astype(jnp.int32).astype(jnp.float32)
        for step in range(width // tile):
            block = slice(step * tile, (step + 1) * tile)
            out[here, block] = keep[here, block] + decode(came[here, block], marks[:, step : step + 1])


def add_kept(keep, came, tile):
    rows, width = came.shape[0], keep.shape[1]
    return pl.pallas_call(
        functools.partial(add_body, tile=tile),
        in_specs=[VMEM] * 2,
        out_specs=VMEM,
        out_shape=jax.ShapeDtypeStruct((rows // 2, width), jnp.float32),
        cost_estimate=UNIT_COST,
        compiler_params=pltpu.CompilerParams(vmem_limit_bytes=VMEM_LIMIT),
    )(keep, came)


def merge_rows(one, two):
    peak = jnp.maximum(one[:, :1], two[:, :1])
    lane = lax.broadcasted_iota(jnp.int32, one.shape, 1)
    factor_one = jnp.where(lane == 1, jnp.exp(one[:, :1] - peak), 1.0)
    factor_two = jnp.where(lane == 1, jnp.exp(two[:, :1] - peak), 1.0)
    return jnp.where(lane == 0, peak, one * factor_one + two * factor_two)


def finish_body(wanted, *refs, tile, choices, first, counts, earlier):
    blocks = []
    for count in counts:
        blocks.append((refs[0], refs[1 : 1 + count]))
        refs = refs[1 + count :]
    before = refs[0] if earlier else None
    total_logits, stats, logits, sems = refs[-4:]
    rows, width = logits.shape
    height = 16
    lane = lax.broadcasted_iota(jnp.int32, (height, LANES), 1)
    copies = []
    for index, row in enumerate(range(0, rows, height)):
        here = slice(row, row + height)
        ids = wanted[here, :] - first
        columns = [jnp.broadcast_to(ids[:, k : k + 1], (height, LANES)) for k in range(choices)]
        peak = None
        picks = [None] * choices
        start = 0
        for keep, arrivals in blocks:
            wide = keep.shape[1]
            marks = [came[here, wide:].astype(jnp.int32).astype(jnp.float32) for came in arrivals]
            for step in range(wide // tile):
                block = slice(step * tile, (step + 1) * tile)
                value = keep[here, block]
                for came, mark in zip(arrivals, marks):
                    value = value + decode(came[here, block], mark[:, step : step + 1])
                logits[here, start : start + tile] = value
                for part in range(tile // LANES):
                    piece = value[:, part * LANES : (part + 1) * LANES]
                    at = lane + (start + part * LANES)
                    peak = piece if peak is None else jnp.maximum(peak, piece)
                    for k in range(choices):
                        term = jnp.where(at == columns[k], piece, 0.0)
                        picks[k] = term if picks[k] is None else picks[k] + term
                start += tile
        copies.append(
            pltpu.make_async_copy(
                logits.at[pl.ds(row, height), :],
                total_logits.at[pl.ds(row, height), pl.ds(first, width)],
                sems.at[index],
            )
        )
        copies[-1].start()
        peak = jnp.max(peak, axis=1, keepdims=True)
        total = None
        for part in range(width // LANES):
            term = jnp.exp(logits[here, part * LANES : (part + 1) * LANES] - peak)
            total = term if total is None else total + term
        out = jnp.where(lane == 0, peak, jnp.zeros((height, LANES), jnp.float32))
        for k, item in enumerate([total] + picks):
            out = jnp.where(lane == k + 1, jnp.sum(item, axis=1, keepdims=True), out)
        stats[here, :] = out if before is None else merge_rows(before[here, :], out)
    for copy in copies:
        copy.wait()


def finish(wanted, blocks, tile, choices, first, vocab_width, earlier, after):
    rows = wanted.shape[0]
    width = sum(keep.shape[1] for keep, _ in blocks)
    operands = [wanted]
    for keep, arrivals in blocks:
        operands += [keep, *arrivals]
    operands += [earlier[1]] if earlier else []
    buffer = [earlier[0]] if earlier else []
    return pl.pallas_call(
        functools.partial(
            finish_body,
            tile=tile,
            choices=choices,
            first=first,
            counts=[len(arrivals) for _, arrivals in blocks],
            earlier=bool(earlier),
        ),
        in_specs=[VMEM] * len(operands) + [ANY] * len(buffer + after),
        out_specs=[ANY, VMEM],
        out_shape=[
            jax.ShapeDtypeStruct((rows, vocab_width), jnp.float32),
            jax.ShapeDtypeStruct((rows, LANES), jnp.float32),
        ],
        scratch_shapes=[
            pltpu.VMEM((rows, width), jnp.float32),
            pltpu.SemaphoreType.DMA((rows // 16,)),
        ],
        input_output_aliases={len(operands): 0} if earlier else {},
        cost_estimate=UNIT_COST,
        compiler_params=pltpu.CompilerParams(vmem_limit_bytes=FINISH_LIMIT),
    )(*operands, *buffer, *after)


def merge_body(low, own, came, out):
    first = jnp.where(low[0] == 1, own[...], came[...])
    second = jnp.where(low[0] == 1, came[...], own[...])
    out[...] = merge_rows(first, second)


def merge(low, own, came):
    return pl.pallas_call(
        merge_body,
        in_specs=[pl.BlockSpec(memory_space=pltpu.SMEM), VMEM, VMEM],
        out_specs=VMEM,
        out_shape=jax.ShapeDtypeStruct(own.shape, own.dtype),
        cost_estimate=UNIT_COST,
        compiler_params=pltpu.CompilerParams(vmem_limit_bytes=VMEM_LIMIT),
    )(low, own, came)


def tail_body(low, own, came, tree, logits, log_probs, scores, stats, *, heads, height, choices):
    merge_body(low, own, came, stats)
    blocks = log_probs.shape[0] // height
    paths = scores.shape[1]
    width = logits.shape[1]
    tile = widest(1024, width)
    for block in range(blocks):
        there = slice(block * height, (block + 1) * height)
        score = jnp.zeros((height, paths), jnp.float32)
        for head in range(heads):
            row = (block * heads + head) * height
            here = slice(row, row + height)
            normalizer = stats[here, 0:1] + jnp.log(stats[here, 1:2])
            for at in range(0, width, tile):
                log_probs[there, head, at : at + tile] = logits[here, at : at + tile] - normalizer
            found = jnp.zeros((height, paths), jnp.float32)
            for k in range(choices):
                picked = stats[here, 2 + k : 3 + k] - normalizer
                found = jnp.where(tree[head : head + 1, :] == k, picked, found)
            score = score + found
        scores[there, :] = score


def tail(low, own, came, tree, logits, out_rows, height, choices):
    heads, paths = tree.shape
    return pl.pallas_call(
        functools.partial(tail_body, heads=heads, height=height, choices=choices),
        in_specs=[pl.BlockSpec(memory_space=pltpu.SMEM)] + [VMEM] * 4,
        out_specs=[VMEM] * 2,
        out_shape=[
            jax.ShapeDtypeStruct((out_rows, heads, logits.shape[1]), jnp.float32),
            jax.ShapeDtypeStruct((out_rows, paths), jnp.float32),
        ],
        scratch_shapes=[pltpu.VMEM(own.shape, own.dtype)],
        cost_estimate=UNIT_COST,
        compiler_params=pltpu.CompilerParams(vmem_limit_bytes=VMEM_LIMIT),
    )(low, own, came, tree, logits)


def shards(
    hidden_states, accepted, norm_gain, head_weight, head_bias, vocab_weight, cand_ids, tree_paths
):
    batch, mp = lax.axis_size("batch"), lax.axis_size("mp")
    b, m = lax.axis_index("batch"), lax.axis_index("mp")
    rows, positions, feat = hidden_states.shape
    heads, inner, _ = head_weight.shape
    vocab_width = vocab_weight.shape[1]
    out_rows, _, choices = cand_ids.shape
    pieces = feat // inner
    ratio = out_rows // rows
    mp_bits = bits_of(mp)
    pair, core = b // 2, b % 2
    pair_bits = bits_of(batch // 2)

    taken = lax.broadcasted_iota(jnp.int32, (rows, positions, 1), 1) == (accepted - 1)[:, None, None]
    chosen = jnp.sum(jnp.where(taken, hidden_states, 0).astype(jnp.float32), axis=1)
    chosen = chosen.astype(jnp.bfloat16)
    other = swap(chosen, "batch", lambda i: i ^ 1)
    chosen = jnp.concatenate(
        [jnp.where(core == 0, chosen, other), jnp.where(core == 0, other, chosen)], axis=0
    ).astype(jnp.float32)
    gain = lax.dynamic_slice_in_dim(norm_gain, m * feat, feat, 0)

    if pieces == 2:
        sent = lax.dynamic_slice_in_dim(chosen, core * inner, inner, 1)
        sent_gain = lax.dynamic_slice_in_dim(gain, core * inner, inner, 0)
    else:
        sent = lax.dynamic_slice_in_dim(chosen, core * rows, rows, 0)
        sent_gain = gain
    sent = (sent * sent_gain).astype(jnp.bfloat16)
    perm = []
    for i in range(batch):
        for j in range(mp):
            perm.append((i * mp + j, (j * pieces + i % pieces) * mp + ((i // pieces) ^ j)))
    block = lax.ppermute(sent, ("batch", "mp"), perm)
    for bit in mp_bits:
        block = jnp.concatenate([block, swap(block, "mp", lambda i: i ^ bit)], axis=0)

    square_sum = jnp.sum(chosen * chosen, axis=1, keepdims=True)
    for bit in mp_bits:
        square_sum = square_sum + swap(square_sum, "mp", lambda i: i ^ bit)
    row_scale = lax.rsqrt(square_sum / (mp * feat) + EPSILON)
    own_normed = (chosen * row_scale * gain).astype(jnp.bfloat16).astype(jnp.float32)

    spots = []
    for unit in range(batch):
        source = (m ^ (unit // pieces) ^ (b // pieces)) * pieces + unit % pieces
        spots.append(((source // 2) ^ pair) * 2 + source % 2)
    first = jnp.stack([1 - core] + spots).astype(jnp.int32)
    then = jnp.stack([core] + spots).astype(jnp.int32)
    send = head_matmul(first, block, head_weight, rows, jnp.bfloat16)
    came = swap(send, "batch", lambda i: i ^ 1)
    keep = head_matmul(then, block, head_weight, rows, jnp.float32)
    units = batch // 2
    share = feat // 2
    tall = 2 * rows
    orders = (pair_bits, pair_bits[::-1])
    total = keep + came.astype(jnp.float32)
    halves = [
        {u: total[u * tall : (u + 1) * tall, h * share : (h + 1) * share] for u in range(units)}
        for h in range(2)
    ]
    for step in range(len(pair_bits)):
        arrived = []
        for half, order in zip(halves, orders):
            leave = [u for u in half if u & order[step]]
            outbound = jnp.concatenate([half[u] for u in leave], axis=0).astype(jnp.bfloat16)
            arrived.append(swap(outbound, "batch", lambda i: i ^ (2 * order[step])))
        for h, order in enumerate(orders):
            stay = [u for u in halves[h] if not u & order[step]]
            halves[h] = {
                u: halves[h][u] + arrived[h][i * tall : (i + 1) * tall].astype(jnp.float32)
                for i, u in enumerate(stay)
            }
    bias = lax.dynamic_slice_in_dim(head_bias, core, 1, 0)
    before = jnp.concatenate([half[0] for half in halves], axis=1) * row_scale + bias
    residual = (own_normed + jax.nn.silu(before)).astype(jnp.bfloat16)
    filled = [residual[:, :share], residual[:, share:]]
    held = [[0], [0]]
    parts, others = [], []
    block = residual
    for step in reversed(range(len(pair_bits))):
        arrived = [
            swap(filled[h], "batch", lambda i: i ^ (2 * orders[h][step])) for h in range(2)
        ]
        for h in range(2):
            held[h] = held[h] + [u ^ orders[h][step] for u in held[h]]
        came = jnp.concatenate(arrived, axis=1)
        if step == 0:
            parts.append(block)
            others.append(swap(block, "batch", lambda i: i ^ 1))
            block = came
        else:
            block = jnp.concatenate([block, came], axis=0)
            filled = [block[:, :share], block[:, share:]]
    parts.append(block)
    others.append(swap(block, "batch", lambda i: i ^ 1))

    table = []
    for whose in (core, 1 - core):
        for unit in range(batch):
            for h in range(2):
                source = (pair ^ held[h][unit // 2]) * 2 + unit % 2
                table.append((((source // ratio) ^ m) * ratio + source % ratio) * heads + whose)
    all_rows = gather_rows(jnp.stack(table).astype(jnp.int32), parts + others, rows, 2)
    wanted = (cand_ids - b * vocab_width).reshape(ratio, rows, heads, choices)
    wanted = wanted.transpose(0, 2, 1, 3).reshape(out_rows * heads, choices)
    wanted = jnp.pad(wanted, ((0, 0), (0, LANES - choices)), constant_values=-1)

    unit_width = vocab_width // 8
    plan = [(0, 1), (1, 2), (3, 2), (5, 2), (7, 1)]
    plan = [(first * unit_width, count * unit_width) for first, count in plan]
    tile = widest(512, unit_width)
    blocks = len(plan)
    stages = [mp_bits if block % 2 == 0 else mp_bits[::-1] for block in range(blocks)]
    keeps, goes, sends, arrivals = [], [], [], [[] for _ in plan]

    def begin(block, after):
        first, width = plan[block]
        order = sorted(range(mp), key=lambda g: place(g, stages[block]))
        stay, go, send = vocab_matmul(all_rows, vocab_weight, first, width, order, tile, after)
        keeps.append(stay)
        goes.append(go)
        sends.append(send)
        arrivals[block].append(swap(send, "mp", lambda i: i ^ stages[block][0]))

    def go_on(block, after):
        keep, go = keeps[block], goes[block]
        for bit in stages[block][1:]:
            while len(arrivals[block]) > 1:
                rest = arrivals[block].pop(0)
                keep = go = add_kept(keep, rest, tile)
            send = fold(go, arrivals[block][-1], tile, after)
            arrivals[block].append(swap(send, "mp", lambda i: i ^ bit))
        keeps[block] = keep
        return send

    def finish_blocks(group, earlier, after):
        return finish(
            wanted,
            [(keeps[block], arrivals[block]) for block in group],
            tile,
            choices,
            plan[group[0]][0],
            vocab_width,
            earlier,
            after,
        )

    begin(0, [])
    begin(1, [sends[0]])
    begin(2, [sends[1]])
    last = go_on(0, [sends[2]])
    begin(3, [last])
    last = go_on(1, [sends[3]])
    begin(4, [last, arrivals[2][0]])
    last = go_on(2, [sends[4]])
    joined = finish_blocks((0, 1), None, [last])
    last = go_on(3, [joined[1]])
    last = go_on(4, [last])
    joined = finish_blocks((2,), joined, [last])
    joined = finish_blocks((3, 4), joined, [])
    logits, stats = joined

    for bit in bits_of(batch):
        came = swap(stats, "batch", lambda i: i ^ bit)
        low = (1 - (b & bit) // bit).astype(jnp.int32).reshape(1)
        if 2 * bit < batch:
            stats = merge(low, stats, came)
    log_probs, path_scores = tail(
        low, stats, came, tree_paths.T, logits, out_rows, rows, choices
    )
    return (log_probs, path_scores)


def solution(mesh):
    return jax.shard_map(
        shards,
        mesh=mesh,
        in_specs=(
            P("batch", None, "mp"),
            P("batch"),
            P(),
            P(None, "batch", "mp"),
            P(None, "mp"),
            P("mp", "batch"),
            P("mp", None, None),
            P(),
        ),
        out_specs=(P("mp", None, "batch"), P("mp", None)),
        check_vma=False,
    )
```
